128 devices in a mesh: seq: 64 (over y, x, z), head: 2 (over core).
Axes of the slice: x: 4, y: 4, z: 4, core: 2. Of those that a mesh axis runs over, the one named last changes fastest.
Arguments:
- residual: bfloat16 [8192, 2304], P('seq'), may hold values from -40 to 40
- kda_query: bfloat16 [8192, 2048], P('seq', 'head'), may hold values from -6 to 6
- kda_key: bfloat16 [8192, 2048], P('seq', 'head'), may hold values from -6 to 6
- kda_value: bfloat16 [8192, 2048], P('seq', 'head'), may hold values from -6 to 6
- log_decay: float32 [8192, 2048], P('seq', 'head'), may hold values from -1 to 0
- beta_logit: float32 [8192, 16], P('seq', 'head'), may hold values from -8 to 3
- out_gate: bfloat16 [8192, 2048], P('seq', 'head'), may hold values from -8 to 8
- out_gain: float32 [128], replicated, may hold values from 0.25 to 1.75
- out_weight: bfloat16 [2048, 2304], P('head'), may hold values from -0.125 to 0.125
- hidden_gain: float32 [2304], replicated, may hold values from 0.25 to 1.75
- query_weight: bfloat16 [2304, 2048], P(None, 'head'), may hold values from -32 to 32
- latent_weight: bfloat16 [2304, 512], replicated, may hold values from -3 to 3
- latent_gain: float32 [512], replicated, may hold values from 0.25 to 1.75
- key_up_weight: bfloat16 [512, 2048], P(None, 'head'), may hold values from -2 to 2
- value_up_weight: bfloat16 [512, 2048], P(None, 'head'), may hold values from -0.25 to 0.25
Outputs:
- hidden: bfloat16 [8192, 2304], P('seq')
- attended: bfloat16 [8192, 2048], P('seq', 'head')
The draws below stay inside these ranges and needn't reach their ends.
All inputs are finite; a program needn't handle non-finite values.
Results may differ from the reference program's by a relative error of at most 0.0105.
Values may be sent and summed in bfloat16 or wider, within the bound.
A program may use at most 192 MiB of HBM per device.

```python
import jax
import jax.numpy as jnp
from jax import lax

D = 2304
HEADS = 16
DK = 128
HD = 128
LAT = 512
TOK_DEV = 128
TOKEN_COUNT = 8192


def shared_weights(key):
    sequence_streams = jax.random.split(key, 3)
    col_scale = jnp.exp(jax.random.uniform(sequence_streams[0], (1, LAT), jnp.float32, -1.15, 1.15))
    latent_part = jax.random.truncated_normal(sequence_streams[1], -6.0, 6.0, (D, LAT), jnp.float32) * col_scale * D ** (-0.5)
    up_part = jax.random.truncated_normal(sequence_streams[2], -6.0, 6.0, (LAT, HEADS * HD), jnp.float32) * LAT ** (-0.5)
    return (latent_part, up_part)


def draw_latent_weight(key, part):
    latent_part, up_part = shared_weights(key)
    return latent_part.astype(jnp.bfloat16)


def draw_key_up_weight(key, part):
    latent_part, up_part = shared_weights(key)
    return up_part.astype(jnp.bfloat16)


def draw_query_weight(key, part):
    key = jax.random.fold_in(key, 3)
    sequence_streams = jax.random.split(key, 1)
    values = jax.random.truncated_normal(sequence_streams[0], -6.0, 6.0, (D, HEADS * HD), jnp.float32) * D ** (-0.5)
    return values.astype(jnp.bfloat16)


def draw_residual(key, part):
    key = jax.random.fold_in(key, 5)
    sequence_streams = jax.random.split(key, 3)
    row_scale = jnp.exp(jax.random.uniform(sequence_streams[1], (TOKEN_COUNT, 1), jnp.float32, -1.15, 1.15))
    col_scale = jnp.exp(jax.random.uniform(sequence_streams[2], (1, D), jnp.float32, -1.15, 1.15))
    values = jax.random.truncated_normal(sequence_streams[0], -6.0, 6.0, (TOKEN_COUNT, D), jnp.float32) * row_scale * col_scale * 0.3
    return values.astype(jnp.bfloat16)


def draw_log_decay(key, part):
    key = jax.random.fold_in(key, 11)
    sequence_streams = jax.random.split(key, 7)
    channels = HEADS * DK
    pick = jax.random.uniform(sequence_streams[0], (1, channels), jnp.float32)
    share = 0.5
    fast_rate = 1.0 / jax.random.uniform(sequence_streams[1], (1, channels), jnp.float32, 30.0, 50.0)
    slow_rate = jax.random.uniform(sequence_streams[2], (1, channels), jnp.float32, 0.3, 1.2) / TOKEN_COUNT
    baseline = jnp.where(pick < share, fast_rate, slow_rate)
    rough = jnp.exp(jax.random.uniform(sequence_streams[3], (TOKEN_COUNT, channels), jnp.float32, -0.6, 0.6))
    shard_factor = jnp.exp(jax.random.uniform(sequence_streams[4], (TOKEN_COUNT // TOK_DEV, 1, channels), jnp.float32, -0.5, 0.5))
    rate = ((baseline * rough).reshape(TOKEN_COUNT // TOK_DEV, TOK_DEV, channels) * shard_factor).reshape(TOKEN_COUNT, channels)
    spike_positions = jax.random.randint(sequence_streams[5], (5,), 0, TOKEN_COUNT)
    erased_state = jnp.any(jnp.arange(TOKEN_COUNT)[:, None] == spike_positions[None, :], axis=1)
    depth = jax.random.uniform(sequence_streams[6], (1, channels), jnp.float32, -0.69, -0.22)
    values = -rate + jnp.where(erased_state[:, None], depth, 0.0)
    return values.astype(jnp.float32)


def draw_beta_logit(key, part):
    key = jax.random.fold_in(key, 13)
    sequence_streams = jax.random.split(key, 3)
    pick = jax.random.uniform(sequence_streams[0], (1, HEADS), jnp.float32)
    share = 0.5
    slow_level = jnp.log(DK / (2.0 * TOKEN_COUNT))
    fast_level = jax.random.uniform(sequence_streams[1], (1, HEADS), jnp.float32, -1.0, 2.0)
    level = jnp.where(pick < share, fast_level, slow_level)
    noise = jax.random.uniform(sequence_streams[2], (TOKEN_COUNT, HEADS), jnp.float32, -0.7, 0.7)
    return (level + noise).astype(jnp.float32)


def block_scale(rng, extent, cuts, low, high):
    factor_of, own = 1.0, jax.random.fold_in(rng, 6)
    for dim, blocks in cuts:
        heights = jnp.exp(jax.random.uniform(jax.random.fold_in(own, dim), (blocks,), jnp.float32, low / len(cuts), high / len(cuts)))
        factor_of = factor_of * jnp.repeat(heights, extent[dim] // blocks).reshape([-1 if axis == dim else 1 for axis in range(len(extent))])
    return factor_of


def bell_draw(key, extent, deviation, bound, cuts=(), kind=jnp.bfloat16):
    loudness = block_scale(key, extent, cuts, -0.22, 0.18) if cuts else 1.0
    drawn = jax.random.normal(key, extent, jnp.float32) * deviation * loudness
    return jnp.minimum(jnp.maximum(drawn, -bound), bound).astype(kind)


def setup_inputs(seed: int = 0) -> dict:
    seeds = jax.random.split(jax.random.key(seed), 16)
    return {
        "residual": draw_residual(jax.random.fold_in(seeds[15], 71), 0),
        "kda_query": bell_draw(seeds[1], (TOKEN_COUNT, HEADS * DK), 1.0, 6.0, ((0, 64), (1, 2))),
        "kda_key": bell_draw(seeds[2], (TOKEN_COUNT, HEADS * DK), 1.0, 6.0, ((0, 64), (1, 2))),
        "kda_value": bell_draw(seeds[3], (TOKEN_COUNT, HEADS * DK), 1.0, 6.0, ((0, 64), (1, 2))),
        "log_decay": draw_log_decay(jax.random.fold_in(seeds[15], 71), 0),
        "beta_logit": draw_beta_logit(jax.random.fold_in(seeds[15], 71), 0),
        "out_gate": bell_draw(seeds[6], (TOKEN_COUNT, HEADS * DK), 1.5, 8.0, ((0, 64), (1, 2))),
        "out_gain": jnp.clip(1.0 + 0.15 * jax.random.normal(seeds[7], (DK,), jnp.float32), 0.25, 1.75),
        "out_weight": bell_draw(seeds[8], (HEADS * DK, D), (HEADS * DK) ** -0.5, 0.125, ((0, 2),)),
        "hidden_gain": jnp.clip(1.0 + 0.15 * jax.random.normal(seeds[9], (D,), jnp.float32), 0.25, 1.75),
        "query_weight": draw_query_weight(jax.random.fold_in(seeds[15], 71), 0),
        "latent_weight": draw_latent_weight(jax.random.fold_in(seeds[15], 71), 0),
        "latent_gain": jnp.clip(1.0 + 0.15 * jax.random.normal(seeds[12], (LAT,), jnp.float32), 0.25, 1.75),
        "key_up_weight": draw_key_up_weight(jax.random.fold_in(seeds[15], 71), 0),
        "value_up_weight": bell_draw(seeds[14], (LAT, HEADS * HD), LAT ** -0.5, 0.25, ((1, 2),)),
    }


EPS = 1e-06
PRECISION_HIGH = lax.Precision.HIGHEST

def rms_scale(values):
    return values * lax.rsqrt(lax.optimization_barrier(jnp.mean(values * values, axis=-1, keepdims=True)) + EPS)

def unit_length(values):
    return values * lax.rsqrt(lax.optimization_barrier(jnp.sum(values * values, axis=-1, keepdims=True)) + EPS)

def delta_rule(queries, key_heads, values, alpha, write_rate):

    def advance(memory_state, inputs):
        current_token_query, current_token_key, token_value, token_decay, token_rate = inputs
        decayed_state = memory_state * token_decay[:, :, None]
        predicted_value = jnp.einsum('iw,iwd->id', current_token_key, decayed_state, precision=PRECISION_HIGH)
        update = token_rate[:, None] * (token_value - predicted_value)
        memory_state = decayed_state + current_token_key[:, :, None] * update[:, None, :]
        return (memory_state, jnp.einsum('iw,iwd->id', current_token_query, memory_state, precision=PRECISION_HIGH))
    initial = jnp.zeros((HEADS, DK, DK), jnp.float32)
    _, outputs = lax.scan(advance, initial, (queries, key_heads, values, alpha, write_rate))
    return outputs

def reference(residual, kda_query, kda_key, kda_value, log_decay, beta_logit, out_gate, out_gain, out_weight, hidden_gain, query_weight, latent_weight, latent_gain, key_up_weight, value_up_weight):
    head_shape = (TOKEN_COUNT, HEADS, DK)
    queries = unit_length(kda_query.astype(jnp.float32).reshape(head_shape))
    key_heads = unit_length(kda_key.astype(jnp.float32).reshape(head_shape))
    values = kda_value.astype(jnp.float32).reshape(head_shape)
    alpha = jnp.exp(log_decay).reshape(head_shape)
    write_rate = jax.nn.sigmoid(beta_logit)
    kda_raw = delta_rule(queries, key_heads, values, alpha, write_rate)
    gate_value = jax.nn.sigmoid(out_gate.astype(jnp.float32).reshape(head_shape))
    gated = (rms_scale(kda_raw) * out_gain * gate_value).reshape(TOKEN_COUNT, HEADS * DK).astype(jnp.bfloat16)
    summed_out = residual.astype(jnp.float32) + jnp.dot(gated, out_weight, preferred_element_type=jnp.float32)
    hidden = lax.optimization_barrier(summed_out.astype(jnp.bfloat16))
    normed = (rms_scale(hidden.astype(jnp.float32)) * hidden_gain).astype(jnp.bfloat16)
    latent_raw = jnp.dot(normed, latent_weight, preferred_element_type=jnp.float32)
    latent = (rms_scale(latent_raw) * latent_gain).astype(jnp.bfloat16)
    queries_mla = lax.optimization_barrier(jnp.dot(normed, query_weight, preferred_element_type=jnp.float32).astype(jnp.bfloat16))
    key_rows = lax.optimization_barrier(jnp.dot(latent, key_up_weight, preferred_element_type=jnp.float32).astype(jnp.bfloat16))
    value_rows = lax.optimization_barrier(jnp.dot(latent, value_up_weight, preferred_element_type=jnp.float32).astype(jnp.bfloat16))
    key_float = key_rows.astype(jnp.float32).reshape(TOKEN_COUNT, HEADS, HD)
    value_float = value_rows.astype(jnp.float32).reshape(TOKEN_COUNT, HEADS, HD)
    block_rows = 512
    query_blocks = queries_mla.astype(jnp.float32).reshape(TOKEN_COUNT // block_rows, block_rows, HEADS, HD)
    starts = jnp.arange(TOKEN_COUNT // block_rows, dtype=jnp.int32) * block_rows
    positions = jnp.arange(TOKEN_COUNT, dtype=jnp.int32)
    score_scale = HD ** (-0.5)

    def attend(inputs):
        q_block, q_start = inputs
        scores = jnp.einsum('qhd,khd->hqk', q_block, key_float) * score_scale
        q_positions = q_start + jnp.arange(block_rows, dtype=jnp.int32)
        visible = (positions[None, :] <= q_positions[:, None])[None]
        scores = jnp.where(visible, scores, -1e+30)
        row_max = lax.optimization_barrier(jnp.max(scores, axis=-1, keepdims=True))
        probs = jnp.where(visible, jnp.exp(scores - row_max), 0.0)
        row_total = lax.optimization_barrier(jnp.sum(probs, axis=-1))
        rounded = lax.optimization_barrier(probs.astype(jnp.bfloat16)).astype(jnp.float32)
        mixed = jnp.einsum('hqk,khd->qhd', rounded, value_float)
        return mixed / jnp.transpose(row_total)[:, :, None]
    outputs = lax.map(attend, (query_blocks, starts))
    attended = outputs.reshape(TOKEN_COUNT, HEADS * HD).astype(jnp.bfloat16)
    return (hidden, attended)
```

```python
import jax
import jax.numpy as jnp
from jax import lax
from jax.sharding import PartitionSpec as P
from jax.experimental import pallas as pl
from jax.experimental.pallas import tpu as pltpu

F32 = jnp.float32
BF16 = jnp.bfloat16
W = 128
EPS = 1e-06


def halves(x):
    high = x.astype(BF16)
    return high, (x - high.astype(F32)).astype(BF16)


def mm(a, b):
    return jnp.dot(a, b, preferred_element_type=F32)


def mm_nt(a, b):
    return lax.dot_general(a, b, (((1,), (1,)), ((), ())), preferred_element_type=F32)


def wide(x):
    high, low = halves(x)
    return jnp.concatenate([high, low], axis=1)


def mm4(a, b):
    n = b.shape[1]
    right = wide(b)
    out = mm(wide(a), jnp.concatenate([right, right], axis=0))
    return out[:, :n] + out[:, n:]


def mm4_nt(a, b):
    n = b.shape[0]
    high, low = halves(b)
    right = jnp.concatenate(
        [jnp.concatenate([high, high], axis=1), jnp.concatenate([low, low], axis=1)], axis=0
    )
    out = mm_nt(wide(a), right)
    return out[:, :n] + out[:, n:]


def iota(shape, axis):
    return lax.broadcasted_iota(jnp.int32, shape, axis)


def delta_kernel(q_ref, k_ref, v_ref, ld_ref, beta_ref, msg_ref, base_ref, carry_ref):
    rows = q_ref.shape[0]
    heads = q_ref.shape[1] // W
    ti, si = iota((rows, rows), 0), iota((rows, rows), 1)
    ones = jnp.where(si <= ti, 1.0, 0.0).astype(BF16)
    strict = si < ti
    through = si <= ti
    eye = jnp.where(si == ti, 1.0, 0.0)
    rates = 1.0 / (1.0 + jnp.exp(-beta_ref[...]))

    def stage_one(h):
        cols = slice(h * W, (h + 1) * W)
        ld = ld_ref[:, cols]
        high, rest = halves(ld)
        low = (ld - high.astype(F32) - rest.astype(F32)).astype(BF16)
        cum = mm(ones, high) + (mm(ones, rest) + mm(ones, low))
        mid = cum[rows // 2 - 1 : rows // 2, :]
        end = cum[rows - 1 : rows, :]
        key = k_ref[:, cols].astype(F32)
        key = key * lax.rsqrt(jnp.sum(key * key, axis=-1, keepdims=True) + EPS)
        query = q_ref[:, cols].astype(F32)
        query = query * lax.rsqrt(jnp.sum(query * query, axis=-1, keepdims=True) + EPS)
        forward = jnp.exp(cum - mid)
        mixed = mm4_nt(
            jnp.concatenate([key * forward, query * forward], axis=0), key * jnp.exp(mid - cum)
        )
        rate = rates[:, h : h + 1]
        lower = jnp.where(strict, mixed[:rows], 0.0) * rate
        mix = jnp.where(through, mixed[rows:], 0.0)
        growth = jnp.exp(cum)
        right = jnp.concatenate(
            [rate * v_ref[:, cols].astype(F32), rate * (key * growth)], axis=1
        )
        tail = (key * jnp.exp(end - cum)).T
        return lower, mix, right, tail, query * growth, jnp.exp(end)

    def invert(lowers):
        level = jnp.logical_and((ti // 2) == (si // 2), strict)
        found = [eye - jnp.where(level, low, 0.0) for low in lowers]
        size = 2
        while size < rows:
            level = jnp.logical_and((ti // (2 * size)) == (si // (2 * size)),
                                    (ti // size) > (si // size))
            inner = [mm4(jnp.where(level, low, 0.0), x) for low, x in zip(lowers, found)]
            found = [x - mm4(x, y) for x, y in zip(found, inner)]
            size *= 2
        return found

    group = 4
    for start in range(0, heads, group):
        made = [stage_one(h) for h in range(start, start + group)]
        inverses = invert([m[0] for m in made])
        for h in range(start, start + group):
            _, mix, right, tail, query, closing = made[h - start]
            solved = mm4(inverses[h - start], right)
            state = mm4(tail, solved)
            out = mm4(mix, solved)
            cols = slice(h * W, (h + 1) * W)
            base_ref[:, cols] = out[:, :W]
            carry_ref[:, cols] = (query - out[:, W:]).astype(BF16)
            msg_ref[h, :W, :W] = state[:, W:].astype(BF16)
            msg_ref[h, :W, W:] = state[:, :W].astype(BF16)
            msg_ref[h, W:, :] = pack_diag(closing)


def pack_diag(closing):
    high, rest = halves(closing)
    r = iota((16, W), 0)
    block = jnp.where(r == 0, high.astype(F32), jnp.where(r == 1, rest.astype(F32), 0.0))
    return jnp.concatenate([block, jnp.zeros((16, W), F32)], axis=1).astype(BF16)


def delta_terms(q, k, v, ld, beta):
    rows, heads = beta.shape
    vm = pl.BlockSpec(memory_space=pltpu.VMEM)
    return pl.pallas_call(
        delta_kernel,
        out_shape=(
            jax.ShapeDtypeStruct((heads, W + 16, 2 * W), BF16),
            jax.ShapeDtypeStruct((rows, heads * W), F32),
            jax.ShapeDtypeStruct((rows, heads * W), BF16),
        ),
        in_specs=[vm] * 5,
        out_specs=(vm, vm, vm),
        compiler_params=pltpu.CompilerParams(vmem_limit_bytes=48 * 2**20),
        name="delta_terms",
    )(q, k, v, ld, beta)


PIECES = 3
MESH = pl.DeviceIdType.MESH


def unpack_map(block):
    diag = block[W : W + 1, :W].astype(F32) + block[W + 1 : W + 2, :W].astype(F32)
    eye = iota((W, W), 0) == iota((W, W), 1)
    matrix = jnp.where(eye, diag, 0.0) - block[:W, :W].astype(F32)
    return jnp.concatenate([matrix, block[:W, W:].astype(F32)], axis=1), diag


def after(later, earlier):
    n = earlier.shape[1]
    out = mm4(later[:, :W], earlier)
    if n == 2 * W:
        return jnp.concatenate([out[:, :W], out[:, W:] + later[:, W:]], axis=1)
    return out + later[:, W:]


def carry_kernel(
    msg, base, carry, gate, out_gain, residual, hidden_gain, latent_gain, ow_hbm, lw_hbm, qw_hbm, ku_hbm,
    hidden_o, qp_o, latent_o,
    got, total, totals, states, state_in, partial, other, ow, lw, qw, ku,
    send_a, recv_a, send_b, recv_b, send_c, recv_c, send_p, recv_p, load_sem,
):
    heads = msg.shape[0]
    groups = totals.shape[0]
    here, core = lax.axis_index("seq"), lax.axis_index("head")
    mine, rank = here // heads, here % heads
    sibling = (here, 1 - core)

    def member(step):
        peer = (rank + step) % heads
        return peer, (mine * heads + peer, core)

    def cousin(step):
        peer = (mine + step) % groups
        return peer, (peer * heads + rank, core)

    loads = [
        pltpu.make_async_copy(src, dst, load_sem.at[i])
        for i, (src, dst) in enumerate(((ow_hbm, ow), (lw_hbm, lw), (qw_hbm, qw), (ku_hbm, ku)))
    ]

    barrier = pltpu.get_barrier_semaphore()
    for step in range(1, heads):
        pl.semaphore_signal(barrier, inc=1, device_id=member(step)[1], device_id_type=MESH)
    for step in range(1, groups):
        pl.semaphore_signal(barrier, inc=1, device_id=cousin(step)[1], device_id_type=MESH)
    pl.semaphore_signal(barrier, inc=1, device_id=sibling, device_id_type=MESH)
    pl.semaphore_wait(barrier, heads + groups - 1)

    def send_map(step):
        peer, device = member(step)
        return pltpu.make_async_remote_copy(
            src_ref=msg.at[peer], dst_ref=got.at[rank],
            send_sem=send_a.at[peer], recv_sem=recv_a.at[rank],
            device_id=device, device_id_type=MESH,
        )

    def take_map(step):
        peer, device = member(step)
        return pltpu.make_async_remote_copy(
            src_ref=msg.at[peer], dst_ref=got.at[peer],
            send_sem=send_a.at[peer], recv_sem=recv_a.at[peer],
            device_id=device, device_id_type=MESH,
        )

    for step in range(1, heads):
        send_map(step).start()
    for load in loads:
        load.start()
    got[rank] = msg[rank]
    for step in range(1, heads):
        take_map(step).wait_recv()

    maps, diags = [], []
    for i in range(heads):
        matrix, diag = unpack_map(got[i])
        maps.append(matrix)
        diags.append(diag)
    pairs = [after(maps[i + 1], maps[i]) for i in range(0, heads, 2)]
    quads = [after(pairs[i + 1], pairs[i]) for i in range(0, len(pairs), 2)]
    whole = after(quads[1], quads[0])
    diag = diags[0]
    for other_diag in diags[1:]:
        diag = diag * other_diag
    eye = iota((W, W), 0) == iota((W, W), 1)
    total[:W, :W] = (jnp.where(eye, diag, 0.0) - whole[:, :W]).astype(BF16)
    total[:W, W:] = whole[:, W:].astype(BF16)
    total[W:, :] = pack_diag(diag)

    def send_total(step):
        peer, device = cousin(step)
        return peer, pltpu.make_async_remote_copy(
            src_ref=total, dst_ref=totals.at[mine],
            send_sem=send_b.at[peer], recv_sem=recv_b.at[mine],
            device_id=device, device_id_type=MESH,
        )

    def take_total(step):
        peer, device = cousin(step)
        return peer, pltpu.make_async_remote_copy(
            src_ref=total, dst_ref=totals.at[peer],
            send_sem=send_b.at[peer], recv_sem=recv_b.at[peer],
            device_id=device, device_id_type=MESH,
        )

    for step in range(1, groups):
        peer, copy = send_total(step)
        pl.when(peer > mine)(copy.start)

    before = [None] * heads
    before[1] = maps[0]
    before[2] = pairs[0]
    before[4] = quads[0]
    before[3] = after(maps[2], pairs[0])
    before[5] = after(maps[4], quads[0])
    before[6] = after(pairs[2], quads[0])
    before[7] = after(maps[6], before[6])

    for step in range(1, groups):
        peer, copy = take_total(step)
        pl.when(peer < mine)(copy.wait_recv)

    eye_zero = jnp.concatenate([jnp.where(eye, 1.0, 0.0), jnp.zeros((W, W), F32)], axis=1)
    chain = [jnp.where(j < mine, unpack_map(totals[j])[0], eye_zero) for j in range(groups - 1)]
    while len(chain) > 1:
        joined = []
        for i in range(0, len(chain) - 1, 2):
            first = chain[i] if i else chain[i][:, W:]
            joined.append(after(chain[i + 1], first))
        if len(chain) % 2:
            joined.append(chain[-1])
        if joined[0].shape[1] == W:
            joined[0] = jnp.concatenate([jnp.zeros((W, W), F32), joined[0]], axis=1)
        chain = joined
    start = chain[0][:, W:]

    states[0] = start.astype(BF16)
    stacked = mm4(jnp.concatenate([b[:, :W] for b in before[1:]], axis=0), start)
    for i in range(1, heads):
        states[i] = (stacked[(i - 1) * W : i * W] + before[i][:, W:]).astype(BF16)

    def send_state(step):
        peer, device = member(step)
        return pltpu.make_async_remote_copy(
            src_ref=states.at[peer], dst_ref=state_in.at[rank],
            send_sem=send_c.at[peer], recv_sem=recv_c.at[rank],
            device_id=device, device_id_type=MESH,
        )

    def take_state(step):
        peer, device = member(step)
        return pltpu.make_async_remote_copy(
            src_ref=states.at[peer], dst_ref=state_in.at[peer],
            send_sem=send_c.at[peer], recv_sem=recv_c.at[peer],
            device_id=device, device_id_type=MESH,
        )

    for step in range(1, heads):
        send_state(step).start()
    state_in[rank] = states[rank]
    for step in range(1, heads):
        take_state(step).wait_recv()

    gated = []
    for h in range(heads):
        cols = slice(h * W, (h + 1) * W)
        raw = base[:, cols] + mm(carry[:, cols], state_in[h])
        raw = raw * lax.rsqrt(jnp.mean(raw * raw, axis=-1, keepdims=True) + EPS)
        logits = gate[:, cols].astype(F32)
        gated.append((raw * out_gain[...] / (1.0 + jnp.exp(-logits))).astype(BF16))
    gated = jnp.concatenate(gated, axis=1)

    loads[0].wait()
    width = partial.shape[2]

    def swap(p):
        return pltpu.make_async_remote_copy(
            src_ref=partial.at[p], dst_ref=other.at[p],
            send_sem=send_p.at[p], recv_sem=recv_p.at[p],
            device_id=sibling, device_id_type=MESH,
        )

    for p in range(PIECES):
        partial[p] = mm(gated, ow[:, p * width : (p + 1) * width])
        swap(p).start()
    squares = 0.0
    hidden = []
    for p in range(PIECES):
        cols = slice(p * width, (p + 1) * width)
        swap(p).wait_recv()
        summed = residual[:, cols].astype(F32) + (partial[p] + other[p])
        rounded = summed.astype(BF16)
        hidden_o[:, cols] = rounded
        rounded = rounded.astype(F32)
        squares = squares + jnp.sum(rounded * rounded, axis=-1, keepdims=True)
        hidden.append(rounded)
    scale = lax.rsqrt(squares / (PIECES * width) + EPS)
    normed = jnp.concatenate(hidden, axis=1) * scale * hidden_gain[...]
    normed = normed.astype(BF16)
    loads[1].wait()
    latent = mm(normed, lw[...])
    latent = latent * lax.rsqrt(jnp.mean(latent * latent, axis=-1, keepdims=True) + EPS)
    latent_o[...] = (latent * latent_gain[...]).astype(BF16)
    loads[2].wait()
    loads[3].wait()
    queries = mm(normed, qw[...]).astype(BF16)
    for h in range(heads):
        cols = slice(h * W, (h + 1) * W)
        qp_o[h] = (mm_nt(queries[:, cols], ku[:, cols]) * SCORE_SCALE).astype(BF16)

    for step in range(1, heads):
        send_map(step).wait_send()
        send_state(step).wait_send()
    for step in range(1, groups):
        peer, copy = send_total(step)
        pl.when(peer > mine)(copy.wait_send)
    for p in range(PIECES):
        swap(p).wait_send()


SCORE_SCALE = W ** (-0.5) * 1.4426950408889634


def carry_layer(msg, base, carry, gate, out_gain, residual, hidden_gain, latent_gain, ow, lw, qw, ku):
    heads = msg.shape[0]
    rows, width = residual.shape
    latent = lw.shape[1]
    groups = lax.axis_size("seq") // heads
    vm = pl.BlockSpec(memory_space=pltpu.VMEM)
    anywhere = pl.BlockSpec(memory_space=pl.ANY)
    dma = pltpu.SemaphoreType.DMA
    return pl.pallas_call(
        carry_kernel,
        out_shape=(
            jax.ShapeDtypeStruct((rows, width), BF16),
            jax.ShapeDtypeStruct((heads, rows, latent), BF16),
            jax.ShapeDtypeStruct((rows, latent), BF16),
        ),
        in_specs=[vm] * 8 + [anywhere] * 4,
        out_specs=(vm, vm, vm),
        scratch_shapes=[
            pltpu.VMEM(msg.shape, BF16),
            pltpu.VMEM(msg.shape[1:], BF16),
            pltpu.VMEM((groups,) + msg.shape[1:], BF16),
            pltpu.VMEM((heads, W, W), BF16),
            pltpu.VMEM((heads, W, W), BF16),
            pltpu.VMEM((PIECES, rows, width // PIECES), F32),
            pltpu.VMEM((PIECES, rows, width // PIECES), F32),
            pltpu.VMEM(ow.shape, BF16),
            pltpu.VMEM(lw.shape, BF16),
            pltpu.VMEM(qw.shape, BF16),
            pltpu.VMEM(ku.shape, BF16),
            dma((heads,)), dma((heads,)), dma((groups,)), dma((groups,)),
            dma((heads,)), dma((heads,)), dma((PIECES,)), dma((PIECES,)), dma((4,)),
        ],
        compiler_params=pltpu.CompilerParams(
            collective_id=0, has_side_effects=True, vmem_limit_bytes=56 * 2**20
        ),
        name="carry_layer",
    )(msg, base, carry, gate, out_gain, residual, hidden_gain, latent_gain, ow, lw, qw, ku)


KEYS = 512


def attend_kernel(qp_ref, vu_ref, latent_hbm, out_ref, latents, row_max, row_sum, accum, load_sem):
    heads, rows, latent = qp_ref.shape
    here = lax.axis_index("seq")
    lanes = W
    per = KEYS // rows

    def load(j):
        part = pl.ds(pl.multiple_of(j * KEYS, KEYS), KEYS)
        return pltpu.make_async_copy(latent_hbm.at[part], latents.at[part], load_sem.at[j])

    chunks = here // per + 1
    for j in range(latents.shape[0] // KEYS):
        pl.when(j < chunks)(load(j).start)
    row_max[...] = jnp.full(row_max.shape, -1e30, F32)
    row_sum[...] = jnp.zeros(row_sum.shape, F32)
    accum[...] = jnp.zeros(accum.shape, F32)
    block = GROUP * rows

    def chunk(j, masked):
        load(j).wait()
        keys = latents[pl.ds(pl.multiple_of(j * KEYS, KEYS), KEYS), :]
        for b in range(0, heads, GROUP):
            place = slice(b * rows, b * rows + block)
            scores = mm_nt(qp_ref[b : b + GROUP].reshape(block, latent), keys)
            if masked:
                query_pos = here * rows + iota((block, KEYS), 0) % rows
                key_pos = j * KEYS + iota((block, KEYS), 1)
                scores = jnp.where(key_pos <= query_pos, scores, -1e30)
            old = row_max[place, :]
            new = jnp.maximum(old, jnp.max(scores, axis=-1, keepdims=True))
            row_max[place, :] = new
            shrink = jnp.exp2(old - new)
            probs = [
                jnp.exp2(scores[:, c : c + lanes] - new) for c in range(0, KEYS, lanes)
            ]
            added = probs[0]
            for p in probs[1:]:
                added = added + p
            row_sum[place, :] = row_sum[place, :] * shrink + added
            mixed = mm(jnp.concatenate([p.astype(BF16) for p in probs], axis=1), keys)
            accum[place, :] = accum[place, :] * jnp.concatenate(
                [shrink] * (latent // lanes), axis=1
            ) + mixed

    def step(j, nothing):
        chunk(j, False)
        return nothing

    lax.fori_loop(0, chunks - 1, step, 0)
    chunk(chunks - 1, True)
    for h in range(heads):
        place = slice(h * rows, (h + 1) * rows)
        total = jnp.sum(row_sum[place, :], axis=-1, keepdims=True)
        mixed = accum[place, :] / total
        high, low = halves(mixed)
        cols = slice(h * W, (h + 1) * W)
        up = vu_ref[:, cols]
        out_ref[:, cols] = (mm(high, up) + mm(low, up)).astype(BF16)


GROUP = 4


def attend(qp, vu, latents):
    heads, rows, latent = qp.shape
    tokens = latents.shape[0]
    vm = pl.BlockSpec(memory_space=pltpu.VMEM)
    return pl.pallas_call(
        attend_kernel,
        out_shape=jax.ShapeDtypeStruct((rows, heads * W), BF16),
        in_specs=[vm, vm, pl.BlockSpec(memory_space=pl.ANY)],
        out_specs=vm,
        scratch_shapes=[
            pltpu.VMEM((tokens, latent), BF16),
            pltpu.VMEM((heads * rows, W), F32),
            pltpu.VMEM((heads * rows, W), F32),
            pltpu.VMEM((heads * rows, latent), F32),
            pltpu.SemaphoreType.DMA((tokens // KEYS,)),
        ],
        compiler_params=pltpu.CompilerParams(vmem_limit_bytes=56 * 2**20),
        name="attend",
    )(qp, vu, latents)


def body(
    residual, kda_query, kda_key, kda_value, log_decay, beta_logit, out_gate, out_gain, out_weight,
    hidden_gain, query_weight, latent_weight, latent_gain, key_up_weight, value_up_weight,
):
    msg, base, carry = delta_terms(kda_query, kda_key, kda_value, log_decay, beta_logit)
    hidden, qp, latent = carry_layer(
        msg, base, carry, out_gate, out_gain[None], residual, hidden_gain[None], latent_gain[None],
        out_weight, latent_weight, query_weight, key_up_weight,
    )
    latents = lax.all_gather(latent, "seq", axis=0, tiled=True)
    return hidden, attend(qp, value_up_weight, latents)


def solution(mesh):
    in_specs = (
        P("seq", None),
        P("seq", "head"),
        P("seq", "head"),
        P("seq", "head"),
        P("seq", "head"),
        P("seq", "head"),
        P("seq", "head"),
        P(),
        P("head", None),
        P(),
        P(None, "head"),
        P(),
        P(),
        P(None, "head"),
        P(None, "head"),
    )
    out_specs = (P("seq", None), P("seq", "head"))
    return jax.shard_map(body, mesh=mesh, in_specs=in_specs, out_specs=out_specs, check_vma=False)
```

```python
import functools
import jax
import jax.numpy as jnp
from jax import lax
from jax.sharding import PartitionSpec as P
from jax.experimental import pallas as pl
from jax.experimental.pallas import tpu as pltpu

F32 = jnp.float32
BF16 = jnp.bfloat16
W = 128
EPS = 1e-06


def halves(x):
    high = x.astype(BF16)
    return high, (x - high.astype(F32)).astype(BF16)


def mm(a, b):
    return jnp.dot(a, b, preferred_element_type=F32)


def mm_nt(a, b):
    return lax.dot_general(a, b, (((1,), (1,)), ((), ())), preferred_element_type=F32)


def wide(x):
    high, low = halves(x)
    return jnp.concatenate([high, low], axis=1)


def mm4(a, b):
    n = b.shape[1]
    right = wide(b)
    out = mm(wide(a), jnp.concatenate([right, right], axis=0))
    return out[:, :n] + out[:, n:]


def mm4_nt(a, b):
    n = b.shape[0]
    high, low = halves(b)
    right = jnp.concatenate(
        [jnp.concatenate([high, high], axis=1), jnp.concatenate([low, low], axis=1)], axis=0
    )
    out = mm_nt(wide(a), right)
    return out[:, :n] + out[:, n:]


def iota(shape, axis):
    return lax.broadcasted_iota(jnp.int32, shape, axis)


def delta_kernel(q_ref, k_ref, v_ref, ld_ref, beta_ref, msg_ref, base_ref, carry_ref):
    rows = q_ref.shape[0]
    heads = q_ref.shape[1] // W
    ti, si = iota((rows, rows), 0), iota((rows, rows), 1)
    ones = jnp.where(si <= ti, 1.0, 0.0).astype(BF16)
    strict = si < ti
    through = si <= ti
    eye = jnp.where(si == ti, 1.0, 0.0)
    rates = 1.0 / (1.0 + jnp.exp(-beta_ref[...]))

    def stage_one(h):
        cols = slice(h * W, (h + 1) * W)
        ld = ld_ref[:, cols]
        high, rest = halves(ld)
        low = (ld - high.astype(F32) - rest.astype(F32)).astype(BF16)
        cum = mm(ones, high) + (mm(ones, rest) + mm(ones, low))
        mid = cum[rows // 2 - 1 : rows // 2, :]
        end = cum[rows - 1 : rows, :]
        key = k_ref[:, cols].astype(F32)
        key = key * lax.rsqrt(jnp.sum(key * key, axis=-1, keepdims=True) + EPS)
        query = q_ref[:, cols].astype(F32)
        query = query * lax.rsqrt(jnp.sum(query * query, axis=-1, keepdims=True) + EPS)
        forward = jnp.exp(cum - mid)
        mixed = mm4_nt(
            jnp.concatenate([key * forward, query * forward], axis=0), key * jnp.exp(mid - cum)
        )
        rate = rates[:, h : h + 1]
        lower = jnp.where(strict, mixed[:rows], 0.0) * rate
        mix = jnp.where(through, mixed[rows:], 0.0)
        growth = jnp.exp(cum)
        right = jnp.concatenate(
            [rate * v_ref[:, cols].astype(F32), rate * (key * growth)], axis=1
        )
        tail = (key * jnp.exp(end - cum)).T
        return lower, mix, right, tail, query * growth, jnp.exp(end)

    def invert(lowers):
        level = jnp.logical_and((ti // 2) == (si // 2), strict)
        found = [eye - jnp.where(level, low, 0.0) for low in lowers]
        size = 2
        while size < rows:
            level = jnp.logical_and((ti // (2 * size)) == (si // (2 * size)),
                                    (ti // size) > (si // size))
            inner = [mm4(jnp.where(level, low, 0.0), x) for low, x in zip(lowers, found)]
            found = [x - mm4(x, y) for x, y in zip(found, inner)]
            size *= 2
        return found

    group = 4
    for start in range(0, heads, group):
        made = [stage_one(h) for h in range(start, start + group)]
        inverses = invert([m[0] for m in made])
        for h in range(start, start + group):
            _, mix, right, tail, query, closing = made[h - start]
            solved = mm4(inverses[h - start], right)
            state = mm4(tail, solved)
            out = mm4(mix, solved)
            cols = slice(h * W, (h + 1) * W)
            base_ref[:, cols] = out[:, :W]
            carry_ref[:, cols] = (query - out[:, W:]).astype(BF16)
            msg_ref[h, :W, :W] = state[:, W:].astype(BF16)
            msg_ref[h, :W, W:] = state[:, :W].astype(BF16)
            msg_ref[h, W:, :] = pack_diag(closing)


def pack_diag(closing):
    high, rest = halves(closing)
    r = iota((16, W), 0)
    block = jnp.where(r == 0, high.astype(F32), jnp.where(r == 1, rest.astype(F32), 0.0))
    return jnp.concatenate([block, jnp.zeros((16, W), F32)], axis=1).astype(BF16)


def delta_terms(q, k, v, ld, beta):
    rows, heads = beta.shape
    vm = pl.BlockSpec(memory_space=pltpu.VMEM)
    return pl.pallas_call(
        delta_kernel,
        out_shape=(
            jax.ShapeDtypeStruct((heads, W + 16, 2 * W), BF16),
            jax.ShapeDtypeStruct((rows, heads * W), F32),
            jax.ShapeDtypeStruct((rows, heads * W), BF16),
        ),
        in_specs=[vm] * 5,
        out_specs=(vm, vm, vm),
        compiler_params=pltpu.CompilerParams(vmem_limit_bytes=48 * 2**20),
        name="delta_terms",
    )(q, k, v, ld, beta)


PIECES = 3
MESH = pl.DeviceIdType.MESH


def unpack_map(block):
    diag = block[W : W + 1, :W].astype(F32) + block[W + 1 : W + 2, :W].astype(F32)
    eye = iota((W, W), 0) == iota((W, W), 1)
    matrix = jnp.where(eye, diag, 0.0) - block[:W, :W].astype(F32)
    return jnp.concatenate([matrix, block[:W, W:].astype(F32)], axis=1), diag


def after(later, earlier):
    n = earlier.shape[1]
    out = mm4(later[:, :W], earlier)
    if n == 2 * W:
        return jnp.concatenate([out[:, :W], out[:, W:] + later[:, W:]], axis=1)
    return out + later[:, W:]


def carry_kernel(
    msg, base, carry, gate, out_gain, residual, hidden_gain, latent_gain, ow_hbm, lw_hbm, qw_hbm, ku_hbm,
    hidden_o, qp_o, latent_o,
    got, total, totals, states, state_in, partial, other, ow, lw, qw, ku,
    send_a, recv_a, send_b, recv_b, send_c, recv_c, send_p, recv_p, load_sem,
):
    heads = msg.shape[0]
    groups = totals.shape[0]
    here, core = lax.axis_index("seq"), lax.axis_index("head")
    mine, rank = here // heads, here % heads
    sibling = (here, 1 - core)

    def member(step):
        peer = (rank + step) % heads
        return peer, (mine * heads + peer, core)

    def cousin(step):
        peer = (mine + step) % groups
        return peer, (peer * heads + rank, core)

    loads = [
        pltpu.make_async_copy(src, dst, load_sem.at[i])
        for i, (src, dst) in enumerate(((ow_hbm, ow), (lw_hbm, lw), (qw_hbm, qw), (ku_hbm, ku)))
    ]

    barrier = pltpu.get_barrier_semaphore()
    for step in range(1, heads):
        pl.semaphore_signal(barrier, inc=1, device_id=member(step)[1], device_id_type=MESH)
    for step in range(1, groups):
        pl.semaphore_signal(barrier, inc=1, device_id=cousin(step)[1], device_id_type=MESH)
    pl.semaphore_signal(barrier, inc=1, device_id=sibling, device_id_type=MESH)
    pl.semaphore_wait(barrier, heads + groups - 1)

    def send_map(step):
        peer, device = member(step)
        return pltpu.make_async_remote_copy(
            src_ref=msg.at[peer], dst_ref=got.at[rank],
            send_sem=send_a.at[peer], recv_sem=recv_a.at[rank],
            device_id=device, device_id_type=MESH,
        )

    def take_map(step):
        peer, device = member(step)
        return pltpu.make_async_remote_copy(
            src_ref=msg.at[peer], dst_ref=got.at[peer],
            send_sem=send_a.at[peer], recv_sem=recv_a.at[peer],
            device_id=device, device_id_type=MESH,
        )

    for step in range(1, heads):
        send_map(step).start()
    for load in loads:
        load.start()
    got[rank] = msg[rank]
    for step in range(1, heads):
        take_map(step).wait_recv()

    maps, diags = [], []
    for i in range(heads):
        matrix, diag = unpack_map(got[i])
        maps.append(matrix)
        diags.append(diag)
    pairs = [after(maps[i + 1], maps[i]) for i in range(0, heads, 2)]
    quads = [after(pairs[i + 1], pairs[i]) for i in range(0, len(pairs), 2)]
    whole = after(quads[1], quads[0])
    diag = diags[0]
    for other_diag in diags[1:]:
        diag = diag * other_diag
    eye = iota((W, W), 0) == iota((W, W), 1)
    total[:W, :W] = (jnp.where(eye, diag, 0.0) - whole[:, :W]).astype(BF16)
    total[:W, W:] = whole[:, W:].astype(BF16)
    total[W:, :] = pack_diag(diag)

    def send_total(step):
        peer, device = cousin(step)
        return peer, pltpu.make_async_remote_copy(
            src_ref=total, dst_ref=totals.at[mine],
            send_sem=send_b.at[peer], recv_sem=recv_b.at[mine],
            device_id=device, device_id_type=MESH,
        )

    def take_total(step):
        peer, device = cousin(step)
        return peer, pltpu.make_async_remote_copy(
            src_ref=total, dst_ref=totals.at[peer],
            send_sem=send_b.at[peer], recv_sem=recv_b.at[peer],
            device_id=device, device_id_type=MESH,
        )

    for step in range(1, groups):
        peer, copy = send_total(step)
        pl.when(peer > mine)(copy.start)

    before = [None] * heads
    before[1] = maps[0]
    before[2] = pairs[0]
    before[4] = quads[0]
    before[3] = after(maps[2], pairs[0])
    before[5] = after(maps[4], quads[0])
    before[6] = after(pairs[2], quads[0])
    before[7] = after(maps[6], before[6])

    for step in range(1, groups):
        peer, copy = take_total(step)
        pl.when(peer < mine)(copy.wait_recv)

    eye_zero = jnp.concatenate([jnp.where(eye, 1.0, 0.0), jnp.zeros((W, W), F32)], axis=1)
    chain = [jnp.where(j < mine, unpack_map(totals[j])[0], eye_zero) for j in range(groups - 1)]
    while len(chain) > 1:
        joined = []
        for i in range(0, len(chain) - 1, 2):
            first = chain[i] if i else chain[i][:, W:]
            joined.append(after(chain[i + 1], first))
        if len(chain) % 2:
            joined.append(chain[-1])
        if joined[0].shape[1] == W:
            joined[0] = jnp.concatenate([jnp.zeros((W, W), F32), joined[0]], axis=1)
        chain = joined
    start = chain[0][:, W:]

    states[0] = start.astype(BF16)
    stacked = mm4(jnp.concatenate([b[:, :W] for b in before[1:]], axis=0), start)
    for i in range(1, heads):
        states[i] = (stacked[(i - 1) * W : i * W] + before[i][:, W:]).astype(BF16)

    def send_state(step):
        peer, device = member(step)
        return pltpu.make_async_remote_copy(
            src_ref=states.at[peer], dst_ref=state_in.at[rank],
            send_sem=send_c.at[peer], recv_sem=recv_c.at[rank],
            device_id=device, device_id_type=MESH,
        )

    def take_state(step):
        peer, device = member(step)
        return pltpu.make_async_remote_copy(
            src_ref=states.at[peer], dst_ref=state_in.at[peer],
            send_sem=send_c.at[peer], recv_sem=recv_c.at[peer],
            device_id=device, device_id_type=MESH,
        )

    for step in range(1, heads):
        send_state(step).start()
    state_in[rank] = states[rank]
    for step in range(1, heads):
        take_state(step).wait_recv()

    gated = []
    for h in range(heads):
        cols = slice(h * W, (h + 1) * W)
        raw = base[:, cols] + mm(carry[:, cols], state_in[h])
        raw = raw * lax.rsqrt(jnp.mean(raw * raw, axis=-1, keepdims=True) + EPS)
        logits = gate[:, cols].astype(F32)
        gated.append((raw * out_gain[...] / (1.0 + jnp.exp(-logits))).astype(BF16))
    gated = jnp.concatenate(gated, axis=1)

    loads[0].wait()
    width = partial.shape[2]

    def swap(p):
        return pltpu.make_async_remote_copy(
            src_ref=partial.at[p], dst_ref=other.at[p],
            send_sem=send_p.at[p], recv_sem=recv_p.at[p],
            device_id=sibling, device_id_type=MESH,
        )

    for p in range(PIECES):
        partial[p] = mm(gated, ow[:, p * width : (p + 1) * width])
        swap(p).start()
    squares = 0.0
    hidden = []
    for p in range(PIECES):
        cols = slice(p * width, (p + 1) * width)
        swap(p).wait_recv()
        summed = residual[:, cols].astype(F32) + (partial[p] + other[p])
        rounded = summed.astype(BF16)
        hidden_o[:, cols] = rounded
        rounded = rounded.astype(F32)
        squares = squares + jnp.sum(rounded * rounded, axis=-1, keepdims=True)
        hidden.append(rounded)
    scale = lax.rsqrt(squares / (PIECES * width) + EPS)
    normed = jnp.concatenate(hidden, axis=1) * scale * hidden_gain[...]
    normed = normed.astype(BF16)
    loads[1].wait()
    latent = mm(normed, lw[...])
    latent = latent * lax.rsqrt(jnp.mean(latent * latent, axis=-1, keepdims=True) + EPS)
    latent_o[...] = (latent * latent_gain[...]).astype(BF16)
    loads[2].wait()
    loads[3].wait()
    queries = mm(normed, qw[...]).astype(BF16)
    for h in range(heads):
        cols = slice(h * W, (h + 1) * W)
        qp_o[h] = (mm_nt(queries[:, cols], ku[:, cols]) * SCORE_SCALE).astype(BF16)

    for step in range(1, heads):
        send_map(step).wait_send()
        send_state(step).wait_send()
    for step in range(1, groups):
        peer, copy = send_total(step)
        pl.when(peer > mine)(copy.wait_send)
    for p in range(PIECES):
        swap(p).wait_send()


SCORE_SCALE = W ** (-0.5) * 1.4426950408889634


def carry_layer(msg, base, carry, gate, out_gain, residual, hidden_gain, latent_gain, ow, lw, qw, ku):
    heads = msg.shape[0]
    rows, width = residual.shape
    latent = lw.shape[1]
    groups = lax.axis_size("seq") // heads
    vm = pl.BlockSpec(memory_space=pltpu.VMEM)
    anywhere = pl.BlockSpec(memory_space=pl.ANY)
    dma = pltpu.SemaphoreType.DMA
    return pl.pallas_call(
        carry_kernel,
        out_shape=(
            jax.ShapeDtypeStruct((rows, width), BF16),
            jax.ShapeDtypeStruct((heads, rows, latent), BF16),
            jax.ShapeDtypeStruct((rows, latent), BF16),
        ),
        in_specs=[vm] * 8 + [anywhere] * 4,
        out_specs=(vm, vm, vm),
        scratch_shapes=[
            pltpu.VMEM(msg.shape, BF16),
            pltpu.VMEM(msg.shape[1:], BF16),
            pltpu.VMEM((groups,) + msg.shape[1:], BF16),
            pltpu.VMEM((heads, W, W), BF16),
            pltpu.VMEM((heads, W, W), BF16),
            pltpu.VMEM((PIECES, rows, width // PIECES), F32),
            pltpu.VMEM((PIECES, rows, width // PIECES), F32),
            pltpu.VMEM(ow.shape, BF16),
            pltpu.VMEM(lw.shape, BF16),
            pltpu.VMEM(qw.shape, BF16),
            pltpu.VMEM(ku.shape, BF16),
            dma((heads,)), dma((heads,)), dma((groups,)), dma((groups,)),
            dma((heads,)), dma((heads,)), dma((PIECES,)), dma((PIECES,)), dma((4,)),
        ],
        compiler_params=pltpu.CompilerParams(
            collective_id=0, has_side_effects=True, vmem_limit_bytes=56 * 2**20
        ),
        name="carry_layer",
    )(msg, base, carry, gate, out_gain, residual, hidden_gain, latent_gain, ow, lw, qw, ku)


RING = 4
HALF = 64
GROUP = 4


def attend_kernel(
    qp_ref, vu_ref, latent_ref, out_ref, lat, row_max, row_sum, accum,
    send_y, recv_y, send_b, recv_b, send_a, recv_a, send_s, recv_s,
):
    heads, rows, latent = qp_ref.shape
    here, core = lax.axis_index("seq"), lax.axis_index("head")
    y, x, z = here // (RING * RING), (here // RING) % RING, here % RING
    mine_a = jnp.where(core == 0, z, x)
    mine_b = jnp.where(core == 0, x, z)
    piece_rows = RING * HALF

    def device(to_y, to_a, to_b):
        inside = jnp.where(core == 0, to_b * RING + to_a, to_a * RING + to_b)
        return (to_y * RING * RING + inside, core)

    sibling = (here, 1 - core)

    def other(coordinate, step):
        return (coordinate + step) % RING

    barrier = pltpu.get_barrier_semaphore()
    for step in range(1, RING):
        for peer in (
            device(other(y, step), mine_a, mine_b),
            device(y, other(mine_a, step), mine_b),
            device(y, mine_a, other(mine_b, step)),
        ):
            pl.semaphore_signal(barrier, inc=1, device_id=peer, device_id_type=MESH)
    pl.semaphore_signal(barrier, inc=1, device_id=sibling, device_id_type=MESH)
    pl.semaphore_wait(barrier, 3 * (RING - 1) + 1)

    def remote(place, peer, send, recv):
        return pltpu.make_async_remote_copy(
            src_ref=place, dst_ref=place, send_sem=send, recv_sem=recv,
            device_id=peer, device_id_type=MESH,
        )

    def over_y(step):
        peer = device(other(y, step), mine_a, mine_b)
        return other(y, step), remote(
            lat.at[core, y, mine_a, mine_b], peer, send_y.at[step], recv_y.at[y]
        )

    def from_y(at):
        return remote(
            lat.at[core, at, mine_a, mine_b], sibling, send_y.at[0], recv_y.at[at]
        )

    def over_b(at, step):
        return remote(
            lat.at[core, at, mine_a, mine_b], device(y, mine_a, other(mine_b, step)),
            send_b.at[at, step], recv_b.at[at, RING - step],
        )

    def from_b(at, step):
        return remote(
            lat.at[core, at, mine_a, other(mine_b, step)], sibling,
            send_b.at[at, 0], recv_b.at[at, step],
        )

    def over_a(at, step):
        return remote(
            lat.at[core, at, mine_a], device(y, other(mine_a, step), mine_b),
            send_a.at[at, step], recv_a.at[at, RING - step],
        )

    def from_a(at, step):
        return remote(
            lat.at[core, at, other(mine_a, step)], sibling, send_a.at[at, 0], recv_a.at[at, step]
        )

    def to_sibling(at, step):
        return remote(
            lat.at[core, at, other(mine_a, step)], sibling, send_s.at[at, step], recv_s.at[at, step]
        )

    def from_sibling(at, step):
        return remote(
            lat.at[1 - core, at, other(mine_b, step)], sibling,
            send_s.at[at, step], recv_s.at[at, step],
        )

    lat[core, y, mine_a, mine_b] = latent_ref[pl.ds(pl.multiple_of(core * HALF, HALF), HALF), :]
    for step in range(1, RING):
        peer_y, copy = over_y(step)
        pl.when(peer_y > y)(copy.start)

    def spread(at):
        for step in range(1, RING):
            over_b(at, step).start()

    def complete(at):
        for step in range(1, RING):
            from_b(at, step).wait_recv()
        for step in (1, 3, 2):
            over_a(at, step).start()
        to_sibling(at, 0).start()

    spread(y)
    for at in range(RING - 1):

        @pl.when(at < y)
        def _():
            from_y(at).wait_recv()
            spread(at)

    row_max[...] = jnp.full(row_max.shape, -1e30, F32)
    row_sum[...] = jnp.zeros(row_sum.shape, F32)
    accum[...] = jnp.zeros(accum.shape, F32)
    block = GROUP * rows

    complete(y)
    for at in range(RING - 1):
        pl.when(at < y)(functools.partial(complete, at))

    def work(at, step, masked):
        first_a, second_a = other(z, step), other(x, step)
        keys = (
            lat[0, at, first_a].reshape(piece_rows, latent),
            lat[1, at, second_a].reshape(piece_rows, latent),
        )
        for b in range(0, heads, GROUP):
            place = slice(b * rows, b * rows + block)
            queries = qp_ref[b : b + GROUP].reshape(block, latent)
            scores = [mm_nt(queries, part) for part in keys]
            if masked:
                query_pos = here * rows + iota((block, piece_rows), 0) % rows
                column = iota((block, piece_rows), 1)
                slot, inner = column // HALF, column % HALF
                first_pos = (at * RING * RING + slot * RING + first_a) * rows + inner
                second_pos = (at * RING * RING + second_a * RING + slot) * rows + HALF + inner
                scores = [
                    jnp.where(pos <= query_pos, part, -2e30)
                    for pos, part in zip((first_pos, second_pos), scores)
                ]
            old = row_max[place, :]
            top = jnp.maximum(scores[0], scores[1])
            new = jnp.maximum(old, jnp.max(top, axis=-1, keepdims=True))
            row_max[place, :] = new
            shrink = jnp.exp2(old - new)
            added = row_sum[place, :] * shrink
            mixed = accum[place, :] * jnp.concatenate([shrink] * (latent // W), axis=1)
            for part, key in zip(scores, keys):
                probs = [jnp.exp2(part[:, c : c + W] - new) for c in range(0, piece_rows, W)]
                for p in probs:
                    added = added + p
                mixed = mixed + mm(jnp.concatenate([p.astype(BF16) for p in probs], axis=1), key)
            row_sum[place, :] = added
            accum[place, :] = mixed

    def near(at, masked):
        from_sibling(at, 0).wait_recv()
        work(at, 0, masked)

    def far(at, step, masked):
        from_a(at, step).wait_recv()
        to_sibling(at, step).start()
        from_sibling(at, step).wait_recv()
        work(at, step, masked)

    def loop(lower, upper, visit):
        lax.fori_loop(lower, upper, lambda i, nothing: (visit(i), nothing)[1], 0)

    near(y, True)
    loop(0, y, lambda at: near(at, False))

    def round_of(step):
        far(y, step, True)
        loop(0, y, lambda at: far(at, step, False))

    loop(1, RING, round_of)

    for h in range(heads):
        place = slice(h * rows, (h + 1) * rows)
        total = jnp.sum(row_sum[place, :], axis=-1, keepdims=True)
        mixed = accum[place, :] / total
        high, low = halves(mixed)
        cols = slice(h * W, (h + 1) * W)
        up = vu_ref[:, cols]
        out_ref[:, cols] = (mm(high, up) + mm(low, up)).astype(BF16)

    for step in range(1, RING):
        peer_y, copy = over_y(step)
        pl.when(peer_y > y)(copy.wait_send)

    def drain(at):
        for step in range(1, RING):
            over_b(at, step).wait_send()
            over_a(at, step).wait_send()
        for step in range(RING):
            to_sibling(at, step).wait_send()

    loop(0, y + 1, drain)


def attend(qp, vu, latent):
    heads, rows, width = qp.shape
    vm = pl.BlockSpec(memory_space=pltpu.VMEM)
    dma = pltpu.SemaphoreType.DMA
    ring = (RING, RING)
    return pl.pallas_call(
        attend_kernel,
        out_shape=jax.ShapeDtypeStruct((rows, heads * W), BF16),
        in_specs=[vm, vm, vm],
        out_specs=vm,
        scratch_shapes=[
            pltpu.VMEM((2, RING, RING, RING, HALF, width), BF16),
            pltpu.VMEM((heads * rows, W), F32),
            pltpu.VMEM((heads * rows, W), F32),
            pltpu.VMEM((heads * rows, width), F32),
            dma((RING,)), dma((RING,)), dma(ring), dma(ring), dma(ring), dma(ring), dma(ring), dma(ring),
        ],
        compiler_params=pltpu.CompilerParams(
            collective_id=1, has_side_effects=True, vmem_limit_bytes=56 * 2**20
        ),
        name="attend",
    )(qp, vu, latent)


def body(
    residual, kda_query, kda_key, kda_value, log_decay, beta_logit, out_gate, out_gain, out_weight,
    hidden_gain, query_weight, latent_weight, latent_gain, key_up_weight, value_up_weight,
):
    msg, base, carry = delta_terms(kda_query, kda_key, kda_value, log_decay, beta_logit)
    hidden, qp, latent = carry_layer(
        msg, base, carry, out_gate, out_gain[None], residual, hidden_gain[None], latent_gain[None],
        out_weight, latent_weight, query_weight, key_up_weight,
    )
    return hidden, attend(qp, value_up_weight, latent)


def solution(mesh):
    in_specs = (
        P("seq", None),
        P("seq", "head"),
        P("seq", "head"),
        P("seq", "head"),
        P("seq", "head"),
        P("seq", "head"),
        P("seq", "head"),
        P(),
        P("head", None),
        P(),
        P(None, "head"),
        P(),
        P(),
        P(None, "head"),
        P(None, "head"),
    )
    out_specs = (P("seq", None), P("seq", "head"))
    return jax.shard_map(body, mesh=mesh, in_specs=in_specs, out_specs=out_specs, check_vma=False)
```

```python
import functools
import jax
import jax.numpy as jnp
from jax import lax
from jax.sharding import PartitionSpec as P
from jax.experimental import pallas as pl
from jax.experimental.pallas import tpu as pltpu

F32 = jnp.float32
BF16 = jnp.bfloat16
W = 128
EPS = 1e-06


def halves(x):
    high = x.astype(BF16)
    return high, (x - high.astype(F32)).astype(BF16)


def mm(a, b):
    return jnp.dot(a, b, preferred_element_type=F32)


def mm_nt(a, b):
    return lax.dot_general(a, b, (((1,), (1,)), ((), ())), preferred_element_type=F32)


def wide(x):
    high, low = halves(x)
    return jnp.concatenate([high, low], axis=1)


def mm4(a, b):
    n = b.shape[1]
    right = wide(b)
    out = mm(wide(a), jnp.concatenate([right, right], axis=0))
    return out[:, :n] + out[:, n:]


def mm4_nt(a, b):
    n = b.shape[0]
    high, low = halves(b)
    right = jnp.concatenate(
        [jnp.concatenate([high, high], axis=1), jnp.concatenate([low, low], axis=1)], axis=0
    )
    out = mm_nt(wide(a), right)
    return out[:, :n] + out[:, n:]


def iota(shape, axis):
    return lax.broadcasted_iota(jnp.int32, shape, axis)


PIECES = 3
MESH = pl.DeviceIdType.MESH
SCORE_SCALE = W ** (-0.5) * 1.4426950408889634
RING = 4
PART = 32
GROUP = 4


def pack_diag(closing):
    high, rest = halves(closing)
    r = iota((16, W), 0)
    block = jnp.where(r == 0, high.astype(F32), jnp.where(r == 1, rest.astype(F32), 0.0))
    return jnp.concatenate([block, jnp.zeros((16, W), F32)], axis=1).astype(BF16)


def unpack_map(block):
    diag = block[W : W + 1, :W].astype(F32) + block[W + 1 : W + 2, :W].astype(F32)
    eye = iota((W, W), 0) == iota((W, W), 1)
    matrix = jnp.where(eye, diag, 0.0) - block[:W, :W].astype(F32)
    return jnp.concatenate([matrix, block[:W, W:].astype(F32)], axis=1), diag


def after(later, earlier):
    n = earlier.shape[1]
    out = mm4(later[:, :W], earlier)
    if n == 2 * W:
        return jnp.concatenate([out[:, :W], out[:, W:] + later[:, W:]], axis=1)
    return out + later[:, W:]


def delta_part(q_ref, k_ref, v_ref, ld_ref, beta_ref, msg_ref, base_ref, carry_ref, sent):
    rows = q_ref.shape[0]
    heads = q_ref.shape[1] // W
    ti, si = iota((rows, rows), 0), iota((rows, rows), 1)
    ones = jnp.where(si <= ti, 1.0, 0.0).astype(BF16)
    strict = si < ti
    through = si <= ti
    eye = jnp.where(si == ti, 1.0, 0.0)
    rates = (1.0 / (1.0 + jnp.exp(-beta_ref[...]))).T

    def stage_one(h):
        cols = slice(h * W, (h + 1) * W)
        ld = ld_ref[:, cols]
        high, rest = halves(ld)
        low = (ld - high.astype(F32) - rest.astype(F32)).astype(BF16)
        cum = mm(ones, high) + (mm(ones, rest) + mm(ones, low))
        mid = cum[rows // 2 - 1 : rows // 2, :]
        end = cum[rows - 1 : rows, :]
        key = k_ref[:, cols].astype(F32)
        key = key * lax.rsqrt(jnp.sum(key * key, axis=-1, keepdims=True) + EPS)
        query = q_ref[:, cols].astype(F32)
        query = query * lax.rsqrt(jnp.sum(query * query, axis=-1, keepdims=True) + EPS)
        forward = jnp.exp(cum - mid)
        mixed = mm4_nt(
            jnp.concatenate([key * forward, query * forward], axis=0), key * jnp.exp(mid - cum)
        )
        rate = rates[:, h : h + 1]
        lower = jnp.where(strict, mixed[:rows], 0.0) * rate
        mix = jnp.where(through, mixed[rows:], 0.0)
        growth = jnp.exp(cum)
        right = jnp.concatenate(
            [rate * v_ref[:, cols].astype(F32), rate * (key * growth)], axis=1
        )
        tail = (key * jnp.exp(end - cum)).T
        return lower, mix, right, tail, query * growth, jnp.exp(end)

    def invert(lowers):
        level = jnp.logical_and((ti // 2) == (si // 2), strict)
        found = [eye - jnp.where(level, low, 0.0) for low in lowers]
        size = 2
        while size < rows:
            level = jnp.logical_and((ti // (2 * size)) == (si // (2 * size)),
                                    (ti // size) > (si // size))
            inner = [mm4(jnp.where(level, low, 0.0), x) for low, x in zip(lowers, found)]
            found = [x - mm4(x, y) for x, y in zip(found, inner)]
            size *= 2
        return found

    group = 4
    for start in range(0, heads, group):
        made = [stage_one(h) for h in range(start, start + group)]
        inverses = invert([m[0] for m in made])
        for h in range(start, start + group):
            _, mix, right, tail, query, closing = made[h - start]
            solved = mm4(inverses[h - start], right)
            state = mm4(tail, solved)
            out = mm4(mix, solved)
            cols = slice(h * W, (h + 1) * W)
            base_ref[:, cols] = out[:, :W]
            carry_ref[:, cols] = (query - out[:, W:]).astype(BF16)
            msg_ref[h, :W, :W] = state[:, W:].astype(BF16)
            msg_ref[h, :W, W:] = state[:, :W].astype(BF16)
            msg_ref[h, W:, :] = pack_diag(closing)
        sent(start, start + group)


def layer_kernel(
    q_hbm, k_hbm, v_hbm, ld_hbm, beta_hbm, gate_hbm, residual_hbm, out_gain_hbm, hidden_gain_hbm,
    latent_gain_hbm, ow_hbm, lw_hbm, qw_hbm, ku_hbm, vu_hbm,
    hidden_o, out_ref,
    q_in, k_in, v_in, ld_in, beta_in, gate, residual, out_gain, hidden_gain, latent_gain, ow, lw, qw, ku, vu_ref,
    msg, base, carry, got, total, totals, states, state_in, partial, other,
    qp_ref, lat_a, lat_b, row_max, row_sum, accum,
    load_sem, send_a, recv_a, send_b, recv_b, send_c, recv_c, send_p, recv_p,
    sa1, ra1, sa2, ra2, sa3, ra3, sb1, rb1, sb2, rb2, sb3, rb3, swap_a, got_a, swap_b, got_b,
):
    heads = msg.shape[0]
    groups = totals.shape[0]
    rows, latent = residual.shape[0], lw.shape[1]
    here, core = lax.axis_index("seq"), lax.axis_index("head")
    mine, rank = here // heads, here % heads
    y, x, z = here // (RING * RING), (here // RING) % RING, here % RING
    line = RING * PART
    sibling = (here, 1 - core)

    def device(to_y, to_x, to_z):
        return (to_y * RING * RING + to_x * RING + to_z, core)

    def turn(coordinate, step):
        return (coordinate + step) % RING

    def member(step):
        peer = (rank + step) % heads
        return peer, (mine * heads + peer, core)

    def cousin(step):
        peer = (mine + step) % groups
        return peer, (peer * heads + rank, core)

    barrier = pltpu.get_barrier_semaphore()
    for step in range(1, heads):
        pl.semaphore_signal(barrier, inc=1, device_id=member(step)[1], device_id_type=MESH)
    for step in range(1, groups):
        pl.semaphore_signal(barrier, inc=1, device_id=cousin(step)[1], device_id_type=MESH)
    pl.semaphore_signal(barrier, inc=1, device_id=sibling, device_id_type=MESH)
    pl.semaphore_signal(barrier, inc=1, device_id=device(y, RING - 1 - x, z), device_id_type=MESH)

    pairs = (
        (k_hbm, k_in), (ld_hbm, ld_in), (q_hbm, q_in), (v_hbm, v_in), (beta_hbm, beta_in), (gate_hbm, gate),
        (residual_hbm, residual), (out_gain_hbm, out_gain), (hidden_gain_hbm, hidden_gain),
        (latent_gain_hbm, latent_gain), (ow_hbm, ow), (lw_hbm, lw), (qw_hbm, qw), (ku_hbm, ku), (vu_hbm, vu_ref),
    )
    loads = [pltpu.make_async_copy(src, dst, load_sem.at[i]) for i, (src, dst) in enumerate(pairs)]
    for load in loads:
        load.start()
    for load in loads[:5]:
        load.wait()

    def map_to(peer):
        return pltpu.make_async_remote_copy(
            src_ref=msg.at[peer], dst_ref=got.at[rank],
            send_sem=send_a.at[peer], recv_sem=recv_a.at[rank],
            device_id=(mine * heads + peer, core), device_id_type=MESH,
        )

    def map_from(peer):
        return pltpu.make_async_remote_copy(
            src_ref=msg.at[peer], dst_ref=got.at[peer],
            send_sem=send_a.at[peer], recv_sem=recv_a.at[peer],
            device_id=(mine * heads + peer, core), device_id_type=MESH,
        )

    def sent(begin, end):
        if begin == 0:
            pl.semaphore_wait(barrier, heads + groups)
        for peer in range(begin, end):
            pl.when(peer != rank)(map_to(peer).start)

    delta_part(q_in, k_in, v_in, ld_in, beta_in, msg, base, carry, sent)
    got[rank] = msg[rank]
    for step in range(1, heads):
        map_from(member(step)[0]).wait_recv()

    maps, diags = [], []
    for i in range(heads):
        matrix, diag = unpack_map(got[i])
        maps.append(matrix)
        diags.append(diag)
    pairs = [after(maps[i + 1], maps[i]) for i in range(0, heads, 2)]
    quads = [after(pairs[i + 1], pairs[i]) for i in range(0, len(pairs), 2)]
    whole = after(quads[1], quads[0])
    diag = diags[0]
    for other_diag in diags[1:]:
        diag = diag * other_diag
    eye = iota((W, W), 0) == iota((W, W), 1)
    total[:W, :W] = (jnp.where(eye, diag, 0.0) - whole[:, :W]).astype(BF16)
    total[:W, W:] = whole[:, W:].astype(BF16)
    total[W:, :] = pack_diag(diag)

    def send_total(step):
        peer, device = cousin(step)
        return peer, pltpu.make_async_remote_copy(
            src_ref=total, dst_ref=totals.at[mine],
            send_sem=send_b.at[peer], recv_sem=recv_b.at[mine],
            device_id=device, device_id_type=MESH,
        )

    def take_total(step):
        peer, device = cousin(step)
        return peer, pltpu.make_async_remote_copy(
            src_ref=total, dst_ref=totals.at[peer],
            send_sem=send_b.at[peer], recv_sem=recv_b.at[peer],
            device_id=device, device_id_type=MESH,
        )

    for step in range(1, groups):
        peer, copy = send_total(step)
        pl.when(peer > mine)(copy.start)

    before = [None] * heads
    before[1] = maps[0]
    before[2] = pairs[0]
    before[4] = quads[0]
    before[3] = after(maps[2], pairs[0])
    before[5] = after(maps[4], quads[0])
    before[6] = after(pairs[2], quads[0])
    before[7] = after(maps[6], before[6])

    for step in range(1, groups):
        peer, copy = take_total(step)
        pl.when(peer < mine)(copy.wait_recv)

    eye_zero = jnp.concatenate([jnp.where(eye, 1.0, 0.0), jnp.zeros((W, W), F32)], axis=1)
    chain = [jnp.where(j < mine, unpack_map(totals[j])[0], eye_zero) for j in range(groups - 1)]
    while len(chain) > 1:
        joined = []
        for i in range(0, len(chain) - 1, 2):
            first = chain[i] if i else chain[i][:, W:]
            joined.append(after(chain[i + 1], first))
        if len(chain) % 2:
            joined.append(chain[-1])
        if joined[0].shape[1] == W:
            joined[0] = jnp.concatenate([jnp.zeros((W, W), F32), joined[0]], axis=1)
        chain = joined
    start = chain[0][:, W:]

    states[0] = start.astype(BF16)
    stacked = mm4(jnp.concatenate([b[:, :W] for b in before[1:]], axis=0), start)
    for i in range(1, heads):
        states[i] = (stacked[(i - 1) * W : i * W] + before[i][:, W:]).astype(BF16)

    def send_state(step):
        peer, device = member(step)
        return pltpu.make_async_remote_copy(
            src_ref=states.at[peer], dst_ref=state_in.at[rank],
            send_sem=send_c.at[peer], recv_sem=recv_c.at[rank],
            device_id=device, device_id_type=MESH,
        )

    def take_state(step):
        peer, device = member(step)
        return pltpu.make_async_remote_copy(
            src_ref=states.at[peer], dst_ref=state_in.at[peer],
            send_sem=send_c.at[peer], recv_sem=recv_c.at[peer],
            device_id=device, device_id_type=MESH,
        )

    for step in range(1, heads):
        send_state(step).start()
    state_in[rank] = states[rank]
    for step in range(1, heads):
        take_state(step).wait_recv()

    for load in loads[5:10]:
        load.wait()
    gated = []
    for h in range(heads):
        cols = slice(h * W, (h + 1) * W)
        raw = base[:, cols] + mm(carry[:, cols], state_in[h])
        raw = raw * lax.rsqrt(jnp.mean(raw * raw, axis=-1, keepdims=True) + EPS)
        logits = gate[:, cols].astype(F32)
        gated.append((raw * out_gain[...] / (1.0 + jnp.exp(-logits))).astype(BF16))
    gated = jnp.concatenate(gated, axis=1)

    loads[10].wait()
    width = partial.shape[2]

    def swap(p):
        return pltpu.make_async_remote_copy(
            src_ref=partial.at[p], dst_ref=other.at[p],
            send_sem=send_p.at[p], recv_sem=recv_p.at[p],
            device_id=sibling, device_id_type=MESH,
        )

    for p in range(PIECES):
        partial[p] = mm(gated, ow[:, p * width : (p + 1) * width])
        swap(p).start()
    squares = 0.0
    hidden = []
    for p in range(PIECES):
        cols = slice(p * width, (p + 1) * width)
        swap(p).wait_recv()
        summed = residual[:, cols].astype(F32) + (partial[p] + other[p])
        rounded = summed.astype(BF16)
        hidden_o[:, cols] = rounded
        rounded = rounded.astype(F32)
        squares = squares + jnp.sum(rounded * rounded, axis=-1, keepdims=True)
        hidden.append(rounded)
    scale = lax.rsqrt(squares / (PIECES * width) + EPS)
    gain = jnp.concatenate([hidden_gain[i : i + 1] for i in range(hidden_gain.shape[0])], axis=1)
    normed = jnp.concatenate(hidden, axis=1) * scale * gain
    normed = normed.astype(BF16)
    loads[11].wait()
    raw = mm(normed, lw[...])
    raw = raw * lax.rsqrt(jnp.mean(raw * raw, axis=-1, keepdims=True) + EPS)
    raw = (raw * latent_gain[...]).astype(BF16)

    def place_parts(which):
        first = which * 2 * PART
        lat_a[core, y, x, z] = raw[first : first + PART]
        lat_b[core, y, z, x] = raw[first + PART : first + 2 * PART]

    for which in range(2):
        pl.when(core == which)(functools.partial(place_parts, which))
    def remote(place, peer, send, recv):
        return pltpu.make_async_remote_copy(
            src_ref=place, dst_ref=place, send_sem=send, recv_sem=recv,
            device_id=peer, device_id_type=MESH,
        )

    def a_over_z(step):
        return remote(lat_a.at[core, y, x, z], device(y, x, turn(z, step)), sa1.at[step], ra1.at[RING - step])

    def a_from_z(step):
        return remote(lat_a.at[core, y, x, turn(z, step)], sibling, sa1.at[0], ra1.at[step])

    def a_over_x(step):
        return remote(lat_a.at[core, y, x], device(y, turn(x, step), z), sa2.at[step], ra2.at[RING - step])

    def a_from_x(step):
        return remote(lat_a.at[core, y, turn(x, step)], sibling, sa2.at[0], ra2.at[step])

    def a_over_y(to, step):
        return remote(
            lat_a.at[core, y, turn(x, step)], device(to, x, z), sa3.at[to, step], ra3.at[y, step]
        )

    def a_from_y(at, step):
        return remote(lat_a.at[core, at, turn(x, step)], sibling, sa3.at[at, 0], ra3.at[at, step])

    def b_over_y(to):
        return remote(lat_b.at[core, y, z, x], device(to, x, z), sb1.at[to], rb1.at[y])

    def b_from_y(at):
        return remote(lat_b.at[core, at, z, x], sibling, sb1.at[at], rb1.at[at])

    def b_over_x(at, step):
        return remote(
            lat_b.at[core, at, z, x], device(y, turn(x, step), z), sb2.at[at, step], rb2.at[at, RING - step]
        )

    def b_from_x(at, step):
        return remote(lat_b.at[core, at, z, turn(x, step)], sibling, sb2.at[at, 0], rb2.at[at, step])

    def b_over_z(at, step):
        return remote(
            lat_b.at[core, at, z], device(y, x, turn(z, step)), sb3.at[at, step], rb3.at[at, RING - step]
        )

    def b_from_z(at, step):
        return remote(lat_b.at[core, at, turn(z, step)], sibling, sb3.at[at, 0], rb3.at[at, step])

    def give_a(at, step):
        return remote(lat_a.at[core, at, turn(x, step)], sibling, swap_a.at[at, step], got_a.at[at, step])

    def take_a(at, step):
        return remote(lat_a.at[1 - core, at, turn(x, step)], sibling, swap_a.at[at, step], got_a.at[at, step])

    def give_b(at, step):
        return remote(lat_b.at[core, at, turn(z, step)], sibling, swap_b.at[at, step], got_b.at[at, step])

    def take_b(at, step):
        return remote(lat_b.at[1 - core, at, turn(z, step)], sibling, swap_b.at[at, step], got_b.at[at, step])

    others = (1, 3, 2)

    def higher(action):
        for to in range(1, RING):
            pl.when(to > y)(functools.partial(action, to))

    def lower(action):
        for at in range(RING - 2, -1, -1):
            pl.when(at < y)(functools.partial(action, at))

    for step in others:
        a_over_z(step).start()
    higher(lambda to: b_over_y(to).start())
    for step in others:
        b_over_x(y, step).start()

    row_max[...] = jnp.full(row_max.shape, -1e30, F32)
    row_sum[...] = jnp.zeros(row_sum.shape, F32)
    accum[...] = jnp.zeros(accum.shape, F32)
    block = GROUP * rows

    def spread_a(step):
        higher(lambda to: a_over_y(to, step).start())
        give_a(y, step).start()

    def spread_b(at):
        for step in others:
            b_from_x(at, step).wait_recv()
        for step in others:
            b_over_z(at, step).start()
        give_b(at, 0).start()

    loads[12].wait()
    queries = mm(normed, qw[...]).astype(BF16)
    for step in others:
        a_from_z(step).wait_recv()
    for step in others:
        a_over_x(step).start()
    spread_a(0)
    spread_b(y)

    def pass_b(at):
        b_from_y(at).wait_recv()
        for step in others:
            b_over_x(at, step).start()

    loads[13].wait()
    for h in range(heads):
        cols = slice(h * W, (h + 1) * W)
        qp_ref[h] = (mm_nt(queries[:, cols], ku[:, cols]) * SCORE_SCALE).astype(BF16)
    lower(pass_b)
    for step in others:
        a_from_x(step).wait_recv()
        spread_a(step)
    lower(spread_b)

    def work(at, pair, part, masked):
        steps = (pair * 2, pair * 2 + 1)
        if part == 0:
            places = [(turn(x, s), 0) for s in steps]
            keys = [
                lat_a[c, at, turn(x, s)].reshape(line, latent) for s in steps for c in range(2)
            ]
        else:
            keys = [
                lat_b[c, at, turn(z, s)].reshape(line, latent) for s in steps for c in range(2)
            ]
        count = len(keys) * line

        def positions(shape):
            column = iota(shape, 1)
            slot, inner = (column // PART) % RING, column % PART
            half = (column // line) % 2
            inner = inner + half * (2 * PART) + part * PART
            first_step = column < 2 * line
            if part == 0:
                block_x = jnp.where(first_step, turn(x, steps[0]), turn(x, steps[1]))
                chip = block_x * RING + slot
            else:
                block_z = jnp.where(first_step, turn(z, steps[0]), turn(z, steps[1]))
                chip = slot * RING + block_z
            return (at * RING * RING + chip) * rows + inner

        keys = jnp.concatenate(keys, axis=0)
        for b in range(0, heads, GROUP):
            place = slice(b * rows, b * rows + block)
            queries = qp_ref[b : b + GROUP].reshape(block, latent)
            scores = mm_nt(queries, keys)
            if masked:
                query_pos = here * rows + iota((block, count), 0) % rows
                scores = jnp.where(positions((block, count)) <= query_pos, scores, -2e30)
            old = row_max[place, :]
            new = jnp.maximum(old, jnp.max(scores, axis=-1, keepdims=True))
            row_max[place, :] = new
            shrink = jnp.exp2(old - new)
            probs = [jnp.exp2(scores[:, c : c + W] - new) for c in range(0, count, W)]
            added = row_sum[place, :] * shrink
            for p in probs:
                added = added + p
            row_sum[place, :] = added
            mixed = mm(jnp.concatenate([p.astype(BF16) for p in probs], axis=1), keys)
            accum[place, :] = accum[place, :] * jnp.concatenate([shrink] * (latent // W), axis=1) + mixed

    def fetch_a(at, pair):
        for s in range(2):
            step = pair * 2 + s
            a_from_y(at, step).wait_recv()
            give_a(at, step).start()

    def fetch_b(at, pair):
        for s in range(2):
            step = pair * 2 + s

            def far():
                b_from_z(at, step).wait_recv()
                give_b(at, step).start()

            pl.when(step > 0)(far)

    def ready_a(at, pair):
        for s in range(2):
            take_a(at, pair * 2 + s).wait_recv()

    def ready_b(at, pair):
        for s in range(2):
            take_b(at, pair * 2 + s).wait_recv()

    def loop(begin, end, visit):
        lax.fori_loop(begin, end, lambda i, nothing: (visit(i), nothing)[1], 0)

    fetch_b(y, 0)

    def own(pair):
        ready_a(y, pair)
        work(y, pair, 0, True)

        def next_a():
            fetch_a(y - 1, 0)

        pl.when(jnp.logical_and(pair == 1, y > 0))(next_a)
        pl.when(pair == 0)(lambda: fetch_b(y, 1))
        ready_b(y, pair)
        work(y, pair, 1, True)

    loop(0, 2, own)

    def earlier(i):
        at, pair = y - 1 - i // 2, i % 2
        fetch_b(at, pair)
        ready_a(at, pair)
        work(at, pair, 0, False)
        following = y - 1 - (i + 1) // 2

        @pl.when(following >= 0)
        def _():
            fetch_a(following, (i + 1) % 2)

        ready_b(at, pair)
        work(at, pair, 1, False)

    loop(0, 2 * y, earlier)

    loads[14].wait()
    for h in range(heads):
        place = slice(h * rows, (h + 1) * rows)
        row_total = jnp.sum(row_sum[place, :], axis=-1, keepdims=True)
        mixed = accum[place, :] / row_total
        high, low = halves(mixed)
        cols = slice(h * W, (h + 1) * W)
        up = vu_ref[:, cols]
        out_ref[:, cols] = (mm(high, up) + mm(low, up)).astype(BF16)

    for step in others:
        a_over_z(step).wait_send()
        a_over_x(step).wait_send()

    def drain_up(to):
        b_over_y(to).wait_send()
        for step in range(RING):
            a_over_y(to, step).wait_send()

    higher(drain_up)

    def drain(at):
        for step in range(1, RING):
            b_over_x(at, step).wait_send()
            b_over_z(at, step).wait_send()
        for step in range(RING):
            give_a(at, step).wait_send()
            give_b(at, step).wait_send()

    loop(0, y + 1, drain)


    for step in range(1, heads):
        map_to(member(step)[0]).wait_send()
        send_state(step).wait_send()
    for step in range(1, groups):
        peer, copy = send_total(step)
        pl.when(peer > mine)(copy.wait_send)
    for p in range(PIECES):
        swap(p).wait_send()


def layer(q, k, v, ld, beta, gate, residual, out_gain, hidden_gain, latent_gain, ow, lw, qw, ku, vu):
    heads = beta.shape[0]
    rows, width = residual.shape
    latent = lw.shape[1]
    groups = lax.axis_size("seq") // heads
    vm = pl.BlockSpec(memory_space=pltpu.VMEM)
    anywhere = pl.BlockSpec(memory_space=pl.ANY)
    dma = pltpu.SemaphoreType.DMA
    operands = (q, k, v, ld, beta, gate, residual, out_gain, hidden_gain, latent_gain, ow, lw, qw, ku, vu)
    message = (W + 16, 2 * W)
    one, two = dma((RING,)), dma((RING, RING))
    return pl.pallas_call(
        layer_kernel,
        out_shape=(
            jax.ShapeDtypeStruct((rows, width), BF16),
            jax.ShapeDtypeStruct((rows, heads * W), BF16),
        ),
        in_specs=[anywhere] * len(operands),
        out_specs=(vm, vm),
        scratch_shapes=[pltpu.VMEM(a.shape, a.dtype) for a in operands] + [
            pltpu.VMEM((heads,) + message, BF16),
            pltpu.VMEM((rows, heads * W), F32),
            pltpu.VMEM((rows, heads * W), BF16),
            pltpu.VMEM((heads,) + message, BF16),
            pltpu.VMEM(message, BF16),
            pltpu.VMEM((groups,) + message, BF16),
            pltpu.VMEM((heads, W, W), BF16),
            pltpu.VMEM((heads, W, W), BF16),
            pltpu.VMEM((PIECES, rows, width // PIECES), F32),
            pltpu.VMEM((PIECES, rows, width // PIECES), F32),
            pltpu.VMEM((heads, rows, latent), BF16),
            pltpu.VMEM((2, RING, RING, RING, PART, latent), BF16),
            pltpu.VMEM((2, RING, RING, RING, PART, latent), BF16),
            pltpu.VMEM((heads * rows, W), F32),
            pltpu.VMEM((heads * rows, W), F32),
            pltpu.VMEM((heads * rows, latent), F32),
            dma((len(operands),)),
            dma((heads,)), dma((heads,)), dma((groups,)), dma((groups,)),
            dma((heads,)), dma((heads,)), dma((PIECES,)), dma((PIECES,)),
            one, one, one, one, two, two, one, one, two, two, two, two, two, two, two, two,
        ],
        compiler_params=pltpu.CompilerParams(
            collective_id=0, has_side_effects=True, vmem_limit_bytes=60 * 2**20
        ),
        name="layer",
    )(*operands)


def body(
    residual, kda_query, kda_key, kda_value, log_decay, beta_logit, out_gate, out_gain, out_weight,
    hidden_gain, query_weight, latent_weight, latent_gain, key_up_weight, value_up_weight,
):
    return layer(
        kda_query, kda_key, kda_value, log_decay, beta_logit.T, out_gate, residual, out_gain[None],
        hidden_gain.reshape(-1, W), latent_gain[None], out_weight, latent_weight, query_weight, key_up_weight,
        value_up_weight,
    )


def solution(mesh):
    in_specs = (
        P("seq", None),
        P("seq", "head"),
        P("seq", "head"),
        P("seq", "head"),
        P("seq", "head"),
        P("seq", "head"),
        P("seq", "head"),
        P(),
        P("head", None),
        P(),
        P(None, "head"),
        P(),
        P(),
        P(None, "head"),
        P(None, "head"),
    )
    out_specs = (P("seq", None), P("seq", "head"))
    return jax.shard_map(body, mesh=mesh, in_specs=in_specs, out_specs=out_specs, check_vma=False)
```

```python
import functools
import jax
import jax.numpy as jnp
from jax import lax
from jax.sharding import PartitionSpec as P
from jax.experimental import pallas as pl
from jax.experimental.pallas import tpu as pltpu

F32 = jnp.float32
BF16 = jnp.bfloat16
W = 128
EPS = 1e-06


def halves(x):
    high = x.astype(BF16)
    return high, (x - high.astype(F32)).astype(BF16)


def mm(a, b):
    return jnp.dot(a, b, preferred_element_type=F32)


def mm_nt(a, b):
    return lax.dot_general(a, b, (((1,), (1,)), ((), ())), preferred_element_type=F32)


def wide(x):
    high, low = halves(x)
    return jnp.concatenate([high, low], axis=1)


def mm4(a, b):
    n = b.shape[1]
    right = wide(b)
    out = mm(wide(a), jnp.concatenate([right, right], axis=0))
    return out[:, :n] + out[:, n:]


def mm4_nt(a, b):
    n = b.shape[0]
    high, low = halves(b)
    right = jnp.concatenate(
        [jnp.concatenate([high, high], axis=1), jnp.concatenate([low, low], axis=1)], axis=0
    )
    out = mm_nt(wide(a), right)
    return out[:, :n] + out[:, n:]


def iota(shape, axis):
    return lax.broadcasted_iota(jnp.int32, shape, axis)


PIECES = 3
MESH = pl.DeviceIdType.MESH
SCORE_SCALE = W ** (-0.5) * 1.4426950408889634
RING = 4
PART = 32
GROUP = 8


def pack_diag(closing):
    high, rest = halves(closing)
    r = iota((16, W), 0)
    block = jnp.where(r == 0, high.astype(F32), jnp.where(r == 1, rest.astype(F32), 0.0))
    return jnp.concatenate([block, jnp.zeros((16, W), F32)], axis=1).astype(BF16)


def unpack_map(block):
    diag = block[W : W + 1, :W].astype(F32) + block[W + 1 : W + 2, :W].astype(F32)
    eye = iota((W, W), 0) == iota((W, W), 1)
    matrix = jnp.where(eye, diag, 0.0) - block[:W, :W].astype(F32)
    return jnp.concatenate([matrix, block[:W, W:].astype(F32)], axis=1), diag


def after(later, earlier):
    n = earlier.shape[1]
    out = mm4(later[:, :W], earlier)
    if n == 2 * W:
        return jnp.concatenate([out[:, :W], out[:, W:] + later[:, W:]], axis=1)
    return out + later[:, W:]


def delta_part(q_ref, k_ref, v_ref, ld_ref, beta_ref, msg_ref, base_ref, carry_ref, sent):
    rows = q_ref.shape[0]
    heads = q_ref.shape[1] // W
    ti, si = iota((rows, rows), 0), iota((rows, rows), 1)
    ones = jnp.where(si <= ti, 1.0, 0.0).astype(BF16)
    strict = si < ti
    through = si <= ti
    eye = jnp.where(si == ti, 1.0, 0.0)
    rates = (1.0 / (1.0 + jnp.exp(-beta_ref[...]))).T

    def stage_one(h):
        cols = slice(h * W, (h + 1) * W)
        ld = ld_ref[:, cols]
        high, rest = halves(ld)
        low = (ld - high.astype(F32) - rest.astype(F32)).astype(BF16)
        cum = mm(ones, high) + (mm(ones, rest) + mm(ones, low))
        mid = cum[rows // 2 - 1 : rows // 2, :]
        end = cum[rows - 1 : rows, :]
        key = k_ref[:, cols].astype(F32)
        key = key * lax.rsqrt(jnp.sum(key * key, axis=-1, keepdims=True) + EPS)
        query = q_ref[:, cols].astype(F32)
        query = query * lax.rsqrt(jnp.sum(query * query, axis=-1, keepdims=True) + EPS)
        forward = jnp.exp(cum - mid)
        mixed = mm4_nt(
            jnp.concatenate([key * forward, query * forward], axis=0), key * jnp.exp(mid - cum)
        )
        rate = rates[:, h : h + 1]
        lower = jnp.where(strict, mixed[:rows], 0.0) * rate
        mix = jnp.where(through, mixed[rows:], 0.0)
        growth = jnp.exp(cum)
        right = jnp.concatenate(
            [rate * v_ref[:, cols].astype(F32), rate * (key * growth)], axis=1
        )
        tail = (key * jnp.exp(end - cum)).T
        return lower, mix, right, tail, query * growth, jnp.exp(end)

    def invert(lowers):
        level = jnp.logical_and((ti // 2) == (si // 2), strict)
        found = [eye - jnp.where(level, low, 0.0) for low in lowers]
        size = 2
        while size < rows:
            level = jnp.logical_and((ti // (2 * size)) == (si // (2 * size)),
                                    (ti // size) > (si // size))
            inner = [mm4(jnp.where(level, low, 0.0), x) for low, x in zip(lowers, found)]
            found = [x - mm4(x, y) for x, y in zip(found, inner)]
            size *= 2
        return found

    group = 4
    for start in range(0, heads, group):
        made = [stage_one(h) for h in range(start, start + group)]
        inverses = invert([m[0] for m in made])
        for h in range(start, start + group):
            _, mix, right, tail, query, closing = made[h - start]
            solved = mm4(inverses[h - start], right)
            state = mm4(tail, solved)
            out = mm4(mix, solved)
            cols = slice(h * W, (h + 1) * W)
            base_ref[:, cols] = out[:, :W]
            carry_ref[:, cols] = (query - out[:, W:]).astype(BF16)
            msg_ref[h, :W, :W] = state[:, W:].astype(BF16)
            msg_ref[h, :W, W:] = state[:, :W].astype(BF16)
            msg_ref[h, W:, :] = pack_diag(closing)
        sent(start, start + group)


def layer_kernel(
    q_hbm, k_hbm, v_hbm, ld_hbm, beta_hbm, gate_hbm, residual_hbm, out_gain_hbm, hidden_gain_hbm,
    latent_gain_hbm, ow_hbm, lw_hbm, qw_hbm, ku_hbm, vu_hbm,
    hidden_o, out_ref,
    q_in, k_in, v_in, ld_in, beta_in, gate, residual, out_gain, hidden_gain, latent_gain, ow, lw, qw, ku, vu_ref,
    msg, base, carry, got, total, totals, states, state_in, partial, other,
    qp_ref, lat_a, lat_b, row_max, row_sum, accum, mail_out, mail_in, note_out, note_in,
    load_sem, send_a, recv_a, send_b, recv_b, send_c, recv_c, send_p, recv_p,
    sa1, ra1, sa2, ra2, sa3, ra3, sb1, rb1, sb2, rb2, sb3, rb3, swap_a, got_a, swap_b, got_b, sm, rm,
):
    heads = msg.shape[0]
    groups = totals.shape[0]
    rows, latent = residual.shape[0], lw.shape[1]
    here, core = lax.axis_index("seq"), lax.axis_index("head")
    mine, rank = here // heads, here % heads
    y, x, z = here // (RING * RING), (here // RING) % RING, here % RING
    line = RING * PART
    sibling = (here, 1 - core)

    def device(to_y, to_x, to_z):
        return (to_y * RING * RING + to_x * RING + to_z, core)

    def turn(coordinate, step):
        return (coordinate + step) % RING

    def member(step):
        peer = (rank + step) % heads
        return peer, (mine * heads + peer, core)

    def cousin(step):
        peer = (mine + step) % groups
        return peer, (peer * heads + rank, core)

    barrier = pltpu.get_barrier_semaphore()
    for step in range(1, heads):
        pl.semaphore_signal(barrier, inc=1, device_id=member(step)[1], device_id_type=MESH)
    for step in range(1, groups):
        pl.semaphore_signal(barrier, inc=1, device_id=cousin(step)[1], device_id_type=MESH)
    pl.semaphore_signal(barrier, inc=1, device_id=sibling, device_id_type=MESH)
    pl.semaphore_signal(barrier, inc=1, device_id=device(y, RING - 1 - x, z), device_id_type=MESH)

    pairs = (
        (k_hbm, k_in), (ld_hbm, ld_in), (q_hbm, q_in), (v_hbm, v_in), (beta_hbm, beta_in), (gate_hbm, gate),
        (residual_hbm, residual), (out_gain_hbm, out_gain), (hidden_gain_hbm, hidden_gain),
        (latent_gain_hbm, latent_gain), (ow_hbm, ow), (lw_hbm, lw), (qw_hbm, qw), (ku_hbm, ku), (vu_hbm, vu_ref),
    )
    loads = [pltpu.make_async_copy(src, dst, load_sem.at[i]) for i, (src, dst) in enumerate(pairs)]
    for load in loads:
        load.start()
    for load in loads[:5]:
        load.wait()

    def map_to(peer):
        return pltpu.make_async_remote_copy(
            src_ref=msg.at[peer], dst_ref=got.at[rank],
            send_sem=send_a.at[peer], recv_sem=recv_a.at[rank],
            device_id=(mine * heads + peer, core), device_id_type=MESH,
        )

    def map_from(peer):
        return pltpu.make_async_remote_copy(
            src_ref=msg.at[peer], dst_ref=got.at[peer],
            send_sem=send_a.at[peer], recv_sem=recv_a.at[peer],
            device_id=(mine * heads + peer, core), device_id_type=MESH,
        )

    def sent(begin, end):
        if begin == 0:
            pl.semaphore_wait(barrier, heads + groups)
        for peer in range(begin, end):
            pl.when(peer != rank)(map_to(peer).start)

    delta_part(q_in, k_in, v_in, ld_in, beta_in, msg, base, carry, sent)
    got[rank] = msg[rank]
    for step in range(1, heads):
        map_from(member(step)[0]).wait_recv()

    maps, diags = [], []
    for i in range(heads):
        matrix, diag = unpack_map(got[i])
        maps.append(matrix)
        diags.append(diag)
    pairs = [after(maps[i + 1], maps[i]) for i in range(0, heads, 2)]
    quads = [after(pairs[i + 1], pairs[i]) for i in range(0, len(pairs), 2)]
    whole = after(quads[1], quads[0])
    diag = diags[0]
    for other_diag in diags[1:]:
        diag = diag * other_diag
    eye = iota((W, W), 0) == iota((W, W), 1)
    total[:W, :W] = (jnp.where(eye, diag, 0.0) - whole[:, :W]).astype(BF16)
    total[:W, W:] = whole[:, W:].astype(BF16)
    total[W:, :] = pack_diag(diag)

    def send_total(step):
        peer, device = cousin(step)
        return peer, pltpu.make_async_remote_copy(
            src_ref=total, dst_ref=totals.at[mine],
            send_sem=send_b.at[peer], recv_sem=recv_b.at[mine],
            device_id=device, device_id_type=MESH,
        )

    def take_total(step):
        peer, device = cousin(step)
        return peer, pltpu.make_async_remote_copy(
            src_ref=total, dst_ref=totals.at[peer],
            send_sem=send_b.at[peer], recv_sem=recv_b.at[peer],
            device_id=device, device_id_type=MESH,
        )

    for step in range(1, groups):
        peer, copy = send_total(step)
        pl.when(peer > mine)(copy.start)

    before = [None] * heads
    before[1] = maps[0]
    before[2] = pairs[0]
    before[4] = quads[0]
    before[3] = after(maps[2], pairs[0])
    before[5] = after(maps[4], quads[0])
    before[6] = after(pairs[2], quads[0])
    before[7] = after(maps[6], before[6])

    for step in range(1, groups):
        peer, copy = take_total(step)
        pl.when(peer < mine)(copy.wait_recv)

    eye_zero = jnp.concatenate([jnp.where(eye, 1.0, 0.0), jnp.zeros((W, W), F32)], axis=1)
    chain = [jnp.where(j < mine, unpack_map(totals[j])[0], eye_zero) for j in range(groups - 1)]
    while len(chain) > 1:
        joined = []
        for i in range(0, len(chain) - 1, 2):
            first = chain[i] if i else chain[i][:, W:]
            joined.append(after(chain[i + 1], first))
        if len(chain) % 2:
            joined.append(chain[-1])
        if joined[0].shape[1] == W:
            joined[0] = jnp.concatenate([jnp.zeros((W, W), F32), joined[0]], axis=1)
        chain = joined
    start = chain[0][:, W:]

    states[0] = start.astype(BF16)
    stacked = mm4(jnp.concatenate([b[:, :W] for b in before[1:]], axis=0), start)
    for i in range(1, heads):
        states[i] = (stacked[(i - 1) * W : i * W] + before[i][:, W:]).astype(BF16)

    def send_state(step):
        peer, device = member(step)
        return pltpu.make_async_remote_copy(
            src_ref=states.at[peer], dst_ref=state_in.at[rank],
            send_sem=send_c.at[peer], recv_sem=recv_c.at[rank],
            device_id=device, device_id_type=MESH,
        )

    def take_state(step):
        peer, device = member(step)
        return pltpu.make_async_remote_copy(
            src_ref=states.at[peer], dst_ref=state_in.at[peer],
            send_sem=send_c.at[peer], recv_sem=recv_c.at[peer],
            device_id=device, device_id_type=MESH,
        )

    for step in range(1, heads):
        send_state(step).start()
    state_in[rank] = states[rank]
    for step in range(1, heads):
        take_state(step).wait_recv()

    for load in loads[5:10]:
        load.wait()
    gated = []
    for h in range(heads):
        cols = slice(h * W, (h + 1) * W)
        raw = base[:, cols] + mm(carry[:, cols], state_in[h])
        raw = raw * lax.rsqrt(jnp.mean(raw * raw, axis=-1, keepdims=True) + EPS)
        logits = gate[:, cols].astype(F32)
        gated.append((raw * out_gain[...] / (1.0 + jnp.exp(-logits))).astype(BF16))
    gated = jnp.concatenate(gated, axis=1)

    loads[10].wait()
    width = partial.shape[2]

    def swap(p):
        return pltpu.make_async_remote_copy(
            src_ref=partial.at[p], dst_ref=other.at[p],
            send_sem=send_p.at[p], recv_sem=recv_p.at[p],
            device_id=sibling, device_id_type=MESH,
        )

    for p in range(PIECES):
        partial[p] = mm(gated, ow[:, p * width : (p + 1) * width])
        swap(p).start()
    squares = 0.0
    hidden = []
    for p in range(PIECES):
        cols = slice(p * width, (p + 1) * width)
        swap(p).wait_recv()
        summed = residual[:, cols].astype(F32) + (partial[p] + other[p])
        rounded = summed.astype(BF16)
        hidden_o[:, cols] = rounded
        rounded = rounded.astype(F32)
        squares = squares + jnp.sum(rounded * rounded, axis=-1, keepdims=True)
        hidden.append(rounded)
    scale = lax.rsqrt(squares / (PIECES * width) + EPS)
    gain = jnp.concatenate([hidden_gain[i : i + 1] for i in range(hidden_gain.shape[0])], axis=1)
    normed = jnp.concatenate(hidden, axis=1) * scale * gain
    normed = normed.astype(BF16)
    loads[11].wait()
    raw = mm(normed, lw[...])
    raw = raw * lax.rsqrt(jnp.mean(raw * raw, axis=-1, keepdims=True) + EPS)
    raw = (raw * latent_gain[...]).astype(BF16)

    def remote(place, peer, send, recv):
        return pltpu.make_async_remote_copy(
            src_ref=place, dst_ref=place, send_sem=send, recv_sem=recv,
            device_id=peer, device_id_type=MESH,
        )

    def a_over_z(step):
        return remote(lat_a.at[core, y, x, z], device(y, x, turn(z, step)), sa1.at[step], ra1.at[RING - step])

    def a_from_z(step):
        return remote(lat_a.at[core, y, x, turn(z, step)], sibling, sa1.at[0], ra1.at[step])

    def a_over_x(step):
        return remote(lat_a.at[core, y, x], device(y, turn(x, step), z), sa2.at[step], ra2.at[RING - step])

    def a_from_x(step):
        return remote(lat_a.at[core, y, turn(x, step)], sibling, sa2.at[0], ra2.at[step])

    def a_over_y(to, step):
        return remote(
            lat_a.at[core, y, turn(x, step)], device(to, x, z), sa3.at[to, step], ra3.at[y, step]
        )

    def a_from_y(at, step):
        return remote(lat_a.at[core, at, turn(x, step)], sibling, sa3.at[at, 0], ra3.at[at, step])

    def axes(at):
        return jnp.where(at < RING // 2, x, z), jnp.where(at < RING // 2, z, x)

    def along(at, first, second):
        return device(y, jnp.where(at < RING // 2, first, second), jnp.where(at < RING // 2, second, first))

    def b_over_y(to):
        u, v = axes(y)
        return remote(lat_b.at[core, y, u, v], device(to, x, z), sb1.at[to], rb1.at[y])

    def b_from_y(at):
        u, v = axes(at)
        return remote(lat_b.at[core, at, u, v], sibling, sb1.at[at], rb1.at[at])

    def b_over_v(at, step):
        u, v = axes(at)
        return remote(
            lat_b.at[core, at, u, v], along(at, u, turn(v, step)), sb2.at[at, step], rb2.at[at, RING - step]
        )

    def b_from_v(at, step):
        u, v = axes(at)
        return remote(lat_b.at[core, at, u, turn(v, step)], sibling, sb2.at[at, 0], rb2.at[at, step])

    def b_over_u(at, step):
        u, v = axes(at)
        return remote(
            lat_b.at[core, at, u], along(at, turn(u, step), v), sb3.at[at, step], rb3.at[at, RING - step]
        )

    def b_from_u(at, step):
        u, v = axes(at)
        return remote(lat_b.at[core, at, turn(u, step)], sibling, sb3.at[at, 0], rb3.at[at, step])

    def give_a(at, step):
        return remote(lat_a.at[core, at, turn(x, step)], sibling, swap_a.at[at, step], got_a.at[at, step])

    def take_a(at, step):
        return remote(lat_a.at[1 - core, at, turn(x, step)], sibling, swap_a.at[at, step], got_a.at[at, step])

    def give_b(at, step):
        return remote(lat_b.at[core, at, turn(axes(at)[0], step)], sibling, swap_b.at[at, step], got_b.at[at, step])

    def take_b(at, step):
        return remote(lat_b.at[1 - core, at, turn(axes(at)[0], step)], sibling, swap_b.at[at, step], got_b.at[at, step])

    others = (1, 3, 2)

    partner = device(RING - 1 - y, x, z)

    def mail():
        return pltpu.make_async_remote_copy(
            src_ref=mail_out, dst_ref=mail_in, send_sem=sm.at[0], recv_sem=rm.at[0],
            device_id=partner, device_id_type=MESH,
        )

    def note():
        return pltpu.make_async_remote_copy(
            src_ref=note_out, dst_ref=note_in, send_sem=sm.at[1], recv_sem=rm.at[1],
            device_id=partner, device_id_type=MESH,
        )

    def higher(action):
        for to in range(RING - 1, 0, -1):
            pl.when(jnp.logical_and(to > y, to - y < RING - 1))(functools.partial(action, to))

    def lower(action):
        for at in range(RING - 2, -1, -1):
            pl.when(jnp.logical_and(at < y, y - at < RING - 1))(functools.partial(action, at))

    def place_parts(which):
        first = which * 2 * PART
        lat_a[core, y, x, z] = raw[first : first + PART]
        u, v = axes(y)
        lat_b[core, y, u, v] = raw[first + PART : first + 2 * PART]

    for which in range(2):
        pl.when(core == which)(functools.partial(place_parts, which))
    for step in others:
        a_over_z(step).start()
    higher(lambda to: b_over_y(to).start())
    for step in others:
        b_over_v(y, step).start()

    def clear():
        row_max[...] = jnp.full(row_max.shape, -1e30, F32)
        row_sum[...] = jnp.zeros(row_sum.shape, F32)
        accum[...] = jnp.zeros(accum.shape, F32)

    clear()
    block = GROUP * rows

    def spread_a(step):
        higher(lambda to: a_over_y(to, step).start())
        give_a(y, step).start()

    def spread_b(at):
        for step in others:
            b_from_v(at, step).wait_recv()
        for step in others:
            b_over_u(at, step).start()
        give_b(at, 0).start()

    loads[12].wait()
    mail_out[...] = mm(normed, qw[...]).astype(BF16)
    pl.when(y == RING - 1)(lambda: mail().start())
    for step in others:
        a_from_z(step).wait_recv()
    for step in others:
        a_over_x(step).start()
    spread_a(0)
    spread_b(y)

    def pass_b(at):
        b_from_y(at).wait_recv()
        for step in others:
            b_over_v(at, step).start()

    lower(pass_b)
    loads[13].wait()

    def absorb(queries):
        for h in range(heads):
            cols = slice(h * W, (h + 1) * W)
            qp_ref[h] = (mm_nt(queries[:, cols], ku[:, cols]) * SCORE_SCALE).astype(BF16)

    absorb(mail_out)

    def attend(pieces, mask):
        keys = jnp.concatenate([piece.reshape(line, latent) for piece in pieces], axis=0)
        count = keys.shape[0]
        for b in range(0, heads, GROUP):
            place = slice(b * rows, b * rows + block)
            queries = qp_ref[b : b + GROUP].reshape(block, latent)
            scores = mm_nt(queries, keys)
            if mask is not None:
                query_pos = here * rows + iota((block, count), 0) % rows
                scores = jnp.where(mask((1, count)) <= query_pos, scores, -2e30)
            old = row_max[place, :]
            new = jnp.maximum(old, jnp.max(scores, axis=-1, keepdims=True))
            row_max[place, :] = new
            shrink = jnp.exp2(old - new)
            probs = [jnp.exp2(scores[:, c : c + W] - new) for c in range(0, count, W)]
            added = row_sum[place, :] * shrink
            for p in probs:
                added = added + p
            row_sum[place, :] = added
            mixed = mm(jnp.concatenate([p.astype(BF16) for p in probs], axis=1), keys)
            accum[place, :] = accum[place, :] * jnp.concatenate([shrink] * (latent // W), axis=1) + mixed

    def own_lines(step):
        u = turn(axes(y)[0], step)
        line_x = turn(x, step)
        return lat_a[0, y, line_x], lat_a[1, y, line_x], lat_b[0, y, u], lat_b[1, y, u]

    def own(step):
        u = turn(axes(y)[0], step)
        line_x = turn(x, step)

        def positions(shape):
            column = iota(shape, 1)
            slot, inner, piece = (column // PART) % RING, column % PART, column // line
            part_b = piece // 2
            chip_a = line_x * RING + slot
            chip_b = jnp.where(y < RING // 2, u * RING + slot, slot * RING + u)
            chip = jnp.where(part_b == 1, chip_b, chip_a)
            return (y * RING * RING + chip) * rows + (piece % 2) * (2 * PART) + part_b * PART + inner

        take_a(y, step).wait_recv()
        take_b(y, step).wait_recv()
        attend(own_lines(step), positions)

    def fetch_a(at, step):
        a_from_y(at, step).wait_recv()
        give_a(at, step).start()

    def fetch_b(at, step):
        def far():
            b_from_u(at, step).wait_recv()
            give_b(at, step).start()

        pl.when(step > 0)(far)

    def both(pair, visit):
        for s in range(2):
            visit(jnp.where(pair == 0, s, RING - 1 - s))

    def loop(begin, end, visit):
        lax.fori_loop(begin, end, lambda i, nothing: (visit(i), nothing)[1], 0)

    lower(spread_b)
    own(0)
    for step in others:
        a_from_x(step).wait_recv()
        spread_a(step)
    for step in others:
        fetch_b(y, step)

    def own_round(i):
        own(jnp.where(i == 0, 1, jnp.where(i == 1, 3, 2)))

    loop(0, RING - 1, own_round)

    last_plane = jnp.where(y == RING - 1, 1, 0)
    pl.when(y > 0)(lambda: both(0, lambda step: fetch_a(y - 1, step)))

    def earlier(i):
        at, pair = y - 1 - i // 2, i % 2
        steps = (jnp.where(pair == 0, 0, 3), jnp.where(pair == 0, 1, 2))
        both(pair, lambda step: fetch_b(at, step))
        both(pair, lambda step: take_a(at, step).wait_recv())
        attend([lat_a[c, at, turn(x, step)] for step in steps for c in range(2)], None)
        following = y - 1 - (i + 1) // 2

        @pl.when(following >= last_plane)
        def _():
            both((i + 1) % 2, lambda step: fetch_a(following, step))

        both(pair, lambda step: take_b(at, step).wait_recv())
        u = axes(at)[0]
        attend([lat_b[c, at, turn(u, step)] for step in steps for c in range(2)], None)

    loop(0, 2 * (y - last_plane), earlier)

    loads[14].wait()

    def result(h):
        place = slice(h * rows, (h + 1) * rows)
        row_total = jnp.sum(row_sum[place, :], axis=-1, keepdims=True)
        high, low = halves(accum[place, :] / row_total)
        up = vu_ref[:, h * W : (h + 1) * W]
        return mm(high, up) + mm(low, up), row_max[place, :] + jnp.log2(row_total)

    @pl.when(y < RING - 1)
    def _():
        for h in range(heads):
            out_ref[:, h * W : (h + 1) * W] = result(h)[0].astype(BF16)

    @pl.when(y == 0)
    def _():
        mail().wait_recv()
        absorb(mail_in)
        clear()
        loop(0, RING, lambda step: attend(own_lines(step), None))
        lane = iota((rows, W), 1)
        level = jnp.zeros((rows, W), F32)
        for h in range(heads):
            mixed, log_sum = result(h)
            mail_out[:, h * W : (h + 1) * W] = mixed.astype(BF16)
            level = jnp.where(lane == h, log_sum, level)
        note_out[...] = level
        note().start()
        mail().start()
        note().wait_send()
        mail().wait_send()

    @pl.when(y == RING - 1)
    def _():
        mail().wait_send()
        note().wait_recv()
        mail().wait_recv()
        for h in range(heads):
            cols = slice(h * W, (h + 1) * W)
            mixed, log_sum = result(h)
            gap = log_sum - note_in[:, h : h + 1]
            far = mail_in[:, cols].astype(F32)
            out_ref[:, cols] = (
                mixed / (1.0 + jnp.exp2(-gap)) + far / (1.0 + jnp.exp2(gap))
            ).astype(BF16)

    for step in others:
        a_over_z(step).wait_send()
        a_over_x(step).wait_send()

    def drain_up(to):
        b_over_y(to).wait_send()
        for step in range(RING):
            a_over_y(to, step).wait_send()

    higher(drain_up)

    def drain(at):
        for step in range(1, RING):
            b_over_v(at, step).wait_send()
            b_over_u(at, step).wait_send()
        for step in range(RING):
            give_a(at, step).wait_send()
            give_b(at, step).wait_send()

    loop(last_plane, y + 1, drain)


    for step in range(1, heads):
        map_to(member(step)[0]).wait_send()
        send_state(step).wait_send()
    for step in range(1, groups):
        peer, copy = send_total(step)
        pl.when(peer > mine)(copy.wait_send)
    for p in range(PIECES):
        swap(p).wait_send()


def layer(q, k, v, ld, beta, gate, residual, out_gain, hidden_gain, latent_gain, ow, lw, qw, ku, vu):
    heads = beta.shape[0]
    rows, width = residual.shape
    latent = lw.shape[1]
    groups = lax.axis_size("seq") // heads
    vm = pl.BlockSpec(memory_space=pltpu.VMEM)
    anywhere = pl.BlockSpec(memory_space=pl.ANY)
    dma = pltpu.SemaphoreType.DMA
    operands = (q, k, v, ld, beta, gate, residual, out_gain, hidden_gain, latent_gain, ow, lw, qw, ku, vu)
    message = (W + 16, 2 * W)
    one, two = dma((RING,)), dma((RING, RING))
    return pl.pallas_call(
        layer_kernel,
        out_shape=(
            jax.ShapeDtypeStruct((rows, width), BF16),
            jax.ShapeDtypeStruct((rows, heads * W), BF16),
        ),
        in_specs=[anywhere] * len(operands),
        out_specs=(vm, vm),
        scratch_shapes=[pltpu.VMEM(a.shape, a.dtype) for a in operands] + [
            pltpu.VMEM((heads,) + message, BF16),
            pltpu.VMEM((rows, heads * W), F32),
            pltpu.VMEM((rows, heads * W), BF16),
            pltpu.VMEM((heads,) + message, BF16),
            pltpu.VMEM(message, BF16),
            pltpu.VMEM((groups,) + message, BF16),
            pltpu.VMEM((heads, W, W), BF16),
            pltpu.VMEM((heads, W, W), BF16),
            pltpu.VMEM((PIECES, rows, width // PIECES), F32),
            pltpu.VMEM((PIECES, rows, width // PIECES), F32),
            pltpu.VMEM((heads, rows, latent), BF16),
            pltpu.VMEM((2, RING, RING, RING, PART, latent), BF16),
            pltpu.VMEM((2, RING, RING, RING, PART, latent), BF16),
            pltpu.VMEM((heads * rows, W), F32),
            pltpu.VMEM((heads * rows, W), F32),
            pltpu.VMEM((heads * rows, latent), F32),
            pltpu.VMEM((rows, heads * W), BF16),
            pltpu.VMEM((rows, heads * W), BF16),
            pltpu.VMEM((rows, W), F32),
            pltpu.VMEM((rows, W), F32),
            dma((len(operands),)),
            dma((heads,)), dma((heads,)), dma((groups,)), dma((groups,)),
            dma((heads,)), dma((heads,)), dma((PIECES,)), dma((PIECES,)),
            one, one, one, one, two, two, one, one, two, two, two, two, two, two, two, two,
            dma((2,)), dma((2,)),
        ],
        compiler_params=pltpu.CompilerParams(
            collective_id=0, has_side_effects=True, vmem_limit_bytes=60 * 2**20
        ),
        name="layer",
    )(*operands)


def finish_kernel(hidden_in, attended_in, hidden_out, attended_out):
    hidden_out[...] = hidden_in[...]
    attended_out[...] = attended_in[...]


def finish(hidden, attended):
    vm = pl.BlockSpec(memory_space=pltpu.VMEM)
    return pl.pallas_call(
        finish_kernel,
        out_shape=tuple(jax.ShapeDtypeStruct(a.shape, a.dtype) for a in (hidden, attended)),
        in_specs=[vm] * 2,
        out_specs=(vm, vm),
        name="finish",
    )(hidden, attended)


def body(
    residual, kda_query, kda_key, kda_value, log_decay, beta_logit, out_gate, out_gain, out_weight,
    hidden_gain, query_weight, latent_weight, latent_gain, key_up_weight, value_up_weight,
):
    hidden, attended = layer(
        kda_query, kda_key, kda_value, log_decay, beta_logit.T, out_gate, residual, out_gain[None],
        hidden_gain.reshape(-1, W), latent_gain[None], out_weight, latent_weight, query_weight, key_up_weight,
        value_up_weight,
    )
    return finish(hidden, attended)


def solution(mesh):
    in_specs = (
        P("seq", None),
        P("seq", "head"),
        P("seq", "head"),
        P("seq", "head"),
        P("seq", "head"),
        P("seq", "head"),
        P("seq", "head"),
        P(),
        P("head", None),
        P(),
        P(None, "head"),
        P(),
        P(),
        P(None, "head"),
        P(None, "head"),
    )
    out_specs = (P("seq", None), P("seq", "head"))
    return jax.shard_map(body, mesh=mesh, in_specs=in_specs, out_specs=out_specs, check_vma=False)
```

```python
import functools
import jax
import jax.numpy as jnp
from jax import lax
from jax.sharding import PartitionSpec as P
from jax.experimental import pallas as pl
from jax.experimental.pallas import tpu as pltpu

F32 = jnp.float32
BF16 = jnp.bfloat16
W = 128
EPS = 1e-06


def halves(x):
    high = x.astype(BF16)
    return high, (x - high.astype(F32)).astype(BF16)


def mm(a, b):
    return jnp.dot(a, b, preferred_element_type=F32)


def mm_nt(a, b):
    return lax.dot_general(a, b, (((1,), (1,)), ((), ())), preferred_element_type=F32)


def wide(x):
    high, low = halves(x)
    return jnp.concatenate([high, low], axis=1)


def mm4(a, b):
    n = b.shape[1]
    right = wide(b)
    out = mm(wide(a), jnp.concatenate([right, right], axis=0))
    return out[:, :n] + out[:, n:]


def mm4_nt(a, b):
    n = b.shape[0]
    high, low = halves(b)
    right = jnp.concatenate(
        [jnp.concatenate([high, high], axis=1), jnp.concatenate([low, low], axis=1)], axis=0
    )
    out = mm_nt(wide(a), right)
    return out[:, :n] + out[:, n:]


def iota(shape, axis):
    return lax.broadcasted_iota(jnp.int32, shape, axis)


PIECES = 3
MESH = pl.DeviceIdType.MESH
SCORE_SCALE = W ** (-0.5) * 1.4426950408889634
RING = 4
PART = 32
GROUP = 8
DELTA_GROUP = 8


def pack_diag(closing):
    high, rest = halves(closing)
    r = iota((16, W), 0)
    block = jnp.where(r == 0, high.astype(F32), jnp.where(r == 1, rest.astype(F32), 0.0))
    return jnp.concatenate([block, jnp.zeros((16, W), F32)], axis=1).astype(BF16)


def unpack_map(block):
    diag = block[W : W + 1, :W].astype(F32) + block[W + 1 : W + 2, :W].astype(F32)
    eye = iota((W, W), 0) == iota((W, W), 1)
    matrix = jnp.where(eye, diag, 0.0) - block[:W, :W].astype(F32)
    return jnp.concatenate([matrix, block[:W, W:].astype(F32)], axis=1), diag


def after(later, earlier):
    n = earlier.shape[1]
    out = mm4(later[:, :W], earlier)
    if n == 2 * W:
        return jnp.concatenate([out[:, :W], out[:, W:] + later[:, W:]], axis=1)
    return out + later[:, W:]


def unit(values):
    return values * lax.rsqrt(jnp.sum(values * values, axis=-1, keepdims=True) + EPS)


def triangle(rows):
    ti, si = iota((rows, rows), 0), iota((rows, rows), 1)
    return ti, si, si < ti


def invert(lowers):
    rows = lowers[0].shape[0]
    ti, si, strict = triangle(rows)
    eye = jnp.where(si == ti, 1.0, 0.0)
    level = jnp.logical_and((ti // 2) == (si // 2), strict)
    found = [eye - jnp.where(level, low, 0.0) for low in lowers]
    size = 2
    while size < rows:
        level = jnp.logical_and((ti // (2 * size)) == (si // (2 * size)), (ti // size) > (si // size))
        inner = [mm4(jnp.where(level, low, 0.0), x) for low, x in zip(lowers, found)]
        found = [x - mm4(x, y) for x, y in zip(found, inner)]
        size *= 2
    return found


def delta_maps(k_ref, v_ref, ld_ref, beta_ref, msg_ref, cum_ref, solved_ref, sent):
    rows = k_ref.shape[0]
    heads = k_ref.shape[1] // W
    ti, si, strict = triangle(rows)
    ones = jnp.where(si <= ti, 1.0, 0.0).astype(BF16)
    rates = (1.0 / (1.0 + jnp.exp(-beta_ref[...]))).T

    def prepare(h):
        cols = slice(h * W, (h + 1) * W)
        ld = ld_ref[:, cols]
        high, rest = halves(ld)
        low = (ld - high.astype(F32) - rest.astype(F32)).astype(BF16)
        cum = mm(ones, high) + (mm(ones, rest) + mm(ones, low))
        cum_ref[:, cols] = cum
        mid = cum[rows // 2 - 1 : rows // 2, :]
        end = cum[rows - 1 : rows, :]
        key = unit(k_ref[:, cols].astype(F32))
        mixed = mm4_nt(key * jnp.exp(cum - mid), key * jnp.exp(mid - cum))
        rate = rates[:, h : h + 1]
        lower = jnp.where(strict, mixed, 0.0) * rate
        right = jnp.concatenate(
            [rate * v_ref[:, cols].astype(F32), rate * (key * jnp.exp(cum))], axis=1
        )
        return lower, right, (key * jnp.exp(end - cum)).T, jnp.exp(end)

    for start in range(0, heads, DELTA_GROUP):
        made = [prepare(h) for h in range(start, start + DELTA_GROUP)]
        inverses = invert([m[0] for m in made])
        for h, inverse, (_, right, tail, closing) in zip(
            range(start, start + DELTA_GROUP), inverses, made
        ):
            solved = mm4(inverse, right)
            solved_ref[h] = solved
            state = mm4(tail, solved)
            msg_ref[h, :W, :W] = state[:, W:].astype(BF16)
            msg_ref[h, :W, W:] = state[:, :W].astype(BF16)
            msg_ref[h, W:, :] = pack_diag(closing)
        sent(start, start + DELTA_GROUP)


def delta_outputs(q_ref, k_ref, cum_ref, solved_ref, base_ref, carry_ref):
    rows = k_ref.shape[0]
    ti, si, _ = triangle(rows)
    for h in range(k_ref.shape[1] // W):
        cols = slice(h * W, (h + 1) * W)
        cum = cum_ref[:, cols]
        mid = cum[rows // 2 - 1 : rows // 2, :]
        key = unit(k_ref[:, cols].astype(F32))
        query = unit(q_ref[:, cols].astype(F32))
        mixed = mm4_nt(query * jnp.exp(cum - mid), key * jnp.exp(mid - cum))
        out = mm4(jnp.where(si <= ti, mixed, 0.0), solved_ref[h])
        base_ref[:, cols] = out[:, :W]
        carry_ref[:, cols] = (query * jnp.exp(cum) - out[:, W:]).astype(BF16)


def layer_kernel(
    q_hbm, k_hbm, v_hbm, ld_hbm, beta_hbm, gate_hbm, residual_hbm, out_gain_hbm, hidden_gain_hbm,
    latent_gain_hbm, ow_hbm, lw_hbm, qw_hbm, ku_hbm, vu_hbm,
    hidden_o, out_ref,
    q_in, k_in, v_in, ld_in, beta_in, gate, residual, out_gain, hidden_gain, latent_gain, ow, lw, qw, ku, vu_ref,
    cum, solved, msg, base, carry, got, total, totals, states, state_in, partial, other,
    qp_ref, lat_a, lat_b, row_max, row_sum, accum, far_qp, far_max, far_sum, far_accum, mail_out, mail_in, note_out, note_in,
    load_sem, send_a, recv_a, send_b, recv_b, send_c, recv_c, send_p, recv_p,
    sa1, ra1, sa2, ra2, sa3, ra3, sb1, rb1, sb2, rb2, sb3, rb3, swap_a, got_a, swap_b, got_b, sm, rm,
):
    heads = msg.shape[0]
    groups = totals.shape[0]
    rows, latent = residual.shape[0], lw.shape[1]
    here, core = lax.axis_index("seq"), lax.axis_index("head")
    mine, rank = here // heads, here % heads
    y, x, z = here // (RING * RING), (here // RING) % RING, here % RING
    line = RING * PART
    sibling = (here, 1 - core)

    def device(to_y, to_x, to_z):
        return (to_y * RING * RING + to_x * RING + to_z, core)

    def turn(coordinate, step):
        return (coordinate + step) % RING

    def member(step):
        peer = (rank + step) % heads
        return peer, (mine * heads + peer, core)

    def cousin(step):
        peer = (mine + step) % groups
        return peer, (peer * heads + rank, core)

    barrier = pltpu.get_barrier_semaphore()
    for step in range(1, heads):
        pl.semaphore_signal(barrier, inc=1, device_id=member(step)[1], device_id_type=MESH)
    for step in range(1, groups):
        pl.semaphore_signal(barrier, inc=1, device_id=cousin(step)[1], device_id_type=MESH)
    pl.semaphore_signal(barrier, inc=1, device_id=sibling, device_id_type=MESH)
    pl.semaphore_signal(barrier, inc=1, device_id=device(y, RING - 1 - x, z), device_id_type=MESH)

    pairs = (
        (k_hbm, k_in), (ld_hbm, ld_in), (v_hbm, v_in), (beta_hbm, beta_in), (q_hbm, q_in), (gate_hbm, gate),
        (residual_hbm, residual), (out_gain_hbm, out_gain), (hidden_gain_hbm, hidden_gain),
        (latent_gain_hbm, latent_gain), (ow_hbm, ow), (lw_hbm, lw), (qw_hbm, qw), (ku_hbm, ku), (vu_hbm, vu_ref),
    )
    loads = [pltpu.make_async_copy(src, dst, load_sem.at[i]) for i, (src, dst) in enumerate(pairs)]
    for load in loads[:4]:
        load.start()
    for load in loads[:4]:
        load.wait()
    for load in loads[4:]:
        load.start()

    def map_to(peer):
        return pltpu.make_async_remote_copy(
            src_ref=msg.at[peer], dst_ref=got.at[rank],
            send_sem=send_a.at[peer], recv_sem=recv_a.at[rank],
            device_id=(mine * heads + peer, core), device_id_type=MESH,
        )

    def map_from(peer):
        return pltpu.make_async_remote_copy(
            src_ref=msg.at[peer], dst_ref=got.at[peer],
            send_sem=send_a.at[peer], recv_sem=recv_a.at[peer],
            device_id=(mine * heads + peer, core), device_id_type=MESH,
        )

    def sent(begin, end):
        if begin == 0:
            pl.semaphore_wait(barrier, heads + groups)
        for peer in range(begin, end):
            pl.when(peer != rank)(map_to(peer).start)

    delta_maps(k_in, v_in, ld_in, beta_in, msg, cum, solved, sent)
    got[rank] = msg[rank]
    loads[4].wait()
    delta_outputs(q_in, k_in, cum, solved, base, carry)
    for step in range(1, heads):
        map_from(member(step)[0]).wait_recv()

    maps, diags = [], []
    for i in range(heads):
        matrix, diag = unpack_map(got[i])
        maps.append(matrix)
        diags.append(diag)
    pairs = [after(maps[i + 1], maps[i]) for i in range(0, heads, 2)]
    quads = [after(pairs[i + 1], pairs[i]) for i in range(0, len(pairs), 2)]
    whole = after(quads[1], quads[0])
    diag = diags[0]
    for other_diag in diags[1:]:
        diag = diag * other_diag
    eye = iota((W, W), 0) == iota((W, W), 1)
    total[:W, :W] = (jnp.where(eye, diag, 0.0) - whole[:, :W]).astype(BF16)
    total[:W, W:] = whole[:, W:].astype(BF16)
    total[W:, :] = pack_diag(diag)

    def send_total(step):
        peer, device = cousin(step)
        return peer, pltpu.make_async_remote_copy(
            src_ref=total, dst_ref=totals.at[mine],
            send_sem=send_b.at[peer], recv_sem=recv_b.at[mine],
            device_id=device, device_id_type=MESH,
        )

    def take_total(step):
        peer, device = cousin(step)
        return peer, pltpu.make_async_remote_copy(
            src_ref=total, dst_ref=totals.at[peer],
            send_sem=send_b.at[peer], recv_sem=recv_b.at[peer],
            device_id=device, device_id_type=MESH,
        )

    for step in range(1, groups):
        peer, copy = send_total(step)
        pl.when(peer > mine)(copy.start)

    before = [None] * heads
    before[1] = maps[0]
    before[2] = pairs[0]
    before[4] = quads[0]
    before[3] = after(maps[2], pairs[0])
    before[5] = after(maps[4], quads[0])
    before[6] = after(pairs[2], quads[0])
    before[7] = after(maps[6], before[6])

    for step in range(1, groups):
        peer, copy = take_total(step)
        pl.when(peer < mine)(copy.wait_recv)

    eye_zero = jnp.concatenate([jnp.where(eye, 1.0, 0.0), jnp.zeros((W, W), F32)], axis=1)
    chain = [jnp.where(j < mine, unpack_map(totals[j])[0], eye_zero) for j in range(groups - 1)]
    while len(chain) > 1:
        joined = []
        for i in range(0, len(chain) - 1, 2):
            first = chain[i] if i else chain[i][:, W:]
            joined.append(after(chain[i + 1], first))
        if len(chain) % 2:
            joined.append(chain[-1])
        if joined[0].shape[1] == W:
            joined[0] = jnp.concatenate([jnp.zeros((W, W), F32), joined[0]], axis=1)
        chain = joined
    start = chain[0][:, W:]

    states[0] = start.astype(BF16)
    stacked = mm4(jnp.concatenate([b[:, :W] for b in before[1:]], axis=0), start)
    for i in range(1, heads):
        states[i] = (stacked[(i - 1) * W : i * W] + before[i][:, W:]).astype(BF16)

    def send_state(step):
        peer, device = member(step)
        return pltpu.make_async_remote_copy(
            src_ref=states.at[peer], dst_ref=state_in.at[rank],
            send_sem=send_c.at[peer], recv_sem=recv_c.at[rank],
            device_id=device, device_id_type=MESH,
        )

    def take_state(step):
        peer, device = member(step)
        return pltpu.make_async_remote_copy(
            src_ref=states.at[peer], dst_ref=state_in.at[peer],
            send_sem=send_c.at[peer], recv_sem=recv_c.at[peer],
            device_id=device, device_id_type=MESH,
        )

    for step in range(1, heads):
        send_state(step).start()
    state_in[rank] = states[rank]
    for step in range(1, heads):
        take_state(step).wait_recv()

    for load in loads[5:10]:
        load.wait()
    gated = []
    for h in range(heads):
        cols = slice(h * W, (h + 1) * W)
        raw = base[:, cols] + mm(carry[:, cols], state_in[h])
        raw = raw * lax.rsqrt(jnp.mean(raw * raw, axis=-1, keepdims=True) + EPS)
        logits = gate[:, cols].astype(F32)
        gated.append((raw * out_gain[...] / (1.0 + jnp.exp(-logits))).astype(BF16))
    gated = jnp.concatenate(gated, axis=1)

    loads[10].wait()
    width = partial.shape[2]

    def swap(p):
        return pltpu.make_async_remote_copy(
            src_ref=partial.at[p], dst_ref=other.at[p],
            send_sem=send_p.at[p], recv_sem=recv_p.at[p],
            device_id=sibling, device_id_type=MESH,
        )

    for p in range(PIECES):
        partial[p] = mm(gated, ow[:, p * width : (p + 1) * width])
        swap(p).start()
    squares = 0.0
    hidden = []
    for p in range(PIECES):
        cols = slice(p * width, (p + 1) * width)
        swap(p).wait_recv()
        summed = residual[:, cols].astype(F32) + (partial[p] + other[p])
        rounded = summed.astype(BF16)
        hidden_o[:, cols] = rounded
        rounded = rounded.astype(F32)
        squares = squares + jnp.sum(rounded * rounded, axis=-1, keepdims=True)
        hidden.append(rounded)
    scale = lax.rsqrt(squares / (PIECES * width) + EPS)
    gain = jnp.concatenate([hidden_gain[i : i + 1] for i in range(hidden_gain.shape[0])], axis=1)
    normed = jnp.concatenate(hidden, axis=1) * scale * gain
    normed = normed.astype(BF16)
    loads[11].wait()
    raw = mm(normed, lw[...])
    raw = raw * lax.rsqrt(jnp.mean(raw * raw, axis=-1, keepdims=True) + EPS)
    raw = (raw * latent_gain[...]).astype(BF16)

    def remote(place, peer, send, recv):
        return pltpu.make_async_remote_copy(
            src_ref=place, dst_ref=place, send_sem=send, recv_sem=recv,
            device_id=peer, device_id_type=MESH,
        )

    def a_over_z(step):
        return remote(lat_a.at[core, y, x, z], device(y, x, turn(z, step)), sa1.at[step], ra1.at[RING - step])

    def a_from_z(step):
        return remote(lat_a.at[core, y, x, turn(z, step)], sibling, sa1.at[0], ra1.at[step])

    def a_over_x(step):
        return remote(lat_a.at[core, y, x], device(y, turn(x, step), z), sa2.at[step], ra2.at[RING - step])

    def a_from_x(step):
        return remote(lat_a.at[core, y, turn(x, step)], sibling, sa2.at[0], ra2.at[step])

    def a_over_y(to, step):
        return remote(
            lat_a.at[core, y, turn(x, step)], device(to, x, z), sa3.at[to, step], ra3.at[y, step]
        )

    def a_from_y(at, step):
        return remote(lat_a.at[core, at, turn(x, step)], sibling, sa3.at[at, 0], ra3.at[at, step])

    def axes(at):
        turned = at + RING // 2 == y
        return jnp.where(turned, x, z), jnp.where(turned, z, x)

    def along(at, first, second):
        turned = at + RING // 2 == y
        return device(y, jnp.where(turned, first, second), jnp.where(turned, second, first))

    def b_over_y(to):
        turned = y + RING // 2 == to
        return pltpu.make_async_remote_copy(
            src_ref=lat_b.at[core, y, z, x],
            dst_ref=lat_b.at[core, y, jnp.where(turned, x, z), jnp.where(turned, z, x)],
            send_sem=sb1.at[to], recv_sem=rb1.at[y], device_id=device(to, x, z), device_id_type=MESH,
        )

    def b_from_y(at):
        u, v = axes(at)
        return remote(lat_b.at[core, at, u, v], sibling, sb1.at[at], rb1.at[at])

    def b_over_v(at, step):
        u, v = axes(at)
        return remote(
            lat_b.at[core, at, u, v], along(at, u, turn(v, step)), sb2.at[at, step], rb2.at[at, RING - step]
        )

    def b_from_v(at, step):
        u, v = axes(at)
        return remote(lat_b.at[core, at, u, turn(v, step)], sibling, sb2.at[at, 0], rb2.at[at, step])

    def b_over_u(at, step):
        u, v = axes(at)
        return remote(
            lat_b.at[core, at, u], along(at, turn(u, step), v), sb3.at[at, step], rb3.at[at, RING - step]
        )

    def b_from_u(at, step):
        u, v = axes(at)
        return remote(lat_b.at[core, at, turn(u, step)], sibling, sb3.at[at, 0], rb3.at[at, step])

    def give_a(at, step):
        return remote(lat_a.at[core, at, turn(x, step)], sibling, swap_a.at[at, step], got_a.at[at, step])

    def take_a(at, step):
        return remote(lat_a.at[1 - core, at, turn(x, step)], sibling, swap_a.at[at, step], got_a.at[at, step])

    def give_b(at, step):
        return remote(lat_b.at[core, at, turn(axes(at)[0], step)], sibling, swap_b.at[at, step], got_b.at[at, step])

    def take_b(at, step):
        return remote(lat_b.at[1 - core, at, turn(axes(at)[0], step)], sibling, swap_b.at[at, step], got_b.at[at, step])

    others = (1, 3, 2)

    partner = device(RING - 1 - y, x, z)

    def mail():
        return pltpu.make_async_remote_copy(
            src_ref=mail_out, dst_ref=mail_in, send_sem=sm.at[0], recv_sem=rm.at[0],
            device_id=partner, device_id_type=MESH,
        )

    def note():
        return pltpu.make_async_remote_copy(
            src_ref=note_out, dst_ref=note_in, send_sem=sm.at[1], recv_sem=rm.at[1],
            device_id=partner, device_id_type=MESH,
        )

    def higher(action):
        for to in range(RING - 1, 0, -1):
            pl.when(jnp.logical_and(to > y, to + y != RING - 1))(functools.partial(action, to))

    def lower(action):
        for at in range(RING - 2, -1, -1):
            pl.when(jnp.logical_and(at < y, at + y != RING - 1))(functools.partial(action, at))

    def place_parts(which):
        first = which * 2 * PART
        lat_a[core, y, x, z] = raw[first : first + PART]
        u, v = axes(y)
        lat_b[core, y, u, v] = raw[first + PART : first + 2 * PART]

    for which in range(2):
        pl.when(core == which)(functools.partial(place_parts, which))
    for step in others:
        a_over_z(step).start()
    higher(lambda to: b_over_y(to).start())
    for step in others:
        b_over_v(y, step).start()

    def clear(store):
        store[1][...] = jnp.full(store[1].shape, -1e30, F32)
        store[2][...] = jnp.zeros(store[2].shape, F32)
        store[3][...] = jnp.zeros(store[3].shape, F32)

    clear((qp_ref, row_max, row_sum, accum))
    block = GROUP * rows

    def spread_a(step):
        higher(lambda to: a_over_y(to, step).start())
        give_a(y, step).start()

    def spread_b(at):
        for step in others:
            b_from_v(at, step).wait_recv()
        for step in others:
            b_over_u(at, step).start()
        give_b(at, 0).start()

    loads[12].wait()
    mail_out[...] = mm(normed, qw[...]).astype(BF16)
    pl.when(y >= RING // 2)(lambda: mail().start())
    for step in others:
        a_from_z(step).wait_recv()
    for step in others:
        a_over_x(step).start()
    spread_a(0)
    spread_b(y)

    def pass_b(at):
        b_from_y(at).wait_recv()
        for step in others:
            b_over_v(at, step).start()

    lower(pass_b)
    loads[13].wait()

    mine_store = (qp_ref, row_max, row_sum, accum)
    far_store = (far_qp, far_max, far_sum, far_accum)

    def absorb(queries, store):
        for h in range(heads):
            cols = slice(h * W, (h + 1) * W)
            store[0][h] = (mm_nt(queries[:, cols], ku[:, cols]) * SCORE_SCALE).astype(BF16)

    absorb(mail_out, mine_store)

    def attend(pieces, mask, store):
        query, top, total_sum, mixed_sum = store
        keys = jnp.concatenate([piece.reshape(line, latent) for piece in pieces], axis=0)
        count = keys.shape[0]
        for b in range(0, heads, GROUP):
            place = slice(b * rows, b * rows + block)
            queries = query[b : b + GROUP].reshape(block, latent)
            scores = mm_nt(queries, keys)
            if mask is not None:
                query_pos = here * rows + iota((block, count), 0) % rows
                scores = jnp.where(mask((1, count)) <= query_pos, scores, -2e30)
            old = top[place, :]
            new = jnp.maximum(old, jnp.max(scores, axis=-1, keepdims=True))
            top[place, :] = new
            shrink = jnp.exp2(old - new)
            probs = [jnp.exp2(scores[:, c : c + W] - new) for c in range(0, count, W)]
            added = total_sum[place, :] * shrink
            for p in probs:
                added = added + p
            total_sum[place, :] = added
            mixed = mm(jnp.concatenate([p.astype(BF16) for p in probs], axis=1), keys)
            mixed_sum[place, :] = mixed_sum[place, :] * jnp.concatenate([shrink] * (latent // W), axis=1) + mixed

    def own_lines(step):
        u = turn(z, step)
        line_x = turn(x, step)
        return lat_a[0, y, line_x], lat_a[1, y, line_x], lat_b[0, y, u], lat_b[1, y, u]

    def own(step):
        u = turn(z, step)
        line_x = turn(x, step)

        def positions(shape):
            column = iota(shape, 1)
            slot, inner, piece = (column // PART) % RING, column % PART, column // line
            part_b = piece // 2
            chip_a = line_x * RING + slot
            chip_b = slot * RING + u
            chip = jnp.where(part_b == 1, chip_b, chip_a)
            return (y * RING * RING + chip) * rows + (piece % 2) * (2 * PART) + part_b * PART + inner

        take_a(y, step).wait_recv()
        take_b(y, step).wait_recv()
        attend(own_lines(step), positions, mine_store)

    def fetch_a(at, step):
        a_from_y(at, step).wait_recv()
        give_a(at, step).start()

    def fetch_b(at, step):
        def far():
            b_from_u(at, step).wait_recv()
            give_b(at, step).start()

        pl.when(step > 0)(far)

    def both(pair, visit):
        for s in range(2):
            visit(jnp.where(pair == 0, s, RING - 1 - s))

    def loop(begin, end, visit):
        lax.fori_loop(begin, end, lambda i, nothing: (visit(i), nothing)[1], 0)

    below = jnp.where(y == RING - 1, 2, jnp.where(y == 0, 0, 1))

    def plane(i):
        return jnp.where(y == RING - 1, RING - 2 - i // 2, 0)

    def fetch(at, pair):
        both(pair, lambda step: fetch_a(at, step))
        both(pair, lambda step: fetch_b(at, step))

    def pass_a(step):
        a_from_x(step).wait_recv()
        spread_a(step)
        fetch_b(y, step)

    own(0)
    lower(spread_b)
    pass_a(1)
    pass_a(3)

    @pl.when(y < RING // 2)
    def _():
        clear(far_store)
        mail().wait_recv()
        absorb(mail_in, far_store)

    def own_round(i):
        pl.when(i == 1)(lambda: pass_a(2))
        pl.when(jnp.logical_and(i == 2, y > 0))(lambda: fetch(plane(0), 0))
        own(jnp.where(i == 0, 1, jnp.where(i == 1, 3, 2)))

        @pl.when(jnp.logical_and(y < RING // 2, i != 1))
        def _():
            first, second = jnp.where(i == 0, 0, 3), jnp.where(i == 0, 1, 2)
            attend(own_lines(first) + own_lines(second), None, far_store)

    loop(0, RING - 1, own_round)

    loads[14].wait()

    def result(h, store):
        place = slice(h * rows, (h + 1) * rows)
        row_total = jnp.sum(store[2][place, :], axis=-1, keepdims=True)
        high, low = halves(store[3][place, :] / row_total)
        up = vu_ref[:, h * W : (h + 1) * W]
        return mm(high, up) + mm(low, up), store[1][place, :] + jnp.log2(row_total)

    @pl.when(y < RING // 2)
    def _():
        lane = iota((rows, W), 1)
        level = jnp.zeros((rows, W), F32)
        for h in range(heads):
            mixed, log_sum = result(h, far_store)
            mail_out[:, h * W : (h + 1) * W] = mixed.astype(BF16)
            level = jnp.where(lane == h, log_sum, level)
        note_out[...] = level
        note().start()
        mail().start()

    def earlier(i):
        at, pair = plane(i), i % 2
        steps = (jnp.where(pair == 0, 0, 3), jnp.where(pair == 0, 1, 2))
        pl.when(i + 1 < 2 * below)(lambda: fetch(plane(i + 1), (i + 1) % 2))
        both(pair, lambda step: take_a(at, step).wait_recv())
        both(pair, lambda step: take_b(at, step).wait_recv())
        u = axes(at)[0]
        attend(
            [lat_a[c, at, turn(x, step)] for step in steps for c in range(2)]
            + [lat_b[c, at, turn(u, step)] for step in steps for c in range(2)],
            None, mine_store,
        )

    loop(0, 2 * below, earlier)

    @pl.when(y < RING // 2)
    def _():
        for h in range(heads):
            out_ref[:, h * W : (h + 1) * W] = result(h, mine_store)[0].astype(BF16)
        note().wait_send()
        mail().wait_send()

    @pl.when(y >= RING // 2)
    def _():
        mail().wait_send()
        note().wait_recv()
        mail().wait_recv()
        for h in range(heads):
            cols = slice(h * W, (h + 1) * W)
            mixed, log_sum = result(h, mine_store)
            gap = log_sum - note_in[:, h : h + 1]
            far = mail_in[:, cols].astype(F32)
            out_ref[:, cols] = (
                mixed / (1.0 + jnp.exp2(-gap)) + far / (1.0 + jnp.exp2(gap))
            ).astype(BF16)

    for step in others:
        a_over_z(step).wait_send()
        a_over_x(step).wait_send()

    def drain_up(to):
        b_over_y(to).wait_send()
        for step in range(RING):
            a_over_y(to, step).wait_send()

    higher(drain_up)

    def drain(at):
        for step in range(1, RING):
            b_over_v(at, step).wait_send()
            b_over_u(at, step).wait_send()
        for step in range(RING):
            give_a(at, step).wait_send()
            give_b(at, step).wait_send()

    loop(0, below, lambda i: drain(plane(2 * i)))
    drain(y)


    for step in range(1, heads):
        map_to(member(step)[0]).wait_send()
        send_state(step).wait_send()
    for step in range(1, groups):
        peer, copy = send_total(step)
        pl.when(peer > mine)(copy.wait_send)
    for p in range(PIECES):
        swap(p).wait_send()


def layer(q, k, v, ld, beta, gate, residual, out_gain, hidden_gain, latent_gain, ow, lw, qw, ku, vu):
    heads = beta.shape[0]
    rows, width = residual.shape
    latent = lw.shape[1]
    groups = lax.axis_size("seq") // heads
    vm = pl.BlockSpec(memory_space=pltpu.VMEM)
    anywhere = pl.BlockSpec(memory_space=pl.ANY)
    dma = pltpu.SemaphoreType.DMA
    operands = (q, k, v, ld, beta, gate, residual, out_gain, hidden_gain, latent_gain, ow, lw, qw, ku, vu)
    message = (W + 16, 2 * W)
    one, two = dma((RING,)), dma((RING, RING))
    return pl.pallas_call(
        layer_kernel,
        out_shape=(
            jax.ShapeDtypeStruct((rows, width), BF16),
            jax.ShapeDtypeStruct((rows, heads * W), BF16),
        ),
        in_specs=[anywhere] * len(operands),
        out_specs=(vm, vm),
        scratch_shapes=[pltpu.VMEM(a.shape, a.dtype) for a in operands] + [
            pltpu.VMEM((rows, heads * W), F32),
            pltpu.VMEM((heads, rows, 2 * W), F32),
            pltpu.VMEM((heads,) + message, BF16),
            pltpu.VMEM((rows, heads * W), F32),
            pltpu.VMEM((rows, heads * W), BF16),
            pltpu.VMEM((heads,) + message, BF16),
            pltpu.VMEM(message, BF16),
            pltpu.VMEM((groups,) + message, BF16),
            pltpu.VMEM((heads, W, W), BF16),
            pltpu.VMEM((heads, W, W), BF16),
            pltpu.VMEM((PIECES, rows, width // PIECES), F32),
            pltpu.VMEM((PIECES, rows, width // PIECES), F32),
            pltpu.VMEM((heads, rows, latent), BF16),
            pltpu.VMEM((2, RING, RING, RING, PART, latent), BF16),
            pltpu.VMEM((2, RING, RING, RING, PART, latent), BF16),
            pltpu.VMEM((heads * rows, W), F32),
            pltpu.VMEM((heads * rows, W), F32),
            pltpu.VMEM((heads * rows, latent), F32),
            pltpu.VMEM((heads, rows, latent), BF16),
            pltpu.VMEM((heads * rows, W), F32),
            pltpu.VMEM((heads * rows, W), F32),
            pltpu.VMEM((heads * rows, latent), F32),
            pltpu.VMEM((rows, heads * W), BF16),
            pltpu.VMEM((rows, heads * W), BF16),
            pltpu.VMEM((rows, W), F32),
            pltpu.VMEM((rows, W), F32),
            dma((len(operands),)),
            dma((heads,)), dma((heads,)), dma((groups,)), dma((groups,)),
            dma((heads,)), dma((heads,)), dma((PIECES,)), dma((PIECES,)),
            one, one, one, one, two, two, one, one, two, two, two, two, two, two, two, two,
            dma((2,)), dma((2,)),
        ],
        compiler_params=pltpu.CompilerParams(
            collective_id=0, has_side_effects=True, vmem_limit_bytes=60 * 2**20
        ),
        name="layer",
    )(*operands)


def finish_kernel(hidden_in, attended_in, hidden_out, attended_out):
    hidden_out[...] = hidden_in[...]
    attended_out[...] = attended_in[...]


def finish(hidden, attended):
    vm = pl.BlockSpec(memory_space=pltpu.VMEM)
    return pl.pallas_call(
        finish_kernel,
        out_shape=tuple(jax.ShapeDtypeStruct(a.shape, a.dtype) for a in (hidden, attended)),
        in_specs=[vm] * 2,
        out_specs=(vm, vm),
        name="finish",
    )(hidden, attended)


def body(
    residual, kda_query, kda_key, kda_value, log_decay, beta_logit, out_gate, out_gain, out_weight,
    hidden_gain, query_weight, latent_weight, latent_gain, key_up_weight, value_up_weight,
):
    hidden, attended = layer(
        kda_query, kda_key, kda_value, log_decay, beta_logit.T, out_gate, residual, out_gain[None],
        hidden_gain.reshape(-1, W), latent_gain[None], out_weight, latent_weight, query_weight, key_up_weight,
        value_up_weight,
    )
    return finish(hidden, attended)


def solution(mesh):
    in_specs = (
        P("seq", None),
        P("seq", "head"),
        P("seq", "head"),
        P("seq", "head"),
        P("seq", "head"),
        P("seq", "head"),
        P("seq", "head"),
        P(),
        P("head", None),
        P(),
        P(None, "head"),
        P(),
        P(),
        P(None, "head"),
        P(None, "head"),
    )
    out_specs = (P("seq", None), P("seq", "head"))
    return jax.shard_map(body, mesh=mesh, in_specs=in_specs, out_specs=out_specs, check_vma=False)
```

```python
import functools
import jax
import jax.numpy as jnp
from jax import lax
from jax.sharding import PartitionSpec as P
from jax.experimental import pallas as pl
from jax.experimental.pallas import tpu as pltpu

F32 = jnp.float32
BF16 = jnp.bfloat16
W = 128
EPS = 1e-06


def halves(x):
    high = x.astype(BF16)
    return high, (x - high.astype(F32)).astype(BF16)


def mm(a, b):
    return jnp.dot(a, b, preferred_element_type=F32)


def mm_nt(a, b):
    return lax.dot_general(a, b, (((1,), (1,)), ((), ())), preferred_element_type=F32)


def wide(x):
    high, low = halves(x)
    return jnp.concatenate([high, low], axis=1)


def mm4(a, b):
    n = b.shape[1]
    right = wide(b)
    out = mm(wide(a), jnp.concatenate([right, right], axis=0))
    return out[:, :n] + out[:, n:]


def mm4_nt(a, b):
    n = b.shape[0]
    high, low = halves(b)
    right = jnp.concatenate(
        [jnp.concatenate([high, high], axis=1), jnp.concatenate([low, low], axis=1)], axis=0
    )
    out = mm_nt(wide(a), right)
    return out[:, :n] + out[:, n:]


def iota(shape, axis):
    return lax.broadcasted_iota(jnp.int32, shape, axis)


PIECES = 2
MESH = pl.DeviceIdType.MESH
SCORE_SCALE = W ** (-0.5) * 1.4426950408889634
RING = 4
PART = 32
GROUP = 8
DELTA_GROUP = 8
SEND_GROUP = 4


def pack_diag(closing):
    high, rest = halves(closing)
    r = iota((16, W), 0)
    block = jnp.where(r == 0, high.astype(F32), jnp.where(r == 1, rest.astype(F32), 0.0))
    return jnp.concatenate([block, jnp.zeros((16, W), F32)], axis=1).astype(BF16)


def unpack_map(block):
    diag = block[W : W + 1, :W].astype(F32) + block[W + 1 : W + 2, :W].astype(F32)
    eye = iota((W, W), 0) == iota((W, W), 1)
    matrix = jnp.where(eye, diag, 0.0) - block[:W, :W].astype(F32)
    return jnp.concatenate([matrix, block[:W, W:].astype(F32)], axis=1), diag


def after(later, earlier):
    n = earlier.shape[1]
    out = mm4(later[:, :W], earlier)
    if n == 2 * W:
        return jnp.concatenate([out[:, :W], out[:, W:] + later[:, W:]], axis=1)
    return out + later[:, W:]


def unit(values):
    return values * lax.rsqrt(jnp.sum(values * values, axis=-1, keepdims=True) + EPS)


def triangle(rows):
    ti, si = iota((rows, rows), 0), iota((rows, rows), 1)
    return ti, si, si < ti


def second_rows(x, size):
    return jnp.concatenate(
        [x[i + size : i + 2 * size] for i in range(0, x.shape[0], 2 * size)], axis=0
    )


def invert(lowers):
    rows = lowers[0].shape[0]
    ti, si, strict = triangle(rows)
    eye = jnp.where(si == ti, 1.0, 0.0)
    level = jnp.logical_and((ti // 2) == (si // 2), strict)
    found = [eye - jnp.where(level, low, 0.0) for low in lowers]
    size = 2
    while size < rows:
        level = jnp.logical_and((ti // (2 * size)) == (si // (2 * size)), (ti // size) > (si // size))
        inside = [jnp.where(level, low, 0.0) for low in lowers]
        if size < 8:
            inner = [mm4(low, x) for low, x in zip(inside, found)]
            found = [x - mm4(x, y) for x, y in zip(found, inner)]
        else:
            zero = jnp.zeros((size, rows), F32)
            inner = [mm4(second_rows(low, size), x) for low, x in zip(inside, found)]
            inner = [
                jnp.concatenate(
                    [part for i in range(0, rows // 2, size) for part in (zero, y[i : i + size])], axis=0
                )
                for y in inner
            ]
            change = [mm4(second_rows(x, size), y) for x, y in zip(found, inner)]
            found = [
                jnp.concatenate(
                    [
                        part
                        for i in range(0, rows // 2, size)
                        for part in (
                            x[2 * i : 2 * i + size],
                            x[2 * i + size : 2 * i + 2 * size] - y[i : i + size],
                        )
                    ],
                    axis=0,
                )
                for x, y in zip(found, change)
            ]
        size *= 2
    return found


def delta_maps(k_ref, v_ref, ld_ref, beta_ref, msg_ref, cum_ref, solved_ref, sent):
    rows = k_ref.shape[0]
    heads = k_ref.shape[1] // W
    ti, si, strict = triangle(rows)
    ones = jnp.where(si <= ti, 1.0, 0.0).astype(BF16)
    rates = (1.0 / (1.0 + jnp.exp(-beta_ref[...]))).T
    ld = ld_ref[...]
    high, rest = halves(ld)
    low = (ld - high.astype(F32) - rest.astype(F32)).astype(BF16)
    twice = jnp.concatenate([ones, ones], axis=1)
    cum_ref[...] = mm(twice, jnp.concatenate([high, rest], axis=0)) + mm(ones, low)

    def prepare(h):
        cols = slice(h * W, (h + 1) * W)
        cum = cum_ref[:, cols]
        mid = cum[rows // 2 - 1 : rows // 2, :]
        end = cum[rows - 1 : rows, :]
        key = unit(k_ref[:, cols].astype(F32))
        mixed = mm4_nt(key * jnp.exp(cum - mid), key * jnp.exp(mid - cum))
        rate = rates[:, h : h + 1]
        lower = jnp.where(strict, mixed, 0.0) * rate
        right = jnp.concatenate(
            [rate * v_ref[:, cols].astype(F32), rate * (key * jnp.exp(cum))], axis=1
        )
        return lower, right, (key * jnp.exp(end - cum)).T, jnp.exp(end)

    for start in range(0, heads, DELTA_GROUP):
        made = [prepare(h) for h in range(start, start + DELTA_GROUP)]
        inverses = invert([m[0] for m in made])
        for h, inverse, (_, right, tail, closing) in zip(
            range(start, start + DELTA_GROUP), inverses, made
        ):
            solved = mm4(inverse, right)
            solved_ref[h] = solved
            state = mm4(tail, solved)
            msg_ref[h, :W, :W] = state[:, W:].astype(BF16)
            msg_ref[h, :W, W:] = state[:, :W].astype(BF16)
            msg_ref[h, W:, :] = pack_diag(closing)
            if (h + 1) % SEND_GROUP == 0:
                sent(h + 1 - SEND_GROUP, h + 1)


def delta_outputs(q_ref, k_ref, cum_ref, solved_ref, base_ref, carry_ref):
    rows = k_ref.shape[0]
    ti, si, _ = triangle(rows)
    for h in range(k_ref.shape[1] // W):
        cols = slice(h * W, (h + 1) * W)
        cum = cum_ref[:, cols]
        mid = cum[rows // 2 - 1 : rows // 2, :]
        key = unit(k_ref[:, cols].astype(F32))
        query = unit(q_ref[:, cols].astype(F32))
        mixed = mm4_nt(query * jnp.exp(cum - mid), key * jnp.exp(mid - cum))
        out = mm4(jnp.where(si <= ti, mixed, 0.0), solved_ref[h])
        base_ref[:, cols] = out[:, :W]
        carry_ref[:, cols] = (query * jnp.exp(cum) - out[:, W:]).astype(BF16)


def layer_kernel(
    q_hbm, k_hbm, v_hbm, ld_hbm, beta_hbm, gate_hbm, residual_hbm, out_gain_hbm, hidden_gain_hbm,
    latent_gain_hbm, ow_hbm, lw_hbm, qw_hbm, ku_hbm, vu_hbm,
    hidden_o, out_ref,
    q_in, k_in, v_in, ld_in, beta_in, gate, residual, out_gain, hidden_gain, latent_gain, ow, lw, qw, ku, vu_ref,
    cum, solved, msg, base, carry, got, total, totals, states, state_in, partial, other,
    qp_ref, lat_a, lat_b, row_max, row_sum, accum, far_qp, far_max, far_sum, far_accum, mail_out, mail_in, note_out, note_in,
    load_sem, send_a, recv_a, send_b, recv_b, send_c, recv_c, send_p, recv_p,
    sa1, ra1, sa2, ra2, sa3, ra3, sb1, rb1, sb2, rb2, sb3, rb3, swap_a, got_a, swap_b, got_b, sm, rm,
):
    heads = msg.shape[0]
    groups = totals.shape[0]
    rows, latent = residual.shape[0], lw.shape[1]
    here, core = lax.axis_index("seq"), lax.axis_index("head")
    mine, rank = here // heads, here % heads
    y, x, z = here // (RING * RING), (here // RING) % RING, here % RING
    line = RING * PART
    sibling = (here, 1 - core)

    def device(to_y, to_x, to_z):
        return (to_y * RING * RING + to_x * RING + to_z, core)

    def turn(coordinate, step):
        return (coordinate + step) % RING

    def member(step):
        peer = (rank + step) % heads
        return peer, (mine * heads + peer, core)

    def cousin(step):
        peer = (mine + step) % groups
        return peer, (peer * heads + rank, core)

    barrier = pltpu.get_barrier_semaphore()
    for step in range(1, heads):
        pl.semaphore_signal(barrier, inc=1, device_id=member(step)[1], device_id_type=MESH)
    for step in range(1, groups):
        pl.semaphore_signal(barrier, inc=1, device_id=cousin(step)[1], device_id_type=MESH)
    pl.semaphore_signal(barrier, inc=1, device_id=sibling, device_id_type=MESH)
    pl.semaphore_signal(barrier, inc=1, device_id=device(y, RING - 1 - x, z), device_id_type=MESH)

    pairs = (
        (k_hbm, k_in), (ld_hbm, ld_in), (v_hbm, v_in), (beta_hbm, beta_in), (q_hbm, q_in), (gate_hbm, gate),
        (residual_hbm, residual), (out_gain_hbm, out_gain), (hidden_gain_hbm, hidden_gain),
        (latent_gain_hbm, latent_gain), (ow_hbm, ow), (lw_hbm, lw), (qw_hbm, qw), (ku_hbm, ku), (vu_hbm, vu_ref),
    )
    loads = [pltpu.make_async_copy(src, dst, load_sem.at[i]) for i, (src, dst) in enumerate(pairs)]
    for load in loads[:4]:
        load.start()
    for load in loads[:4]:
        load.wait()
    for load in loads[4:]:
        load.start()

    def map_to(peer):
        return pltpu.make_async_remote_copy(
            src_ref=msg.at[peer], dst_ref=got.at[rank],
            send_sem=send_a.at[peer], recv_sem=recv_a.at[rank],
            device_id=(mine * heads + peer, core), device_id_type=MESH,
        )

    def map_from(peer):
        return pltpu.make_async_remote_copy(
            src_ref=msg.at[peer], dst_ref=got.at[peer],
            send_sem=send_a.at[peer], recv_sem=recv_a.at[peer],
            device_id=(mine * heads + peer, core), device_id_type=MESH,
        )

    def sent(begin, end):
        if begin == 0:
            pl.semaphore_wait(barrier, heads + groups)
        for peer in range(begin, end):
            pl.when(peer != rank)(map_to(peer).start)

    delta_maps(k_in, v_in, ld_in, beta_in, msg, cum, solved, sent)
    got[rank] = msg[rank]
    loads[4].wait()
    delta_outputs(q_in, k_in, cum, solved, base, carry)
    for step in range(1, heads):
        map_from(member(step)[0]).wait_recv()

    maps, diags = [], []
    for i in range(heads):
        matrix, diag = unpack_map(got[i])
        maps.append(matrix)
        diags.append(diag)
    pairs = [after(maps[i + 1], maps[i]) for i in range(0, heads, 2)]
    quads = [after(pairs[i + 1], pairs[i]) for i in range(0, len(pairs), 2)]
    whole = after(quads[1], quads[0])
    diag = diags[0]
    for other_diag in diags[1:]:
        diag = diag * other_diag
    eye = iota((W, W), 0) == iota((W, W), 1)
    total[:W, :W] = (jnp.where(eye, diag, 0.0) - whole[:, :W]).astype(BF16)
    total[:W, W:] = whole[:, W:].astype(BF16)
    total[W:, :] = pack_diag(diag)

    def send_total(step):
        peer, device = cousin(step)
        return peer, pltpu.make_async_remote_copy(
            src_ref=total, dst_ref=totals.at[mine],
            send_sem=send_b.at[peer], recv_sem=recv_b.at[mine],
            device_id=device, device_id_type=MESH,
        )

    def take_total(step):
        peer, device = cousin(step)
        return peer, pltpu.make_async_remote_copy(
            src_ref=total, dst_ref=totals.at[peer],
            send_sem=send_b.at[peer], recv_sem=recv_b.at[peer],
            device_id=device, device_id_type=MESH,
        )

    for step in range(1, groups):
        peer, copy = send_total(step)
        pl.when(peer > mine)(copy.start)

    before = [None] * heads
    before[1] = maps[0]
    before[2] = pairs[0]
    before[4] = quads[0]
    before[3] = after(maps[2], pairs[0])
    before[5] = after(maps[4], quads[0])
    before[6] = after(pairs[2], quads[0])
    before[7] = after(maps[6], before[6])

    for step in range(1, groups):
        peer, copy = take_total(step)
        pl.when(peer < mine)(copy.wait_recv)

    eye_zero = jnp.concatenate([jnp.where(eye, 1.0, 0.0), jnp.zeros((W, W), F32)], axis=1)
    chain = [jnp.where(j < mine, unpack_map(totals[j])[0], eye_zero) for j in range(groups - 1)]
    while len(chain) > 1:
        joined = []
        for i in range(0, len(chain) - 1, 2):
            first = chain[i] if i else chain[i][:, W:]
            joined.append(after(chain[i + 1], first))
        if len(chain) % 2:
            joined.append(chain[-1])
        if joined[0].shape[1] == W:
            joined[0] = jnp.concatenate([jnp.zeros((W, W), F32), joined[0]], axis=1)
        chain = joined
    start = chain[0][:, W:]

    states[0] = start.astype(BF16)
    stacked = mm4(jnp.concatenate([b[:, :W] for b in before[1:]], axis=0), start)
    for i in range(1, heads):
        states[i] = (stacked[(i - 1) * W : i * W] + before[i][:, W:]).astype(BF16)

    def send_state(step):
        peer, device = member(step)
        return pltpu.make_async_remote_copy(
            src_ref=states.at[peer], dst_ref=state_in.at[rank],
            send_sem=send_c.at[peer], recv_sem=recv_c.at[rank],
            device_id=device, device_id_type=MESH,
        )

    def take_state(step):
        peer, device = member(step)
        return pltpu.make_async_remote_copy(
            src_ref=states.at[peer], dst_ref=state_in.at[peer],
            send_sem=send_c.at[peer], recv_sem=recv_c.at[peer],
            device_id=device, device_id_type=MESH,
        )

    for step in range(1, heads):
        send_state(step).start()
    state_in[rank] = states[rank]
    for step in range(1, heads):
        take_state(step).wait_recv()

    for load in loads[5:10]:
        load.wait()
    gated = []
    for h in range(heads):
        cols = slice(h * W, (h + 1) * W)
        raw = base[:, cols] + mm(carry[:, cols], state_in[h])
        raw = raw * lax.rsqrt(jnp.mean(raw * raw, axis=-1, keepdims=True) + EPS)
        logits = gate[:, cols].astype(F32)
        gated.append((raw * out_gain[...] / (1.0 + jnp.exp(-logits))).astype(BF16))
    gated = jnp.concatenate(gated, axis=1)

    loads[10].wait()
    width = partial.shape[2]

    def swap(p):
        return pltpu.make_async_remote_copy(
            src_ref=partial.at[p], dst_ref=other.at[p],
            send_sem=send_p.at[p], recv_sem=recv_p.at[p],
            device_id=sibling, device_id_type=MESH,
        )

    for p in range(PIECES):
        partial[p] = mm(gated, ow[:, p * width : (p + 1) * width])
        swap(p).start()
    squares = 0.0
    hidden = []
    for p in range(PIECES):
        cols = slice(p * width, (p + 1) * width)
        swap(p).wait_recv()
        summed = residual[:, cols].astype(F32) + (partial[p] + other[p])
        rounded = summed.astype(BF16)
        hidden_o[:, cols] = rounded
        rounded = rounded.astype(F32)
        squares = squares + jnp.sum(rounded * rounded, axis=-1, keepdims=True)
        hidden.append(rounded)
    scale = lax.rsqrt(squares / (PIECES * width) + EPS)
    gain = jnp.concatenate([hidden_gain[i : i + 1] for i in range(hidden_gain.shape[0])], axis=1)
    normed = jnp.concatenate(hidden, axis=1) * scale * gain
    normed = normed.astype(BF16)
    loads[11].wait()
    raw = mm(normed, lw[...])
    raw = raw * lax.rsqrt(jnp.mean(raw * raw, axis=-1, keepdims=True) + EPS)
    raw = (raw * latent_gain[...]).astype(BF16)

    def remote(place, peer, send, recv):
        return pltpu.make_async_remote_copy(
            src_ref=place, dst_ref=place, send_sem=send, recv_sem=recv,
            device_id=peer, device_id_type=MESH,
        )

    def a_over_z(step):
        return remote(lat_a.at[core, y, x, z], device(y, x, turn(z, step)), sa1.at[step], ra1.at[RING - step])

    def a_from_z(step):
        return remote(lat_a.at[core, y, x, turn(z, step)], sibling, sa1.at[0], ra1.at[step])

    def a_over_x(step):
        return remote(lat_a.at[core, y, x], device(y, turn(x, step), z), sa2.at[step], ra2.at[RING - step])

    def a_from_x(step):
        return remote(lat_a.at[core, y, turn(x, step)], sibling, sa2.at[0], ra2.at[step])

    def a_over_y(to, step):
        return remote(
            lat_a.at[core, y, turn(x, step)], device(to, x, z), sa3.at[to, step], ra3.at[y, step]
        )

    def a_from_y(at, step):
        return remote(lat_a.at[core, at, turn(x, step)], sibling, sa3.at[at, 0], ra3.at[at, step])

    def axes(at):
        turned = at + RING // 2 == y
        return jnp.where(turned, x, z), jnp.where(turned, z, x)

    def along(at, first, second):
        turned = at + RING // 2 == y
        return device(y, jnp.where(turned, first, second), jnp.where(turned, second, first))

    def b_over_y(to):
        turned = y + RING // 2 == to
        return pltpu.make_async_remote_copy(
            src_ref=lat_b.at[core, y, z, x],
            dst_ref=lat_b.at[core, y, jnp.where(turned, x, z), jnp.where(turned, z, x)],
            send_sem=sb1.at[to], recv_sem=rb1.at[y], device_id=device(to, x, z), device_id_type=MESH,
        )

    def b_from_y(at):
        u, v = axes(at)
        return remote(lat_b.at[core, at, u, v], sibling, sb1.at[at], rb1.at[at])

    def b_over_v(at, step):
        u, v = axes(at)
        return remote(
            lat_b.at[core, at, u, v], along(at, u, turn(v, step)), sb2.at[at, step], rb2.at[at, RING - step]
        )

    def b_from_v(at, step):
        u, v = axes(at)
        return remote(lat_b.at[core, at, u, turn(v, step)], sibling, sb2.at[at, 0], rb2.at[at, step])

    def b_over_u(at, step):
        u, v = axes(at)
        return remote(
            lat_b.at[core, at, u], along(at, turn(u, step), v), sb3.at[at, step], rb3.at[at, RING - step]
        )

    def b_from_u(at, step):
        u, v = axes(at)
        return remote(lat_b.at[core, at, turn(u, step)], sibling, sb3.at[at, 0], rb3.at[at, step])

    def give_a(at, step):
        return remote(lat_a.at[core, at, turn(x, step)], sibling, swap_a.at[at, step], got_a.at[at, step])

    def take_a(at, step):
        return remote(lat_a.at[1 - core, at, turn(x, step)], sibling, swap_a.at[at, step], got_a.at[at, step])

    def give_b(at, step):
        return remote(lat_b.at[core, at, turn(axes(at)[0], step)], sibling, swap_b.at[at, step], got_b.at[at, step])

    def take_b(at, step):
        return remote(lat_b.at[1 - core, at, turn(axes(at)[0], step)], sibling, swap_b.at[at, step], got_b.at[at, step])

    others = (2, 1, 3)

    partner = device(RING - 1 - y, x, z)

    def mail():
        return pltpu.make_async_remote_copy(
            src_ref=mail_out, dst_ref=mail_in, send_sem=sm.at[0], recv_sem=rm.at[0],
            device_id=partner, device_id_type=MESH,
        )

    def note():
        return pltpu.make_async_remote_copy(
            src_ref=note_out, dst_ref=note_in, send_sem=sm.at[1], recv_sem=rm.at[1],
            device_id=partner, device_id_type=MESH,
        )

    def higher(action):
        for to in range(RING - 1, 0, -1):
            pl.when(jnp.logical_and(to > y, to + y != RING - 1))(functools.partial(action, to))

    def lower(action):
        for at in range(RING - 2, -1, -1):
            pl.when(jnp.logical_and(at < y, at + y != RING - 1))(functools.partial(action, at))

    def place_parts(which):
        first = which * 2 * PART
        lat_a[core, y, x, z] = raw[first : first + PART]
        u, v = axes(y)
        lat_b[core, y, u, v] = raw[first + PART : first + 2 * PART]

    for which in range(2):
        pl.when(core == which)(functools.partial(place_parts, which))
    for step in others:
        a_over_z(step).start()
    higher(lambda to: b_over_y(to).start())
    for step in others:
        b_over_v(y, step).start()

    def clear(store):
        store[1][...] = jnp.full(store[1].shape, -1e30, F32)
        store[2][...] = jnp.zeros(store[2].shape, F32)
        store[3][...] = jnp.zeros(store[3].shape, F32)

    clear((qp_ref, row_max, row_sum, accum))
    block = GROUP * rows

    def spread_a(step):
        higher(lambda to: a_over_y(to, step).start())
        give_a(y, step).start()

    def spread_b(at):
        for step in others:
            b_from_v(at, step).wait_recv()
        for step in others:
            b_over_u(at, step).start()
        give_b(at, 0).start()

    loads[12].wait()
    mail_out[...] = mm(normed, qw[...]).astype(BF16)
    pl.when(y >= RING // 2)(lambda: mail().start())
    for step in others:
        a_from_z(step).wait_recv()
    for step in others:
        a_over_x(step).start()
    spread_a(0)
    spread_b(y)

    def pass_b(at):
        b_from_y(at).wait_recv()
        for step in others:
            b_over_v(at, step).start()

    lower(pass_b)
    loads[13].wait()

    mine_store = (qp_ref, row_max, row_sum, accum)
    far_store = (far_qp, far_max, far_sum, far_accum)

    def absorb(queries, store):
        for h in range(heads):
            cols = slice(h * W, (h + 1) * W)
            store[0][h] = (mm_nt(queries[:, cols], ku[:, cols]) * SCORE_SCALE).astype(BF16)

    absorb(mail_out, mine_store)

    def attend(pieces, mask, store):
        query, top, total_sum, mixed_sum = store
        keys = jnp.concatenate([piece.reshape(line, latent) for piece in pieces], axis=0)
        count = keys.shape[0]
        for b in range(0, heads, GROUP):
            place = slice(b * rows, b * rows + block)
            queries = query[b : b + GROUP].reshape(block, latent)
            scores = mm_nt(queries, keys)
            if mask is not None:
                query_pos = here * rows + iota((block, count), 0) % rows
                scores = jnp.where(mask((1, count)) <= query_pos, scores, -2e30)
            old = top[place, :]
            new = jnp.maximum(old, jnp.max(scores, axis=-1, keepdims=True))
            top[place, :] = new
            shrink = jnp.exp2(old - new)
            probs = [jnp.exp2(scores[:, c : c + W] - new) for c in range(0, count, W)]
            added = total_sum[place, :] * shrink
            for p in probs:
                added = added + p
            total_sum[place, :] = added
            mixed = mm(jnp.concatenate([p.astype(BF16) for p in probs], axis=1), keys)
            mixed_sum[place, :] = mixed_sum[place, :] * jnp.concatenate([shrink] * (latent // W), axis=1) + mixed

    def own_lines(step):
        u = turn(z, step)
        line_x = turn(x, step)
        return lat_a[0, y, line_x], lat_a[1, y, line_x], lat_b[0, y, u], lat_b[1, y, u]

    def own(step):
        u = turn(z, step)
        line_x = turn(x, step)

        def positions(shape):
            column = iota(shape, 1)
            slot, inner, piece = (column // PART) % RING, column % PART, column // line
            part_b = piece // 2
            chip_a = line_x * RING + slot
            chip_b = slot * RING + u
            chip = jnp.where(part_b == 1, chip_b, chip_a)
            return (y * RING * RING + chip) * rows + (piece % 2) * (2 * PART) + part_b * PART + inner

        take_a(y, step).wait_recv()
        take_b(y, step).wait_recv()
        attend(own_lines(step), positions, mine_store)

    def fetch_a(at, step):
        a_from_y(at, step).wait_recv()
        give_a(at, step).start()

    def fetch_b(at, step):
        def far():
            b_from_u(at, step).wait_recv()
            give_b(at, step).start()

        pl.when(step > 0)(far)

    def both(pair, visit):
        for s in range(2):
            visit(jnp.where(pair == 0, s, RING - 1 - s))

    def loop(begin, end, visit):
        lax.fori_loop(begin, end, lambda i, nothing: (visit(i), nothing)[1], 0)

    below = jnp.where(y == RING - 1, 2, jnp.where(y == 0, 0, 1))

    def plane(i):
        return jnp.where(y == RING - 1, RING - 2 - i // 2, 0)

    def fetch(at, pair):
        both(pair, lambda step: fetch_a(at, step))
        both(pair, lambda step: fetch_b(at, step))

    def pass_a(step):
        a_from_x(step).wait_recv()
        spread_a(step)
        fetch_b(y, step)

    own(0)
    lower(spread_b)
    pass_a(1)
    pass_a(3)

    @pl.when(y < RING // 2)
    def _():
        clear(far_store)
        mail().wait_recv()
        absorb(mail_in, far_store)

    def own_round(i):
        pl.when(i == 1)(lambda: pass_a(2))
        pl.when(jnp.logical_and(i == 2, y > 0))(lambda: fetch(plane(0), 0))
        own(jnp.where(i == 0, 1, jnp.where(i == 1, 3, 2)))

        @pl.when(jnp.logical_and(y < RING // 2, i != 1))
        def _():
            first, second = jnp.where(i == 0, 0, 3), jnp.where(i == 0, 1, 2)
            attend(own_lines(first) + own_lines(second), None, far_store)

    loop(0, RING - 1, own_round)

    loads[14].wait()

    def result(h, store):
        place = slice(h * rows, (h + 1) * rows)
        row_total = jnp.sum(store[2][place, :], axis=-1, keepdims=True)
        high, low = halves(store[3][place, :] * (1.0 / row_total))
        up = vu_ref[:, h * W : (h + 1) * W]
        both_parts = mm(jnp.concatenate([high, low], axis=0), up)
        return both_parts[:rows] + both_parts[rows:], store[1][place, :] + jnp.log2(row_total)

    @pl.when(y < RING // 2)
    def _():
        lane = iota((rows, W), 1)
        level = jnp.zeros((rows, W), F32)
        for h in range(heads):
            mixed, log_sum = result(h, far_store)
            mail_out[:, h * W : (h + 1) * W] = mixed.astype(BF16)
            level = jnp.where(lane == h, log_sum, level)
        note_out[...] = level
        note().start()
        mail().start()

    def earlier(i):
        at, pair = plane(i), i % 2
        steps = (jnp.where(pair == 0, 0, 3), jnp.where(pair == 0, 1, 2))
        pl.when(i + 1 < 2 * below)(lambda: fetch(plane(i + 1), (i + 1) % 2))
        both(pair, lambda step: take_a(at, step).wait_recv())
        both(pair, lambda step: take_b(at, step).wait_recv())
        u = axes(at)[0]
        attend(
            [lat_a[c, at, turn(x, step)] for step in steps for c in range(2)]
            + [lat_b[c, at, turn(u, step)] for step in steps for c in range(2)],
            None, mine_store,
        )

    loop(0, 2 * below, earlier)

    @pl.when(y < RING // 2)
    def _():
        for h in range(heads):
            out_ref[:, h * W : (h + 1) * W] = result(h, mine_store)[0].astype(BF16)
        note().wait_send()
        mail().wait_send()

    @pl.when(y >= RING // 2)
    def _():
        mail().wait_send()
        note().wait_recv()
        mail().wait_recv()
        for h in range(heads):
            cols = slice(h * W, (h + 1) * W)
            mixed, log_sum = result(h, mine_store)
            gap = log_sum - note_in[:, h : h + 1]
            far = mail_in[:, cols].astype(F32)
            out_ref[:, cols] = (
                mixed / (1.0 + jnp.exp2(-gap)) + far / (1.0 + jnp.exp2(gap))
            ).astype(BF16)

    for step in others:
        a_over_z(step).wait_send()
        a_over_x(step).wait_send()

    def drain_up(to):
        b_over_y(to).wait_send()
        for step in range(RING):
            a_over_y(to, step).wait_send()

    higher(drain_up)

    def drain(at):
        for step in range(1, RING):
            b_over_v(at, step).wait_send()
            b_over_u(at, step).wait_send()
        for step in range(RING):
            give_a(at, step).wait_send()
            give_b(at, step).wait_send()

    loop(0, below, lambda i: drain(plane(2 * i)))
    drain(y)


    for step in range(1, heads):
        map_to(member(step)[0]).wait_send()
        send_state(step).wait_send()
    for step in range(1, groups):
        peer, copy = send_total(step)
        pl.when(peer > mine)(copy.wait_send)
    for p in range(PIECES):
        swap(p).wait_send()


def layer(q, k, v, ld, beta, gate, residual, out_gain, hidden_gain, latent_gain, ow, lw, qw, ku, vu):
    heads = beta.shape[0]
    rows, width = residual.shape
    latent = lw.shape[1]
    groups = lax.axis_size("seq") // heads
    vm = pl.BlockSpec(memory_space=pltpu.VMEM)
    anywhere = pl.BlockSpec(memory_space=pl.ANY)
    dma = pltpu.SemaphoreType.DMA
    operands = (q, k, v, ld, beta, gate, residual, out_gain, hidden_gain, latent_gain, ow, lw, qw, ku, vu)
    message = (W + 16, 2 * W)
    one, two = dma((RING,)), dma((RING, RING))
    return pl.pallas_call(
        layer_kernel,
        out_shape=(
            jax.ShapeDtypeStruct((rows, width), BF16),
            jax.ShapeDtypeStruct((rows, heads * W), BF16),
        ),
        in_specs=[anywhere] * len(operands),
        out_specs=(vm, vm),
        scratch_shapes=[pltpu.VMEM(a.shape, a.dtype) for a in operands] + [
            pltpu.VMEM((rows, heads * W), F32),
            pltpu.VMEM((heads, rows, 2 * W), F32),
            pltpu.VMEM((heads,) + message, BF16),
            pltpu.VMEM((rows, heads * W), F32),
            pltpu.VMEM((rows, heads * W), BF16),
            pltpu.VMEM((heads,) + message, BF16),
            pltpu.VMEM(message, BF16),
            pltpu.VMEM((groups,) + message, BF16),
            pltpu.VMEM((heads, W, W), BF16),
            pltpu.VMEM((heads, W, W), BF16),
            pltpu.VMEM((PIECES, rows, width // PIECES), F32),
            pltpu.VMEM((PIECES, rows, width // PIECES), F32),
            pltpu.VMEM((heads, rows, latent), BF16),
            pltpu.VMEM((2, RING, RING, RING, PART, latent), BF16),
            pltpu.VMEM((2, RING, RING, RING, PART, latent), BF16),
            pltpu.VMEM((heads * rows, W), F32),
            pltpu.VMEM((heads * rows, W), F32),
            pltpu.VMEM((heads * rows, latent), F32),
            pltpu.VMEM((heads, rows, latent), BF16),
            pltpu.VMEM((heads * rows, W), F32),
            pltpu.VMEM((heads * rows, W), F32),
            pltpu.VMEM((heads * rows, latent), F32),
            pltpu.VMEM((rows, heads * W), BF16),
            pltpu.VMEM((rows, heads * W), BF16),
            pltpu.VMEM((rows, W), F32),
            pltpu.VMEM((rows, W), F32),
            dma((len(operands),)),
            dma((heads,)), dma((heads,)), dma((groups,)), dma((groups,)),
            dma((heads,)), dma((heads,)), dma((PIECES,)), dma((PIECES,)),
            one, one, one, one, two, two, one, one, two, two, two, two, two, two, two, two,
            dma((2,)), dma((2,)),
        ],
        compiler_params=pltpu.CompilerParams(
            collective_id=0, has_side_effects=True, vmem_limit_bytes=60 * 2**20
        ),
        name="layer",
    )(*operands)


def finish_kernel(hidden_in, attended_in, hidden_out, attended_out):
    hidden_out[...] = hidden_in[...]
    attended_out[...] = attended_in[...]


def finish(hidden, attended):
    vm = pl.BlockSpec(memory_space=pltpu.VMEM)
    return pl.pallas_call(
        finish_kernel,
        out_shape=tuple(jax.ShapeDtypeStruct(a.shape, a.dtype) for a in (hidden, attended)),
        in_specs=[vm] * 2,
        out_specs=(vm, vm),
        name="finish",
    )(hidden, attended)


def body(
    residual, kda_query, kda_key, kda_value, log_decay, beta_logit, out_gate, out_gain, out_weight,
    hidden_gain, query_weight, latent_weight, latent_gain, key_up_weight, value_up_weight,
):
    hidden, attended = layer(
        kda_query, kda_key, kda_value, log_decay, beta_logit.T, out_gate, residual, out_gain[None],
        hidden_gain.reshape(-1, W), latent_gain[None], out_weight, latent_weight, query_weight, key_up_weight,
        value_up_weight,
    )
    return finish(hidden, attended)


def solution(mesh):
    in_specs = (
        P("seq", None),
        P("seq", "head"),
        P("seq", "head"),
        P("seq", "head"),
        P("seq", "head"),
        P("seq", "head"),
        P("seq", "head"),
        P(),
        P("head", None),
        P(),
        P(None, "head"),
        P(),
        P(),
        P(None, "head"),
        P(None, "head"),
    )
    out_specs = (P("seq", None), P("seq", "head"))
    return jax.shard_map(body, mesh=mesh, in_specs=in_specs, out_specs=out_specs, check_vma=False)
```

```python
import functools
import jax
import jax.numpy as jnp
from jax import lax
from jax.sharding import PartitionSpec as P
from jax.experimental import pallas as pl
from jax.experimental.pallas import tpu as pltpu

F32 = jnp.float32
BF16 = jnp.bfloat16
W = 128
EPS = 1e-06


def halves(x):
    high = x.astype(BF16)
    return high, (x - high.astype(F32)).astype(BF16)


def mm(a, b):
    return jnp.dot(a, b, preferred_element_type=F32)


def mm_nt(a, b):
    return lax.dot_general(a, b, (((1,), (1,)), ((), ())), preferred_element_type=F32)


def wide(x):
    high, low = halves(x)
    return jnp.concatenate([high, low], axis=1)


def mm4(a, b):
    n = b.shape[1]
    right = wide(b)
    out = mm(wide(a), jnp.concatenate([right, right], axis=0))
    return out[:, :n] + out[:, n:]


def mm4_nt(a, b):
    n = b.shape[0]
    high, low = halves(b)
    right = jnp.concatenate(
        [jnp.concatenate([high, high], axis=1), jnp.concatenate([low, low], axis=1)], axis=0
    )
    out = mm_nt(wide(a), right)
    return out[:, :n] + out[:, n:]


def iota(shape, axis):
    return lax.broadcasted_iota(jnp.int32, shape, axis)


PIECES = 2
MESH = pl.DeviceIdType.MESH
SCORE_SCALE = W ** (-0.5) * 1.4426950408889634
RING = 4
PART = 32
GROUP = 8
DELTA_GROUP = 8
SEND_GROUP = 4


def pack_diag(closing):
    high, rest = halves(closing)
    r = iota((16, W), 0)
    block = jnp.where(r == 0, high.astype(F32), jnp.where(r == 1, rest.astype(F32), 0.0))
    return jnp.concatenate([block, jnp.zeros((16, W), F32)], axis=1).astype(BF16)


def unpack_map(block):
    diag = block[W : W + 1, :W].astype(F32) + block[W + 1 : W + 2, :W].astype(F32)
    eye = iota((W, W), 0) == iota((W, W), 1)
    matrix = jnp.where(eye, diag, 0.0) - block[:W, :W].astype(F32)
    return jnp.concatenate([matrix, block[:W, W:].astype(F32)], axis=1), diag


def after(later, earlier):
    n = earlier.shape[1]
    out = mm4(later[:, :W], earlier)
    if n == 2 * W:
        return jnp.concatenate([out[:, :W], out[:, W:] + later[:, W:]], axis=1)
    return out + later[:, W:]


def unit(values):
    return values * lax.rsqrt(jnp.sum(values * values, axis=-1, keepdims=True) + EPS)


def triangle(rows):
    ti, si = iota((rows, rows), 0), iota((rows, rows), 1)
    return ti, si, si < ti


def second_rows(x, size):
    return jnp.concatenate(
        [x[i + size : i + 2 * size] for i in range(0, x.shape[0], 2 * size)], axis=0
    )


def invert(lowers):
    rows = lowers[0].shape[0]
    ti, si, strict = triangle(rows)
    eye = jnp.where(si == ti, 1.0, 0.0)
    level = jnp.logical_and((ti // 2) == (si // 2), strict)
    found = [eye - jnp.where(level, low, 0.0) for low in lowers]
    size = 2
    while size < rows:
        level = jnp.logical_and((ti // (2 * size)) == (si // (2 * size)), (ti // size) > (si // size))
        inside = [jnp.where(level, low, 0.0) for low in lowers]
        if size < 8:
            inner = [mm4(low, x) for low, x in zip(inside, found)]
            found = [x - mm4(x, y) for x, y in zip(found, inner)]
        else:
            zero = jnp.zeros((size, rows), F32)
            inner = [mm4(second_rows(low, size), x) for low, x in zip(inside, found)]
            inner = [
                jnp.concatenate(
                    [part for i in range(0, rows // 2, size) for part in (zero, y[i : i + size])], axis=0
                )
                for y in inner
            ]
            change = [mm4(second_rows(x, size), y) for x, y in zip(found, inner)]
            found = [
                jnp.concatenate(
                    [
                        part
                        for i in range(0, rows // 2, size)
                        for part in (
                            x[2 * i : 2 * i + size],
                            x[2 * i + size : 2 * i + 2 * size] - y[i : i + size],
                        )
                    ],
                    axis=0,
                )
                for x, y in zip(found, change)
            ]
        size *= 2
    return found


def delta_maps(k_ref, v_ref, ld_ref, beta_ref, msg_ref, cum_ref, solved_ref, sent):
    rows = k_ref.shape[0]
    heads = k_ref.shape[1] // W
    ti, si, strict = triangle(rows)
    ones = jnp.where(si <= ti, 1.0, 0.0).astype(BF16)
    rates = (1.0 / (1.0 + jnp.exp(-beta_ref[...]))).T
    ld = ld_ref[...]
    high, rest = halves(ld)
    low = (ld - high.astype(F32) - rest.astype(F32)).astype(BF16)
    twice = jnp.concatenate([ones, ones], axis=1)
    cum_ref[...] = mm(twice, jnp.concatenate([high, rest], axis=0)) + mm(ones, low)

    def prepare(h):
        cols = slice(h * W, (h + 1) * W)
        cum = cum_ref[:, cols]
        mid = cum[rows // 2 - 1 : rows // 2, :]
        end = cum[rows - 1 : rows, :]
        key = unit(k_ref[:, cols].astype(F32))
        mixed = mm4_nt(key * jnp.exp(cum - mid), key * jnp.exp(mid - cum))
        rate = rates[:, h : h + 1]
        lower = jnp.where(strict, mixed, 0.0) * rate
        right = jnp.concatenate(
            [rate * v_ref[:, cols].astype(F32), rate * (key * jnp.exp(cum))], axis=1
        )
        return lower, right, (key * jnp.exp(end - cum)).T, jnp.exp(end)

    for start in range(0, heads, DELTA_GROUP):
        made = [prepare(h) for h in range(start, start + DELTA_GROUP)]
        inverses = invert([m[0] for m in made])
        for h, inverse, (_, right, tail, closing) in zip(
            range(start, start + DELTA_GROUP), inverses, made
        ):
            solved = mm4(inverse, right)
            solved_ref[h] = solved
            state = mm4(tail, solved)
            msg_ref[h, :W, :W] = state[:, W:].astype(BF16)
            msg_ref[h, :W, W:] = state[:, :W].astype(BF16)
            msg_ref[h, W:, :] = pack_diag(closing)
            if (h + 1) % SEND_GROUP == 0:
                sent(h + 1 - SEND_GROUP, h + 1)


def delta_outputs(q_ref, k_ref, cum_ref, solved_ref, base_ref, carry_ref):
    rows = k_ref.shape[0]
    ti, si, _ = triangle(rows)
    for h in range(k_ref.shape[1] // W):
        cols = slice(h * W, (h + 1) * W)
        cum = cum_ref[:, cols]
        mid = cum[rows // 2 - 1 : rows // 2, :]
        key = unit(k_ref[:, cols].astype(F32))
        query = unit(q_ref[:, cols].astype(F32))
        mixed = mm4_nt(query * jnp.exp(cum - mid), key * jnp.exp(mid - cum))
        out = mm4(jnp.where(si <= ti, mixed, 0.0), solved_ref[h])
        base_ref[:, cols] = out[:, :W]
        carry_ref[:, cols] = (query * jnp.exp(cum) - out[:, W:]).astype(BF16)


def layer_kernel(
    q_hbm, k_hbm, v_hbm, ld_hbm, beta_hbm, gate_hbm, residual_hbm, out_gain_hbm, hidden_gain_hbm,
    latent_gain_hbm, ow_hbm, lw_hbm, qw_hbm, ku_hbm, vu_hbm,
    hidden_o, out_ref,
    q_in, k_in, v_in, ld_in, beta_in, gate, residual, out_gain, hidden_gain, latent_gain, ow, lw, qw, ku, vu_ref,
    cum, solved, msg, base, carry, got, total, totals, states, state_in, partial, other,
    qp_ref, lat_a, lat_b, row_max, row_sum, accum, far_qp, far_max, far_sum, far_accum, mail_out, mail_in, note_out, note_in,
    load_sem, send_a, recv_a, send_b, recv_b, send_c, recv_c, send_p, recv_p,
    sa1, ra1, sa2, ra2, sa3, ra3, sb1, rb1, sb2, rb2, sb3, rb3, swap_a, got_a, swap_b, got_b, sm, rm,
):
    heads = msg.shape[0]
    groups = totals.shape[0]
    rows, latent = residual.shape[0], lw.shape[1]
    here, core = lax.axis_index("seq"), lax.axis_index("head")
    mine, rank = here // heads, here % heads
    y, x, z = here // (RING * RING), (here // RING) % RING, here % RING
    line = RING * PART
    sibling = (here, 1 - core)

    def device(to_y, to_x, to_z):
        return (to_y * RING * RING + to_x * RING + to_z, core)

    def turn(coordinate, step):
        return (coordinate + step) % RING

    def member(step):
        peer = (rank + step) % heads
        return peer, (mine * heads + peer, core)

    def cousin(step):
        peer = (mine + step) % groups
        return peer, (peer * heads + rank, core)

    barrier = pltpu.get_barrier_semaphore()
    for step in range(1, heads):
        pl.semaphore_signal(barrier, inc=1, device_id=member(step)[1], device_id_type=MESH)
    for step in range(1, groups):
        pl.semaphore_signal(barrier, inc=1, device_id=cousin(step)[1], device_id_type=MESH)
    pl.semaphore_signal(barrier, inc=1, device_id=sibling, device_id_type=MESH)
    pl.semaphore_signal(barrier, inc=1, device_id=device(y, RING - 1 - x, z), device_id_type=MESH)

    pairs = (
        (k_hbm, k_in), (ld_hbm, ld_in), (v_hbm, v_in), (beta_hbm, beta_in), (q_hbm, q_in), (gate_hbm, gate),
        (residual_hbm, residual), (out_gain_hbm, out_gain), (hidden_gain_hbm, hidden_gain),
        (latent_gain_hbm, latent_gain), (ow_hbm, ow), (lw_hbm, lw), (qw_hbm, qw), (ku_hbm, ku), (vu_hbm, vu_ref),
    )
    loads = [pltpu.make_async_copy(src, dst, load_sem.at[i]) for i, (src, dst) in enumerate(pairs)]
    for load in loads[:4]:
        load.start()
    for load in loads[:4]:
        load.wait()
    for load in loads[4:]:
        load.start()

    def map_to(peer):
        return pltpu.make_async_remote_copy(
            src_ref=msg.at[peer], dst_ref=got.at[rank],
            send_sem=send_a.at[peer], recv_sem=recv_a.at[rank],
            device_id=(mine * heads + peer, core), device_id_type=MESH,
        )

    def map_from(peer):
        return pltpu.make_async_remote_copy(
            src_ref=msg.at[peer], dst_ref=got.at[peer],
            send_sem=send_a.at[peer], recv_sem=recv_a.at[peer],
            device_id=(mine * heads + peer, core), device_id_type=MESH,
        )

    def sent(begin, end):
        if begin == 0:
            pl.semaphore_wait(barrier, heads + groups)
        for peer in range(begin, end):
            pl.when(peer != rank)(map_to(peer).start)

    delta_maps(k_in, v_in, ld_in, beta_in, msg, cum, solved, sent)
    got[rank] = msg[rank]
    loads[4].wait()
    delta_outputs(q_in, k_in, cum, solved, base, carry)
    for step in range(1, heads):
        map_from(member(step)[0]).wait_recv()

    maps, diags = [], []
    for i in range(heads):
        matrix, diag = unpack_map(got[i])
        maps.append(matrix)
        diags.append(diag)
    pairs = [after(maps[i + 1], maps[i]) for i in range(0, heads, 2)]
    quads = [after(pairs[i + 1], pairs[i]) for i in range(0, len(pairs), 2)]
    whole = after(quads[1], quads[0])
    diag = diags[0]
    for other_diag in diags[1:]:
        diag = diag * other_diag
    eye = iota((W, W), 0) == iota((W, W), 1)
    total[:W, :W] = (jnp.where(eye, diag, 0.0) - whole[:, :W]).astype(BF16)
    total[:W, W:] = whole[:, W:].astype(BF16)
    total[W:, :] = pack_diag(diag)

    def total_copy(peer, slot, device, first):
        place = (slice(0, W), slice(W, 2 * W)) if first else (slice(None), slice(None))
        return pltpu.make_async_remote_copy(
            src_ref=total.at[place], dst_ref=totals.at[(slot,) + place],
            send_sem=send_b.at[peer], recv_sem=recv_b.at[slot],
            device_id=device, device_id_type=MESH,
        )

    def each_total(step, action):
        peer, device = cousin(step)

        @pl.when(jnp.logical_and(peer > mine, mine == 0))
        def _():
            action(total_copy(peer, mine, device, True))

        @pl.when(jnp.logical_and(peer > mine, mine > 0))
        def _():
            action(total_copy(peer, mine, device, False))

    def take_total(step):
        peer, device = cousin(step)

        @pl.when(jnp.logical_and(peer < mine, peer == 0))
        def _():
            total_copy(peer, peer, device, True).wait_recv()

        @pl.when(jnp.logical_and(peer < mine, peer > 0))
        def _():
            total_copy(peer, peer, device, False).wait_recv()

    for step in range(1, groups):
        each_total(step, lambda copy: copy.start())

    before = [None] * heads
    before[1] = maps[0]
    before[2] = pairs[0]
    before[4] = quads[0]
    before[3] = after(maps[2], pairs[0])
    before[5] = after(maps[4], quads[0])
    before[6] = after(pairs[2], quads[0])
    before[7] = after(maps[6], before[6])

    for step in range(1, groups):
        take_total(step)

    eye_zero = jnp.concatenate([jnp.where(eye, 1.0, 0.0), jnp.zeros((W, W), F32)], axis=1)
    chain = [jnp.where(j < mine, unpack_map(totals[j])[0], eye_zero) for j in range(groups - 1)]
    while len(chain) > 1:
        joined = []
        for i in range(0, len(chain) - 1, 2):
            first = chain[i] if i else chain[i][:, W:]
            joined.append(after(chain[i + 1], first))
        if len(chain) % 2:
            joined.append(chain[-1])
        if joined[0].shape[1] == W:
            joined[0] = jnp.concatenate([jnp.zeros((W, W), F32), joined[0]], axis=1)
        chain = joined
    start = chain[0][:, W:]

    states[0] = start.astype(BF16)
    stacked = mm4(jnp.concatenate([b[:, :W] for b in before[1:]], axis=0), start)
    for i in range(1, heads):
        states[i] = (stacked[(i - 1) * W : i * W] + before[i][:, W:]).astype(BF16)

    def send_state(step):
        peer, device = member(step)
        return pltpu.make_async_remote_copy(
            src_ref=states.at[peer], dst_ref=state_in.at[rank],
            send_sem=send_c.at[peer], recv_sem=recv_c.at[rank],
            device_id=device, device_id_type=MESH,
        )

    def take_state(step):
        peer, device = member(step)
        return pltpu.make_async_remote_copy(
            src_ref=states.at[peer], dst_ref=state_in.at[peer],
            send_sem=send_c.at[peer], recv_sem=recv_c.at[peer],
            device_id=device, device_id_type=MESH,
        )

    for step in range(1, heads):
        send_state(step).start()
    state_in[rank] = states[rank]
    for step in range(1, heads):
        take_state(step).wait_recv()

    for load in loads[5:10]:
        load.wait()
    gated = []
    for h in range(heads):
        cols = slice(h * W, (h + 1) * W)
        raw = base[:, cols] + mm(carry[:, cols], state_in[h])
        raw = raw * lax.rsqrt(jnp.mean(raw * raw, axis=-1, keepdims=True) + EPS)
        logits = gate[:, cols].astype(F32)
        gated.append((raw * out_gain[...] / (1.0 + jnp.exp(-logits))).astype(BF16))
    gated = jnp.concatenate(gated, axis=1)

    loads[10].wait()
    width = partial.shape[2]

    def swap(p):
        return pltpu.make_async_remote_copy(
            src_ref=partial.at[p], dst_ref=other.at[p],
            send_sem=send_p.at[p], recv_sem=recv_p.at[p],
            device_id=sibling, device_id_type=MESH,
        )

    for p in range(PIECES):
        partial[p] = mm(gated, ow[:, p * width : (p + 1) * width])
        swap(p).start()
    squares = 0.0
    hidden = []
    for p in range(PIECES):
        cols = slice(p * width, (p + 1) * width)
        swap(p).wait_recv()
        summed = residual[:, cols].astype(F32) + (partial[p] + other[p])
        rounded = summed.astype(BF16)
        hidden_o[:, cols] = rounded
        rounded = rounded.astype(F32)
        squares = squares + jnp.sum(rounded * rounded, axis=-1, keepdims=True)
        hidden.append(rounded)
    scale = lax.rsqrt(squares / (PIECES * width) + EPS)
    gain = jnp.concatenate([hidden_gain[i : i + 1] for i in range(hidden_gain.shape[0])], axis=1)
    normed = jnp.concatenate(hidden, axis=1) * scale * gain
    normed = normed.astype(BF16)
    loads[11].wait()
    raw = mm(normed, lw[...])
    raw = raw * lax.rsqrt(jnp.mean(raw * raw, axis=-1, keepdims=True) + EPS)
    raw = (raw * latent_gain[...]).astype(BF16)

    def remote(place, peer, send, recv):
        return pltpu.make_async_remote_copy(
            src_ref=place, dst_ref=place, send_sem=send, recv_sem=recv,
            device_id=peer, device_id_type=MESH,
        )

    def a_over_z(step):
        return remote(lat_a.at[core, y, x, z], device(y, x, turn(z, step)), sa1.at[step], ra1.at[RING - step])

    def a_from_z(step):
        return remote(lat_a.at[core, y, x, turn(z, step)], sibling, sa1.at[0], ra1.at[step])

    def a_over_x(step):
        return remote(lat_a.at[core, y, x], device(y, turn(x, step), z), sa2.at[step], ra2.at[RING - step])

    def a_from_x(step):
        return remote(lat_a.at[core, y, turn(x, step)], sibling, sa2.at[0], ra2.at[step])

    def a_over_y(to, step):
        return remote(
            lat_a.at[core, y, turn(x, step)], device(to, x, z), sa3.at[to, step], ra3.at[y, step]
        )

    def a_from_y(at, step):
        return remote(lat_a.at[core, at, turn(x, step)], sibling, sa3.at[at, 0], ra3.at[at, step])

    def axes(at):
        turned = at + RING // 2 == y
        return jnp.where(turned, x, z), jnp.where(turned, z, x)

    def along(at, first, second):
        turned = at + RING // 2 == y
        return device(y, jnp.where(turned, first, second), jnp.where(turned, second, first))

    def b_over_y(to):
        turned = y + RING // 2 == to
        return pltpu.make_async_remote_copy(
            src_ref=lat_b.at[core, y, z, x],
            dst_ref=lat_b.at[core, y, jnp.where(turned, x, z), jnp.where(turned, z, x)],
            send_sem=sb1.at[to], recv_sem=rb1.at[y], device_id=device(to, x, z), device_id_type=MESH,
        )

    def b_from_y(at):
        u, v = axes(at)
        return remote(lat_b.at[core, at, u, v], sibling, sb1.at[at], rb1.at[at])

    def b_over_v(at, step):
        u, v = axes(at)
        return remote(
            lat_b.at[core, at, u, v], along(at, u, turn(v, step)), sb2.at[at, step], rb2.at[at, RING - step]
        )

    def b_from_v(at, step):
        u, v = axes(at)
        return remote(lat_b.at[core, at, u, turn(v, step)], sibling, sb2.at[at, 0], rb2.at[at, step])

    def b_over_u(at, step):
        u, v = axes(at)
        return remote(
            lat_b.at[core, at, u], along(at, turn(u, step), v), sb3.at[at, step], rb3.at[at, RING - step]
        )

    def b_from_u(at, step):
        u, v = axes(at)
        return remote(lat_b.at[core, at, turn(u, step)], sibling, sb3.at[at, 0], rb3.at[at, step])

    def give_a(at, step):
        return remote(lat_a.at[core, at, turn(x, step)], sibling, swap_a.at[at, step], got_a.at[at, step])

    def take_a(at, step):
        return remote(lat_a.at[1 - core, at, turn(x, step)], sibling, swap_a.at[at, step], got_a.at[at, step])

    def give_b(at, step):
        return remote(lat_b.at[core, at, turn(axes(at)[0], step)], sibling, swap_b.at[at, step], got_b.at[at, step])

    def take_b(at, step):
        return remote(lat_b.at[1 - core, at, turn(axes(at)[0], step)], sibling, swap_b.at[at, step], got_b.at[at, step])

    others = (2, 1, 3)

    partner = device(RING - 1 - y, x, z)

    def mail():
        return pltpu.make_async_remote_copy(
            src_ref=mail_out, dst_ref=mail_in, send_sem=sm.at[0], recv_sem=rm.at[0],
            device_id=partner, device_id_type=MESH,
        )

    def note():
        return pltpu.make_async_remote_copy(
            src_ref=note_out, dst_ref=note_in, send_sem=sm.at[1], recv_sem=rm.at[1],
            device_id=partner, device_id_type=MESH,
        )

    def higher(action):
        for to in range(RING - 1, 0, -1):
            pl.when(jnp.logical_and(to > y, to + y != RING - 1))(functools.partial(action, to))

    def lower(action):
        for at in range(RING - 2, -1, -1):
            pl.when(jnp.logical_and(at < y, at + y != RING - 1))(functools.partial(action, at))

    def place_parts(which):
        first = which * 2 * PART
        lat_a[core, y, x, z] = raw[first : first + PART]
        u, v = axes(y)
        lat_b[core, y, u, v] = raw[first + PART : first + 2 * PART]

    for which in range(2):
        pl.when(core == which)(functools.partial(place_parts, which))
    for step in others:
        a_over_z(step).start()
    higher(lambda to: b_over_y(to).start())
    for step in others:
        b_over_v(y, step).start()

    def clear(store):
        store[1][...] = jnp.full(store[1].shape, -1e30, F32)
        store[2][...] = jnp.zeros(store[2].shape, F32)
        store[3][...] = jnp.zeros(store[3].shape, F32)

    clear((qp_ref, row_max, row_sum, accum))
    block = GROUP * rows

    def spread_a(step):
        higher(lambda to: a_over_y(to, step).start())
        give_a(y, step).start()

    def spread_b(at):
        for step in others:
            b_from_v(at, step).wait_recv()
        for step in others:
            b_over_u(at, step).start()
        give_b(at, 0).start()

    loads[12].wait()
    mail_out[...] = mm(normed, qw[...]).astype(BF16)
    pl.when(y >= RING // 2)(lambda: mail().start())
    for step in others:
        a_from_z(step).wait_recv()
    for step in others:
        a_over_x(step).start()
    spread_a(0)
    spread_b(y)

    def pass_b(at):
        b_from_y(at).wait_recv()
        for step in others:
            b_over_v(at, step).start()

    lower(pass_b)
    loads[13].wait()

    mine_store = (qp_ref, row_max, row_sum, accum)
    far_store = (far_qp, far_max, far_sum, far_accum)

    def absorb(queries, store):
        for h in range(heads):
            cols = slice(h * W, (h + 1) * W)
            store[0][h] = (mm_nt(queries[:, cols], ku[:, cols]) * SCORE_SCALE).astype(BF16)

    absorb(mail_out, mine_store)

    def attend(pieces, mask, store):
        query, top, total_sum, mixed_sum = store
        keys = jnp.concatenate([piece.reshape(line, latent) for piece in pieces], axis=0)
        count = keys.shape[0]
        for b in range(0, heads, GROUP):
            place = slice(b * rows, b * rows + block)
            queries = query[b : b + GROUP].reshape(block, latent)
            scores = mm_nt(queries, keys)
            if mask is not None:
                query_pos = here * rows + iota((block, count), 0) % rows
                scores = jnp.where(mask((1, count)) <= query_pos, scores, -2e30)
            old = top[place, :]
            new = jnp.maximum(old, jnp.max(scores, axis=-1, keepdims=True))
            top[place, :] = new
            shrink = jnp.exp2(old - new)
            probs = [jnp.exp2(scores[:, c : c + W] - new) for c in range(0, count, W)]
            added = total_sum[place, :] * shrink
            for p in probs:
                added = added + p
            total_sum[place, :] = added
            mixed = mm(jnp.concatenate([p.astype(BF16) for p in probs], axis=1), keys)
            mixed_sum[place, :] = mixed_sum[place, :] * jnp.concatenate([shrink] * (latent // W), axis=1) + mixed

    def own_lines(step):
        u = turn(z, step)
        line_x = turn(x, step)
        return lat_a[0, y, line_x], lat_a[1, y, line_x], lat_b[0, y, u], lat_b[1, y, u]

    def own(step):
        u = turn(z, step)
        line_x = turn(x, step)

        def positions(shape):
            column = iota(shape, 1)
            slot, inner, piece = (column // PART) % RING, column % PART, column // line
            part_b = piece // 2
            chip_a = line_x * RING + slot
            chip_b = slot * RING + u
            chip = jnp.where(part_b == 1, chip_b, chip_a)
            return (y * RING * RING + chip) * rows + (piece % 2) * (2 * PART) + part_b * PART + inner

        take_a(y, step).wait_recv()
        take_b(y, step).wait_recv()
        attend(own_lines(step), positions, mine_store)

    def fetch_a(at, step):
        a_from_y(at, step).wait_recv()
        give_a(at, step).start()

    def fetch_b(at, step):
        def far():
            b_from_u(at, step).wait_recv()
            give_b(at, step).start()

        pl.when(step > 0)(far)

    def both(pair, visit):
        for s in range(2):
            visit(jnp.where(pair == 0, s, RING - 1 - s))

    def loop(begin, end, visit):
        lax.fori_loop(begin, end, lambda i, nothing: (visit(i), nothing)[1], 0)

    below = jnp.where(y == RING - 1, 2, jnp.where(y == 0, 0, 1))

    def plane(i):
        return jnp.where(y == RING - 1, RING - 2 - i // 2, 0)

    def fetch(at, pair):
        both(pair, lambda step: fetch_a(at, step))
        both(pair, lambda step: fetch_b(at, step))

    def pass_a(step):
        a_from_x(step).wait_recv()
        spread_a(step)
        fetch_b(y, step)

    own(0)
    lower(spread_b)
    pass_a(1)
    pass_a(3)

    @pl.when(y < RING // 2)
    def _():
        clear(far_store)
        mail().wait_recv()
        absorb(mail_in, far_store)

    def own_round(i):
        pl.when(i == 1)(lambda: pass_a(2))
        pl.when(jnp.logical_and(i == 2, y > 0))(lambda: fetch(plane(0), 0))
        own(jnp.where(i == 0, 1, jnp.where(i == 1, 3, 2)))

        @pl.when(jnp.logical_and(y < RING // 2, i != 1))
        def _():
            first, second = jnp.where(i == 0, 0, 3), jnp.where(i == 0, 1, 2)
            attend(own_lines(first) + own_lines(second), None, far_store)

    loop(0, RING - 1, own_round)

    loads[14].wait()

    def result(h, store):
        place = slice(h * rows, (h + 1) * rows)
        row_total = jnp.sum(store[2][place, :], axis=-1, keepdims=True)
        high, low = halves(store[3][place, :] * (1.0 / row_total))
        up = vu_ref[:, h * W : (h + 1) * W]
        both_parts = mm(jnp.concatenate([high, low], axis=0), up)
        return both_parts[:rows] + both_parts[rows:], store[1][place, :] + jnp.log2(row_total)

    @pl.when(y < RING // 2)
    def _():
        lane = iota((rows, W), 1)
        level = jnp.zeros((rows, W), F32)
        for h in range(heads):
            mixed, log_sum = result(h, far_store)
            mail_out[:, h * W : (h + 1) * W] = mixed.astype(BF16)
            level = jnp.where(lane == h, log_sum, level)
        note_out[...] = level
        note().start()
        mail().start()

    def earlier(i):
        at, pair = plane(i), i % 2
        steps = (jnp.where(pair == 0, 0, 3), jnp.where(pair == 0, 1, 2))
        pl.when(i + 1 < 2 * below)(lambda: fetch(plane(i + 1), (i + 1) % 2))
        both(pair, lambda step: take_a(at, step).wait_recv())
        both(pair, lambda step: take_b(at, step).wait_recv())
        u = axes(at)[0]
        attend(
            [lat_a[c, at, turn(x, step)] for step in steps for c in range(2)]
            + [lat_b[c, at, turn(u, step)] for step in steps for c in range(2)],
            None, mine_store,
        )

    loop(0, 2 * below, earlier)

    @pl.when(y < RING // 2)
    def _():
        for h in range(heads):
            out_ref[:, h * W : (h + 1) * W] = result(h, mine_store)[0].astype(BF16)
        note().wait_send()
        mail().wait_send()

    @pl.when(y >= RING // 2)
    def _():
        mail().wait_send()
        note().wait_recv()
        mail().wait_recv()
        for h in range(heads):
            cols = slice(h * W, (h + 1) * W)
            mixed, log_sum = result(h, mine_store)
            gap = log_sum - note_in[:, h : h + 1]
            far = mail_in[:, cols].astype(F32)
            out_ref[:, cols] = (
                mixed / (1.0 + jnp.exp2(-gap)) + far / (1.0 + jnp.exp2(gap))
            ).astype(BF16)

    for step in others:
        a_over_z(step).wait_send()
        a_over_x(step).wait_send()

    def drain_up(to):
        b_over_y(to).wait_send()
        for step in range(RING):
            a_over_y(to, step).wait_send()

    higher(drain_up)

    def drain(at):
        for step in range(1, RING):
            b_over_v(at, step).wait_send()
            b_over_u(at, step).wait_send()
        for step in range(RING):
            give_a(at, step).wait_send()
            give_b(at, step).wait_send()

    loop(0, below, lambda i: drain(plane(2 * i)))
    drain(y)


    for step in range(1, heads):
        map_to(member(step)[0]).wait_send()
        send_state(step).wait_send()
    for step in range(1, groups):
        each_total(step, lambda copy: copy.wait_send())
    for p in range(PIECES):
        swap(p).wait_send()


def layer(q, k, v, ld, beta, gate, residual, out_gain, hidden_gain, latent_gain, ow, lw, qw, ku, vu):
    heads = beta.shape[0]
    rows, width = residual.shape
    latent = lw.shape[1]
    groups = lax.axis_size("seq") // heads
    vm = pl.BlockSpec(memory_space=pltpu.VMEM)
    anywhere = pl.BlockSpec(memory_space=pl.ANY)
    dma = pltpu.SemaphoreType.DMA
    operands = (q, k, v, ld, beta, gate, residual, out_gain, hidden_gain, latent_gain, ow, lw, qw, ku, vu)
    message = (W + 16, 2 * W)
    one, two = dma((RING,)), dma((RING, RING))
    return pl.pallas_call(
        layer_kernel,
        out_shape=(
            jax.ShapeDtypeStruct((rows, width), BF16),
            jax.ShapeDtypeStruct((rows, heads * W), BF16),
        ),
        in_specs=[anywhere] * len(operands),
        out_specs=(vm, vm),
        scratch_shapes=[pltpu.VMEM(a.shape, a.dtype) for a in operands] + [
            pltpu.VMEM((rows, heads * W), F32),
            pltpu.VMEM((heads, rows, 2 * W), F32),
            pltpu.VMEM((heads,) + message, BF16),
            pltpu.VMEM((rows, heads * W), F32),
            pltpu.VMEM((rows, heads * W), BF16),
            pltpu.VMEM((heads,) + message, BF16),
            pltpu.VMEM(message, BF16),
            pltpu.VMEM((groups,) + message, BF16),
            pltpu.VMEM((heads, W, W), BF16),
            pltpu.VMEM((heads, W, W), BF16),
            pltpu.VMEM((PIECES, rows, width // PIECES), F32),
            pltpu.VMEM((PIECES, rows, width // PIECES), F32),
            pltpu.VMEM((heads, rows, latent), BF16),
            pltpu.VMEM((2, RING, RING, RING, PART, latent), BF16),
            pltpu.VMEM((2, RING, RING, RING, PART, latent), BF16),
            pltpu.VMEM((heads * rows, W), F32),
            pltpu.VMEM((heads * rows, W), F32),
            pltpu.VMEM((heads * rows, latent), F32),
            pltpu.VMEM((heads, rows, latent), BF16),
            pltpu.VMEM((heads * rows, W), F32),
            pltpu.VMEM((heads * rows, W), F32),
            pltpu.VMEM((heads * rows, latent), F32),
            pltpu.VMEM((rows, heads * W), BF16),
            pltpu.VMEM((rows, heads * W), BF16),
            pltpu.VMEM((rows, W), F32),
            pltpu.VMEM((rows, W), F32),
            dma((len(operands),)),
            dma((heads,)), dma((heads,)), dma((groups,)), dma((groups,)),
            dma((heads,)), dma((heads,)), dma((PIECES,)), dma((PIECES,)),
            one, one, one, one, two, two, one, one, two, two, two, two, two, two, two, two,
            dma((2,)), dma((2,)),
        ],
        compiler_params=pltpu.CompilerParams(
            collective_id=0, has_side_effects=True, vmem_limit_bytes=60 * 2**20
        ),
        name="layer",
    )(*operands)


def finish_kernel(hidden_in, attended_in, hidden_out, attended_out):
    hidden_out[...] = hidden_in[...]
    attended_out[...] = attended_in[...]


def finish(hidden, attended):
    vm = pl.BlockSpec(memory_space=pltpu.VMEM)
    return pl.pallas_call(
        finish_kernel,
        out_shape=tuple(jax.ShapeDtypeStruct(a.shape, a.dtype) for a in (hidden, attended)),
        in_specs=[vm] * 2,
        out_specs=(vm, vm),
        name="finish",
    )(hidden, attended)


def body(
    residual, kda_query, kda_key, kda_value, log_decay, beta_logit, out_gate, out_gain, out_weight,
    hidden_gain, query_weight, latent_weight, latent_gain, key_up_weight, value_up_weight,
):
    hidden, attended = layer(
        kda_query, kda_key, kda_value, log_decay, beta_logit.T, out_gate, residual, out_gain[None],
        hidden_gain.reshape(-1, W), latent_gain[None], out_weight, latent_weight, query_weight, key_up_weight,
        value_up_weight,
    )
    return finish(hidden, attended)


def solution(mesh):
    in_specs = (
        P("seq", None),
        P("seq", "head"),
        P("seq", "head"),
        P("seq", "head"),
        P("seq", "head"),
        P("seq", "head"),
        P("seq", "head"),
        P(),
        P("head", None),
        P(),
        P(None, "head"),
        P(),
        P(),
        P(None, "head"),
        P(None, "head"),
    )
    out_specs = (P("seq", None), P("seq", "head"))
    return jax.shard_map(body, mesh=mesh, in_specs=in_specs, out_specs=out_specs, check_vma=False)
```
